256 devices in a mesh: lon: 16 (over x, y_hi, core), lat: 16 (over z, y_lo).
Axes of the slice: x: 4, y: 4 (y_hi: 2, y_lo: 2; y = y_hi * 2 + y_lo), z: 8, core: 2. Of those that a mesh axis runs over, the one named last changes fastest.
Arguments:
- field: bfloat16 [512, 512, 256], P('lat', 'lon'), may hold values from -6 to 6
- first_weight: bfloat16 [2304, 256], replicated, may hold values from -0.125 to 0.125
- second_weight: bfloat16 [2304, 256], replicated, may hold values from -0.125 to 0.125
- cotangent: bfloat16 [512, 512, 256], P('lat', 'lon'), may hold values from -6 to 6
- live_rows: int32 [16, 16], P('lon', 'lat'), may hold values from 8 to 32, as said below
- polar_links: int32 [2, 512], replicated, may hold values from 0 to 511, as said below
Outputs:
- output: bfloat16 [512, 512, 256], P('lat', 'lon')
- field_grad: bfloat16 [512, 512, 256], P('lat', 'lon')
- first_grad: float32 [2304, 256], P('lat')
- second_grad: float32 [2304, 256], P('lat')
The draws below stay inside these ranges and needn't reach their ends.
Inputs may be any that keep to these rules, and one draw needn't show every extreme that they name: `live_rows`: equals 32 for every tile outside the first and the last row of tiles. `polar_links`: each of the two rows maps column j to (K - j) mod 512 for a whole number K of its own: the loop's columns in reversed order.
All inputs are finite; a program needn't handle non-finite values.
Results may differ from the reference program's by a relative error of at most 0.014.
Values may be sent and summed in bfloat16 or wider, within the bound.
A program may use at most 128 MiB of HBM per device.

```python
import math
import jax
import jax.numpy as jnp
from jax import lax

C = 256
ROWS = 32
COLS = 32
LON_TILES = 16
LAT_TILES = 16
NLON = 512
NLAT = 512


def draw_live_rows(key, part):
    key = jax.random.fold_in(key, 7)
    values = jax.random.randint(key, (LON_TILES, LAT_TILES), ROWS // 4, ROWS + 1, dtype=jnp.int32)
    lat_pos = jnp.arange(LAT_TILES, dtype=jnp.int32)[None, :]
    inner = (lat_pos > 0) & (lat_pos < LAT_TILES - 1)
    return jnp.where(inner, ROWS, values).astype(jnp.int32)


def draw_polar_links(key, part):
    key = jax.random.fold_in(key, 11)
    key_m, key_r = jax.random.split(key)
    pairs = NLON // (2 * COLS)
    blocks = jax.random.randint(key_m, (2, 1), 0, pairs, dtype=jnp.int32)
    rests = jax.random.randint(key_r, (2, 1), 0, 2 * COLS - 1, dtype=jnp.int32)
    rests = rests + (rests >= COLS - 1).astype(jnp.int32)
    pivot = 2 * COLS * blocks + rests
    columns = jnp.arange(NLON, dtype=jnp.int32)[None, :]
    return ((pivot - columns) % NLON).astype(jnp.int32)


def levels(stream_key, shape, cuts, smallest, top_value):
    def one(axis_at, blocks):
        steps = jax.random.uniform(jax.random.fold_in(jax.random.fold_in(stream_key, 6), axis_at), (blocks,), jnp.float32, smallest / len(cuts), top_value / len(cuts))
        return jnp.repeat(jnp.exp(steps), shape[axis_at] // blocks).reshape((-1,) + (1,) * (len(shape) - axis_at - 1))

    loudness = one(*cuts[0])
    for cut in cuts[1:]:
        loudness = loudness * one(*cut)
    return loudness


def noise(key, extent, width, bound, cuts=(), kind=jnp.bfloat16):
    factor_of = levels(key, extent, cuts, -0.22, 0.18) if cuts else 1.0
    values = jax.random.normal(key, extent, jnp.float32) * width * factor_of
    return jnp.minimum(jnp.maximum(values, -bound), bound).astype(kind)


def setup_inputs(seed: int = 0) -> dict:
    seeds = jax.random.split(jax.random.key(seed), 7)
    return {
        "field": noise(seeds[0], (NLAT, NLON, C), 1.0, 6.0, ((0, 16), (1, 16))),
        "first_weight": noise(seeds[1], (9 * C, C), (9 * C) ** -0.5, 0.125),
        "second_weight": noise(seeds[2], (9 * C, C), (9 * C) ** -0.5, 0.125),
        "cotangent": noise(seeds[3], (NLAT, NLON, C), 1.0, 6.0, ((0, 16), (1, 16))),
        "live_rows": draw_live_rows(jax.random.fold_in(seeds[6], 71), 0),
        "polar_links": draw_polar_links(jax.random.fold_in(seeds[6], 71), 0),
    }


def gelu_parts(pre):
    cdf = 0.5 * (1.0 + jax.scipy.special.erf(pre * 0.7071067811865476))
    dens = jnp.exp(-0.5 * pre * pre) * 0.3989422804014327
    return (pre * cdf, cdf + pre * dens)

def grid_mask(live_rows):
    limit = jnp.repeat(jnp.repeat(live_rows.T, ROWS, axis=0), COLS, axis=1)
    local_row = jnp.arange(NLAT, dtype=jnp.int32) % ROWS
    return local_row[:, None] < limit

def pad_field(field, polar_links):
    loop_len = field.shape[1]
    wide = jnp.concatenate([field[:, -1:], field, field[:, :1]], axis=1)
    columns = (jnp.arange(loop_len + 2, dtype=jnp.int32) - 1) % loop_len
    north = jnp.take(field[0], jnp.take(polar_links[0], columns), axis=0)
    south = jnp.take(field[-1], jnp.take(polar_links[1], columns), axis=0)
    return jnp.concatenate([north[None], wide, south[None]], axis=0)

def patches(grown, tile_rows, tile_cols):
    pieces = [grown[row_off:row_off + tile_rows, col_off:col_off + tile_cols] for row_off in range(3) for col_off in range(3)]
    return jnp.concatenate(pieces, axis=-1).reshape(tile_rows * tile_cols, -1)

def conv_blocks(grown, weight, count):
    loop_len = grown.shape[1] - 2

    def single(start):
        piece = lax.dynamic_slice_in_dim(grown, start, ROWS + 2, 0)
        result = jnp.dot(patches(piece, ROWS, loop_len), weight, preferred_element_type=jnp.float32)
        return result.reshape(ROWS, loop_len, weight.shape[1])
    starts = jnp.arange(count, dtype=jnp.int32) * ROWS
    return lax.map(single, starts).reshape(count * ROWS, loop_len, weight.shape[1])

def weight_grad(grown, delta, count):
    loop_len = grown.shape[1] - 2
    channels = delta.shape[2]

    def step(total, index):
        start = index * ROWS
        piece = lax.dynamic_slice_in_dim(grown, start, ROWS + 2, 0)
        part = lax.dynamic_slice_in_dim(delta, start, ROWS, 0).reshape(-1, channels)
        term = lax.dot_general(patches(piece, ROWS, loop_len), part, (((0,), (0,)), ((), ())), preferred_element_type=jnp.float32)
        return (total + term, None)
    total, _ = lax.scan(step, jnp.zeros((9 * channels, channels), jnp.float32), jnp.arange(count, dtype=jnp.int32))
    return total

def conv_back(delta, weight, count):
    channels = weight.shape[1]
    loop_len = delta.shape[1]

    def step(total, index):
        start = index * ROWS
        part = lax.dynamic_slice_in_dim(delta, start, ROWS, 0).reshape(-1, channels)
        spread = jnp.dot(part, weight.T, preferred_element_type=jnp.float32).reshape(ROWS, loop_len, 9, channels)
        window = jnp.zeros((ROWS + 2, loop_len + 2, channels), jnp.float32)
        for tap in range(9):
            row_off, col_off = divmod(tap, 3)
            window = window.at[row_off:row_off + ROWS, col_off:col_off + loop_len].add(spread[:, :, tap])
        before = lax.dynamic_slice_in_dim(total, start, ROWS + 2, 0)
        return (lax.dynamic_update_slice_in_dim(total, before + window, start, 0), None)
    empty = jnp.zeros((delta.shape[0] + 2, loop_len + 2, channels), jnp.float32)
    total, _ = lax.scan(step, empty, jnp.arange(count, dtype=jnp.int32))
    return total

def fold_back(total, polar_links):
    loop_len = total.shape[1] - 2
    inner = total[1:-1, 1:-1]
    inner = inner.at[:, -1].add(total[1:-1, 0]).at[:, 0].add(total[1:-1, -1])
    columns = (jnp.arange(loop_len + 2, dtype=jnp.int32) - 1) % loop_len
    inner = inner.at[0, jnp.take(polar_links[0], columns)].add(total[0])
    inner = inner.at[-1, jnp.take(polar_links[1], columns)].add(total[-1])
    return inner

def reference(field, first_weight, second_weight, cotangent, live_rows, polar_links):
    count = field.shape[0] // ROWS
    keep = grid_mask(live_rows)[:, :, None]
    keep_f = keep.astype(jnp.float32)
    masked = jnp.where(keep, field, jnp.zeros_like(field))
    grown_in = pad_field(masked, polar_links)
    first_pre = conv_blocks(grown_in, first_weight, count)
    activated, slope = gelu_parts(first_pre)
    hidden = (activated * keep_f).astype(jnp.bfloat16)
    grown_hidden = pad_field(hidden, polar_links)
    second_pre = conv_blocks(grown_hidden, second_weight, count)
    output = (masked.astype(jnp.float32) + second_pre * keep_f).astype(jnp.bfloat16)
    delta_two = jnp.where(keep, cotangent, jnp.zeros_like(cotangent))
    scale = 1.0 / math.sqrt(field.shape[0] * field.shape[1])
    second_grad = weight_grad(grown_hidden, delta_two, count) * scale
    back_hidden = fold_back(conv_back(delta_two, second_weight, count), polar_links)
    delta_one = (back_hidden * keep_f * slope).astype(jnp.bfloat16)
    first_grad = weight_grad(grown_in, delta_one, count) * scale
    back_in = fold_back(conv_back(delta_one, first_weight, count), polar_links)
    field_grad = ((cotangent.astype(jnp.float32) + back_in) * keep_f).astype(jnp.bfloat16)
    return (output, field_grad, first_grad, second_grad)
```

```python
import math

import jax
import jax.numpy as jnp
from jax import lax
from jax.experimental import pallas as pl
from jax.experimental.pallas import tpu as pltpu
from jax.sharding import PartitionSpec as P

MESH = pl.DeviceIdType.MESH
BF = jnp.bfloat16
F32 = jnp.float32
C = 256
T = 32
EXT = T + 4
PX = EXT * T
RING = T + 2
MSG = 5 * T
STRIP = 40
LON = 16
LAT = 16
PLANES = 8
SHARE = 3 * T // 2 * 3
FIRST = (0, 3, 6, 8, 10, 12, 14, 16)


def dot(a, b):
    return jnp.dot(a, b, preferred_element_type=F32)


def gelu_parts(pre):
    cdf = 0.5 * (1.0 + lax.erf(pre * 0.7071067811865476))
    dens = jnp.exp(-0.5 * pre * pre) * 0.3989422804014327
    return (pre * cdf, cdf + pre * dens)


def rows(start, size=T):
    return pl.ds(pl.multiple_of(start * T, T), size)


def kernel(
    field,
    w1,
    w2,
    cot,
    live_ref,
    links,
    out,
    fgrad,
    grad1,
    grad2,
    sx,
    sd,
    sh,
    sg,
    zx,
    zd,
    zh,
    zg,
    zs,
    kz,
    cols,
    corner,
    slope,
    xt,
    dz,
    wt1,
    wt2,
    ext,
    send_ns,
    send_ew,
    send_dg,
    halo_ns,
    halo_ew,
    halo_dg,
    polar,
    gkeep,
    gsend,
    gpair,
    gsum,
    parts2,
    tiles,
    parts3,
    own,
    final,
    hs_sem,
    hr_sem,
    ps_sem,
    pr_sem,
    s1_sem,
    r1_sem,
    s2_sem,
    r2_sem,
    s3_sem,
    r3_sem,
    s4_sem,
    r4_sem,
):
    u, v = lax.axis_index("lon"), lax.axis_index("lat")
    core, x, z = u % 2, u // 4, v // 2
    y = (u // 2) % 2 * 2 + v % 2
    spot = x * 4 + y
    north, south = v == 0, v == LAT - 1
    side = jnp.where(south, 1, 0)
    live = live_ref[0, 0]
    east, west = (u + 1) % LON, (u + LON - 1) % LON

    def in_plane(place):
        px, py = place // 4, place % 4
        return {"lon": px * 4 + py // 2 * 2 + core, "lat": z * 2 + py % 2}

    def in_column(plane):
        return {"lon": u, "lat": plane * 2 + v % 2}

    barrier = pltpu.get_barrier_semaphore()

    def greet(lon, lat):
        pl.semaphore_signal(barrier, inc=1, device_id={"lon": lon, "lat": lat}, device_id_type=MESH)

    greet(east, v)
    greet(west, v)

    @pl.when(v > 0)
    def _():
        for lon in (west, u, east):
            greet(lon, v - 1)

    @pl.when(v < LAT - 1)
    def _():
        for lon in (west, u, east):
            greet(lon, v + 1)

    @pl.when(north | south)
    def _():
        @pl.loop(1, LON)
        def _(d):
            greet((u + d) % LON, v)

    @pl.loop(1, 16)
    def _(d):
        to = in_plane((spot + d) % 16)
        greet(to["lon"], to["lat"])

    @pl.loop(1, PLANES)
    def _(d):
        greet(u, (z + d) % PLANES * 2 + v % 2)

    lane_row = lax.broadcasted_iota(jnp.int32, (T, C), 0)

    @pl.loop(0, T)
    def _(i):
        kept = jnp.full((T, C), i, jnp.int32) < live
        for k, (src, dst) in enumerate(((field, sx), (cot, sd))):
            line = jnp.where(kept, src[i].astype(F32), 0.0)
            dst[1, rows(i + 2), :] = line.astype(BF)
            for n, col in enumerate((0, 1, T - 2, T - 1)):
                cols[k, n, pl.ds(i, 1), :] = line[col : col + 1]

    keep_col = jnp.where(lane_row < live, 1.0, 0.0)
    keep_last = jnp.where(jnp.full((T, C), T - 1, jnp.int32) < live, 1.0, 0.0)
    for s in range(2):
        for k, src in enumerate((sx, sd)):
            first = 2 if s == 0 else T
            send_ns[s, 2 * k * T : (2 * k + 2) * T, :] = src[1, first * T : (first + 2) * T, :]
            for n in range(2):
                send_ew[s, (2 * k + n) * T : (2 * k + n + 1) * T, :] = cols[k, 2 * s + n].astype(BF)
        send_ns[s, 4 * T :, :] = jnp.ones((T, C), BF) if s == 0 else keep_last.astype(BF)
        send_ew[s, 4 * T :, :] = keep_col.astype(BF)
    corner[...] = jnp.zeros_like(corner)
    for s in range(2):
        for t in range(2):
            for k in range(2):
                for r in range(2):
                    for n in range(2):
                        at = 4 * k + 2 * r + n
                        line = (0 if s == 0 else T - 2) + r
                        corner[2 * s + t, at : at + 1, :] = cols[k, 2 * t + n, line : line + 1, :]
            corner[2 * s + t, 8:9, :] = jnp.ones((1, C), F32) if s == 0 else keep_last[0:1]
    send_dg[...] = corner[...].astype(BF)

    here = jnp.where(v > 0, 3, 0) + jnp.where(v < LAT - 1, 3, 0) + jnp.where(north | south, 15, 0)
    pl.semaphore_wait(barrier, here + 2 + 15 + 7)

    def edge(src, dst, n, lon, lat):
        return pltpu.make_async_remote_copy(
            src_ref=src,
            dst_ref=dst,
            send_sem=hs_sem.at[n],
            recv_sem=hr_sem.at[n],
            device_id={"lon": lon, "lat": lat},
            device_id_type=MESH,
        )

    to_west = edge(send_ew.at[0], halo_ew.at[1], 0, west, v)
    to_east = edge(send_ew.at[1], halo_ew.at[0], 1, east, v)
    to_north = [
        edge(send_ns.at[0], halo_ns.at[1], 2, u, v - 1),
        edge(send_dg.at[0], halo_dg.at[3], 3, west, v - 1),
        edge(send_dg.at[1], halo_dg.at[2], 4, east, v - 1),
    ]
    to_south = [
        edge(send_ns.at[1], halo_ns.at[0], 5, u, v + 1),
        edge(send_dg.at[2], halo_dg.at[1], 6, west, v + 1),
        edge(send_dg.at[3], halo_dg.at[0], 7, east, v + 1),
    ]

    def around(lon):
        return pltpu.make_async_remote_copy(
            src_ref=send_ns.at[side],
            dst_ref=polar.at[u],
            send_sem=ps_sem,
            recv_sem=pr_sem,
            device_id={"lon": lon, "lat": v},
            device_id_type=MESH,
        )

    @pl.when(north | south)
    def _():
        @pl.loop(1, LON)
        def _(d):
            around((u + d) % LON).start()

    to_west.start()
    to_east.start()

    @pl.when(v > 0)
    def _():
        for copy in to_north:
            copy.start()

    @pl.when(v < LAT - 1)
    def _():
        for copy in to_south:
            copy.start()

    @pl.loop(0, 9)
    def _(tap):
        at = pl.ds(pl.multiple_of(tap * C, C), C)
        wt1[at, :] = w1[at, :].T
        wt2[at, :] = w2[at, :].T

    for ref in (zx, zd, zh, zg, zs, ext):
        ref[...] = jnp.zeros_like(ref)
    for b in range(3):
        sh[b, 0:T, :] = jnp.zeros((T, C), BF)
        sh[b, PX - T : PX, :] = jnp.zeros((T, C), BF)
    dz[0 : 3 * T, :] = jnp.zeros((3 * T, C), BF)
    dz[35 * T : 38 * T, :] = jnp.zeros((3 * T, C), BF)
    dz[3 * T : 35 * T, :] = sd[1, 2 * T : 34 * T, :]

    to_west.wait_recv()
    to_east.wait_recv()

    @pl.when(v > 0)
    def _():
        for copy in to_south:
            copy.wait_recv()

    @pl.when(v < LAT - 1)
    def _():
        for copy in to_north:
            copy.wait_recv()

    def drain(ref, sem):
        pltpu.make_async_copy(ref, ref, sem).wait()

    @pl.when(north | south)
    def _():
        drain(polar.at[pl.ds(0, LON - 1)], pr_sem)
        drain(polar.at[pl.ds(0, LON - 1)], ps_sem)
        polar[u] = send_ns[side]
        pivot = links[side, 0]
        n = lax.broadcasted_iota(jnp.int32, (2 * T, LON * T), 0)
        at = lax.broadcasted_iota(jnp.int32, (2 * T, LON * T), 1)
        q = n & 15
        in_east = n >= T + 16
        ring_col = jnp.where(in_east, T, -1)
        outer_col = jnp.where(in_east, T, -2) + (q & 1)
        col = jnp.where(n < T, n, jnp.where(q == 8, ring_col, outer_col))
        hit = ((pivot - u * T - col) & (LON * T - 1)) == at
        line = jnp.where(q == 8, 4, jnp.where(q < 8, q // 2, 5))
        corners = jnp.zeros((T, C), F32)
        for part in range(5):
            target = part if part == 4 else part ^ 1
            pick = jnp.where(hit & ((n < T) | (line == target)), 1.0, 0.0).astype(BF)
            lines = polar[:, part * T : (part + 1) * T, :].reshape(LON * T, C)
            found = dot(pick, lines)
            halo_ns[side, target * T : (target + 1) * T, :] = found[:T].astype(BF)
            corners = corners + found[T:]
        halo_dg[2 * side] = corners[:16].astype(BF)
        halo_dg[2 * side + 1] = corners[16:].astype(BF)

    for k, (s, zz) in enumerate(((sx, zx), (sd, zd))):
        s[1, 0 : 2 * T, :] = halo_ns[0, 2 * k * T : (2 * k + 2) * T, :]
        s[1, 34 * T : 36 * T, :] = halo_ns[1, 2 * k * T : (2 * k + 2) * T, :]
        for n in range(2):
            zz[n, 2 : 2 + T, :] = halo_ew[0, (2 * k + n) * T : (2 * k + n + 1) * T, :].astype(F32)
            zz[4 + n, 2 : 2 + T, :] = halo_ew[1, (2 * k + n) * T : (2 * k + n + 1) * T, :].astype(F32)
        for dg in range(4):
            px = halo_dg[dg].astype(F32)
            for r in range(2):
                for n in range(2):
                    e = dg // 2 * 34 + r
                    at = 4 * k + 2 * r + n
                    zz[dg % 2 * 4 + n, e : e + 1, :] = px[at : at + 1]
    kz[...] = jnp.zeros_like(kz)
    for t in range(2):
        kz[t, 2 : 2 + T, :] = halo_ew[t, 4 * T :, :].astype(F32)
        kz[t, 1:2, :] = halo_dg[t].astype(F32)[8:9]
        kz[t, 34:35, :] = halo_dg[2 + t].astype(F32)[8:9]

    def shifted(s, left, right, lo, hi, zz=None):
        @pl.loop(lo, hi)
        def _(e):
            at = rows(e)
            line = s[1, at, :].astype(F32)
            s[0, at, :] = jnp.where(lane_row == 0, left[pl.ds(e, 1), :], pltpu.roll(line, 1, 0)).astype(BF)
            s[2, at, :] = jnp.where(
                lane_row == T - 1, right[pl.ds(e, 1), :], pltpu.roll(line, T - 1, 0)
            ).astype(BF)
            if zz is not None:
                zz[2, pl.ds(e, 1), :] = line[0:1]
                zz[3, pl.ds(e, 1), :] = line[T - 1 : T]

    def transposed(s):
        @pl.loop(0, PX // 128)
        def _(k):
            at = pl.ds(pl.multiple_of(k * 128, 128), 128)
            for b in range(3):
                xt[b * C : (b + 1) * C, at] = s[b, at, :].T

    shifted(sx, zx.at[1], zx.at[4], 0, EXT, zx)
    shifted(sd, zd.at[1], zd.at[4], 0, EXT, zd)

    e_out, e_ring = jnp.where(south, 35, 0), jnp.where(south, 34, 1)
    e_edge, e_in = jnp.where(south, 33, 2), jnp.where(south, 32, 3)
    far = jnp.where(south, 2, 0)

    def extend(n, s, left, right, e):
        ext[n, 2 : 2 + T, :] = s[1, rows(e), :].astype(F32)
        for k, ref in enumerate(left):
            at = 2 - len(left) + k
            ext[n, at : at + 1, :] = ref[pl.ds(e, 1), :]
        for k, ref in enumerate(right):
            ext[n, 34 + k : 35 + k, :] = ref[pl.ds(e, 1), :]

    def straight(n):
        return jnp.concatenate([ext[n, 2 - b : 42 - b, :] for b in range(3)], axis=1).astype(BF)

    def turned(n):
        return jnp.concatenate([ext[n, b : b + 40, :] for b in range(3)], axis=1).astype(BF)

    def taps(w, row):
        return w[pl.ds(pl.multiple_of(row * 3 * C, 3 * C), 3 * C), :]

    def strips(zz, w, back):
        order = (2, 1, 0) if back else (0, 1, 2)
        both = jnp.concatenate(
            [jnp.concatenate([zz[3 * t + b] for b in order], axis=1) for t in range(2)], axis=0
        ).astype(BF)
        up, mid, down = (dot(both, w[a * 3 * C : (a + 1) * 3 * C, :]) for a in range(3))
        if back:
            up, down = down, up
        return pltpu.roll(up, 1, 0) + mid + pltpu.roll(down, 2 * STRIP - 1, 0)

    step = 272

    @pl.loop(0, RING * T // step)
    def _(c):
        m = pl.multiple_of(c * step, 16)
        stacked = jnp.concatenate(
            [sx[b, pl.ds(pl.multiple_of(m + a * T, 16), step), :] for a in range(3) for b in range(3)],
            axis=1,
        )
        act, slp = gelu_parts(dot(stacked, w1[...]))
        row = (lax.broadcasted_iota(jnp.int32, (step, C), 0) + m) // T
        kept = (row - 1 < live) | (row == RING - 1)
        sh[1, pl.ds(pl.multiple_of(m + T, 16), step), :] = jnp.where(kept, act, 0.0).astype(BF)
        slope[pl.ds(m, step), :] = jnp.where(kept, slp, 0.0)

    act, slp = gelu_parts(strips(zx, w1, False))
    for t in range(2):
        zh[t] = act[t * STRIP : (t + 1) * STRIP] * kz[t]
        zs[t] = slp[t * STRIP : (t + 1) * STRIP] * kz[t]

    @pl.when(north | south)
    def _():
        for n, e in enumerate((e_out, e_ring, e_edge)):
            extend(n, sx, (zx.at[0], zx.at[1]), (zx.at[4], zx.at[5]), e)
        pre = dot(straight(2), taps(w1, far)) + dot(straight(1), taps(w1, 1)) + dot(straight(0), taps(w1, 2 - far))
        act, slp = gelu_parts(pre)
        sh[1, rows(e_ring), :] = act[1 : 1 + T].astype(BF)
        slope[rows(e_ring - 1), :] = slp[1 : 1 + T]
        for t in range(2):
            at = t * (T + 1)
            mask = kz[t, pl.ds(e_ring, 1), :]
            zh[t, pl.ds(e_ring, 1), :] = act[at : at + 1] * mask
            zs[t, pl.ds(e_ring, 1), :] = slp[at : at + 1] * mask

    for s in range(2):
        mask = halo_ns[s, 4 * T :, :].astype(F32)
        e = 1 if s == 0 else 34
        sh[1, e * T : (e + 1) * T, :] = (sh[1, e * T : (e + 1) * T, :].astype(F32) * mask).astype(BF)
        slope[(e - 1) * T : e * T, :] = slope[(e - 1) * T : e * T, :] * mask

    shifted(sh, zh.at[0], zh.at[1], 1, 35)
    transposed(sh)

    sibling = {"lon": u + 1 - 2 * core, "lat": v}

    def pair(g, a):
        return pltpu.make_async_remote_copy(
            src_ref=gsend.at[g, a],
            dst_ref=gpair.at[g, a],
            send_sem=s1_sem.at[g, a],
            recv_sem=r1_sem.at[g, a],
            device_id=sibling,
            device_id_type=MESH,
        )

    def scatter(g, a):
        pair(g, a).wait()
        gsum[g, a] = (gkeep[g, a] + gpair[g, a].astype(F32)).astype(BF)

        @pl.loop(1, 16)
        def _(d):
            to = (spot + d) % 16
            pltpu.make_async_remote_copy(
                src_ref=gsum.at[g, a, :, pl.ds(pl.multiple_of(to * 16, 16), 16), :],
                dst_ref=parts2.at[g, a, spot],
                send_sem=s2_sem.at[g, a],
                recv_sem=r2_sem.at[g, a],
                device_id=in_plane(to),
                device_id_type=MESH,
            ).start()

    def weight_grad(g):
        @pl.loop(0, 3)
        def _(a):
            res = dot(xt[...], dz[rows(2 - a, PX), :])
            lo, hi = res[:, : C // 2], res[:, C // 2 :]
            gkeep[g, a] = jnp.where(core == 0, lo, hi).reshape(3, C, C // 2)
            gsend[g, a] = jnp.where(core == 0, hi, lo).astype(BF).reshape(3, C, C // 2)
            pair(g, a).start()

            @pl.when(a > 0)
            def _():
                scatter(g, a - 1)

    weight_grad(0)

    @pl.loop(0, RING * T // step)
    def _(c):
        m = pl.multiple_of(c * step, 16)
        stacked = jnp.concatenate(
            [
                sd[2 - b, pl.ds(pl.multiple_of(m + (2 - a) * T, 16), step), :]
                for a in range(3)
                for b in range(3)
            ],
            axis=1,
        )
        back = dot(stacked, wt2[...])
        sg[1, pl.ds(pl.multiple_of(m + T, 16), step), :] = (back * slope[pl.ds(m, step), :]).astype(BF)

    scatter(0, 2)
    back = strips(zd, wt2, True)
    for t in range(2):
        zg[t] = back[t * STRIP : (t + 1) * STRIP] * zs[t]

    @pl.when(north | south)
    def _():
        for n, e in enumerate((e_out, e_ring, e_edge, e_in)):
            extend(n, sd, (zd.at[0], zd.at[1]), (zd.at[4], zd.at[5]), e)
        w_far, w_mid = taps(wt2, far), taps(wt2, 1)
        ring = dot(turned(0), w_far) + dot(straight(2), w_far) + dot(turned(1), w_mid)
        rim = dot(turned(1), w_far) + dot(straight(3), w_far) + dot(straight(2), w_mid)
        for e, res in ((e_ring, ring), (e_edge, rim)):
            sg[1, rows(e), :] = (res[1 : 1 + T] * slope[rows(e - 1), :]).astype(BF)
            for t in range(2):
                at = t * (T + 1)
                zg[t, pl.ds(e, 1), :] = res[at : at + 1] * zs[t, pl.ds(e, 1), :]

    shifted(sg, zg.at[0], zg.at[1], 1, 35)
    dz[3 * T : 35 * T, :] = sg[1, 2 * T : 34 * T, :]
    transposed(sx)
    weight_grad(1)

    size = 8 * T

    @pl.loop(0, T * T // size)
    def _(c):
        m = pl.multiple_of(c * size, size)
        stacked = jnp.concatenate(
            [
                sh[b, pl.ds(pl.multiple_of(m + (1 + a) * T, T), size), :]
                for a in range(3)
                for b in range(3)
            ],
            axis=1,
        )
        pre = dot(stacked, w2[...])
        row = (lax.broadcasted_iota(jnp.int32, (size, C), 0) + m) // T
        masked = sx[1, pl.ds(pl.multiple_of(m + 2 * T, T), size), :].astype(F32)
        res = (masked + jnp.where(row < live, pre, 0.0)).astype(BF)
        out[pl.ds(c * 8, 8)] = res.reshape(8, T, C)

    scatter(1, 2)

    @pl.loop(0, T * T // size)
    def _(c):
        m = pl.multiple_of(c * size, size)
        stacked = jnp.concatenate(
            [
                sg[2 - b, pl.ds(pl.multiple_of(m + (3 - a) * T, T), size), :]
                for a in range(3)
                for b in range(3)
            ],
            axis=1,
        )
        back = dot(stacked, wt1[...])
        row = (lax.broadcasted_iota(jnp.int32, (size, C), 0) + m) // T
        total = cot[pl.ds(c * 8, 8)].reshape(size, C).astype(F32) + back
        fgrad[pl.ds(c * 8, 8)] = jnp.where(row < live, total, 0.0).astype(BF).reshape(8, T, C)

    @pl.when(north | south)
    def _():
        for n, e in ((1, e_ring), (2, e_edge), (3, e_in)):
            extend(n, sg, (zg.at[0],), (zg.at[1],), e)
        w_far, w_mid = taps(wt1, far), taps(wt1, 1)
        rim = dot(turned(1), w_far) + dot(straight(3), w_far) + dot(straight(2), w_mid)
        i = e_edge - 2
        total = cot[i].astype(F32) + rim[1 : 1 + T]
        kept = jnp.full((T, C), i, jnp.int32) < live
        fgrad[i] = jnp.where(kept, total, 0.0).astype(BF)

    tiles[18] = jnp.zeros((16, C // 2), BF)
    for g in range(2):
        for a in range(3):
            drain(parts2.at[g, a, pl.ds(0, 15)], r2_sem.at[g, a])
            parts2[g, a, spot] = gsum[g, a, :, pl.ds(pl.multiple_of(spot * 16, 16), 16), :]
            total = parts2[g, a, 0].astype(F32)
            for k in range(1, 16):
                total = total + parts2[g, a, k].astype(F32)
            tiles[9 * g + 3 * a : 9 * g + 3 * a + 3] = total.astype(BF)

    def window(plane):
        start = plane * 3
        for k, first in enumerate(FIRST):
            if first != 3 * k:
                start = jnp.where(plane == k, first, start)
        return start

    @pl.loop(1, PLANES)
    def _(d):
        to = (z + d) % PLANES
        pltpu.make_async_remote_copy(
            src_ref=tiles.at[pl.ds(window(to), 3)],
            dst_ref=parts3.at[z],
            send_sem=s3_sem,
            recv_sem=r3_sem,
            device_id=in_column(to),
            device_id_type=MESH,
        ).start()

    mine = window(z)
    drain(parts3.at[pl.ds(0, PLANES - 1)], r3_sem)
    parts3[z] = tiles[pl.ds(mine, 3)]
    total = parts3[0].astype(F32)
    for k in range(1, PLANES):
        total = total + parts3[k].astype(F32)
    own[...] = total.astype(BF)

    def deliver(slot, act):
        tile = mine + slot
        g = tile // 9
        place = tile % 9 * 16 + spot
        lat, at = place // 9, place % 9

        @pl.loop(0, LON)
        def _(d):
            to = (u + d) % LON
            src, dst = own.at[slot], final.at[g, at, core]

            @pl.when((d == 0) & (lat == v))
            def _():
                if act:
                    pltpu.make_async_copy(src, dst, r4_sem).start()

            @pl.when((d > 0) | (lat != v))
            def _():
                copy = pltpu.make_async_remote_copy(
                    src_ref=src,
                    dst_ref=dst,
                    send_sem=s4_sem.at[slot, d],
                    recv_sem=r4_sem,
                    device_id={"lon": to, "lat": lat},
                    device_id_type=MESH,
                )
                if act:
                    copy.start()
                else:
                    copy.wait_send()

    for act in (True, False):
        deliver(0, act)
        deliver(1, act)

        @pl.when(z < 2)
        def _(act=act):
            deliver(2, act)

        if act:
            drain(final, r4_sem)

    scale = 1.0 / math.sqrt(LON * T * LAT * T)
    for g, ref in enumerate((grad2, grad1)):
        for k in range(9):
            for h in range(2):
                ref[k * 16 : (k + 1) * 16, h * 128 : (h + 1) * 128] = final[g, k, h].astype(F32) * scale

    to_west.wait_send()
    to_east.wait_send()

    @pl.when(v > 0)
    def _():
        for copy in to_north:
            copy.wait_send()

    @pl.when(v < LAT - 1)
    def _():
        for copy in to_south:
            copy.wait_send()

    for g in range(2):
        for a in range(3):
            drain(parts2.at[g, a, pl.ds(0, 15)], s2_sem.at[g, a])
    drain(parts3.at[pl.ds(0, PLANES - 1)], s3_sem)


def local(field, first_weight, second_weight, cotangent, live_rows, polar_links):
    vmem = pl.BlockSpec(memory_space=pltpu.VMEM)
    smem = pl.BlockSpec(memory_space=pltpu.SMEM)
    tile = jax.ShapeDtypeStruct((T, T, C), BF)
    share = jax.ShapeDtypeStruct((SHARE, C), F32)
    flat = pltpu.VMEM((3, PX, C), BF)
    columns = pltpu.VMEM((6, STRIP, C), F32)
    two = pltpu.VMEM((2, STRIP, C), F32)
    half = C // 2
    output, field_grad, grad1, grad2 = pl.pallas_call(
        kernel,
        out_shape=(tile, tile, share, share),
        in_specs=[vmem, vmem, vmem, vmem, smem, smem],
        out_specs=(vmem, vmem, vmem, vmem),
        scratch_shapes=[
            flat,
            flat,
            flat,
            flat,
            columns,
            columns,
            two,
            two,
            two,
            two,
            pltpu.VMEM((2, 4, T, C), F32),
            pltpu.VMEM((4, 16, C), F32),
            pltpu.VMEM((RING * T, C), F32),
            pltpu.VMEM((3 * C, PX), BF),
            pltpu.VMEM((38 * T, C), BF),
            pltpu.VMEM((9 * C, C), BF),
            pltpu.VMEM((9 * C, C), BF),
            pltpu.VMEM((4, 48, C), F32),
            pltpu.VMEM((2, MSG, C), BF),
            pltpu.VMEM((2, MSG, C), BF),
            pltpu.VMEM((4, 16, C), BF),
            pltpu.VMEM((2, MSG, C), BF),
            pltpu.VMEM((2, MSG, C), BF),
            pltpu.VMEM((4, 16, C), BF),
            pltpu.VMEM((LON, MSG, C), BF),
            pltpu.VMEM((2, 3, 3, C, half), F32),
            pltpu.VMEM((2, 3, 3, C, half), BF),
            pltpu.VMEM((2, 3, 3, C, half), BF),
            pltpu.VMEM((2, 3, 3, C, half), BF),
            pltpu.VMEM((2, 3, 16, 3, 16, half), BF),
            pltpu.VMEM((19, 16, half), BF),
            pltpu.VMEM((PLANES, 3, 16, half), BF),
            pltpu.VMEM((3, 16, half), BF),
            pltpu.VMEM((2, 9, 2, 16, half), BF),
            pltpu.SemaphoreType.DMA((8,)),
            pltpu.SemaphoreType.DMA((8,)),
            pltpu.SemaphoreType.DMA,
            pltpu.SemaphoreType.DMA,
            pltpu.SemaphoreType.DMA((2, 3)),
            pltpu.SemaphoreType.DMA((2, 3)),
            pltpu.SemaphoreType.DMA((2, 3)),
            pltpu.SemaphoreType.DMA((2, 3)),
            pltpu.SemaphoreType.DMA,
            pltpu.SemaphoreType.DMA,
            pltpu.SemaphoreType.DMA((3, LON)),
            pltpu.SemaphoreType.DMA,
        ],
        compiler_params=pltpu.CompilerParams(
            collective_id=0, has_side_effects=True, vmem_limit_bytes=56 * 1024 * 1024
        ),
        cost_estimate=pl.CostEstimate(
            flops=12 * T * T * 9 * C * C, bytes_accessed=6_000_000, transcendentals=2 * T * T * C
        ),
    )(field, first_weight, second_weight, cotangent, live_rows, polar_links)
    return (output, field_grad, grad1, grad2)


def solution(mesh):
    in_specs = (P("lat", "lon", None), P(), P(), P("lat", "lon", None), P("lon", "lat"), P())
    out_specs = (P("lat", "lon", None), P("lat", "lon", None), P("lat", None), P("lat", None))
    return jax.shard_map(local, mesh=mesh, in_specs=in_specs, out_specs=out_specs, check_vma=False)
```

```python
import math

import jax
import jax.numpy as jnp
from jax import lax
from jax.experimental import pallas as pl
from jax.experimental.pallas import tpu as pltpu
from jax.sharding import PartitionSpec as P

MESH = pl.DeviceIdType.MESH
BF = jnp.bfloat16
F32 = jnp.float32
C = 256
T = 32
EXT = T + 4
PX = EXT * T
RING = T + 2
MSG = 5 * T
STRIP = 40
LON = 16
LAT = 16
PLANES = 8
SHARE = 3 * T // 2 * 3
PICK = MSG + T


def dot(a, b):
    return jnp.dot(a, b, preferred_element_type=F32)


def gelu_parts(pre):
    cdf = 0.5 * (1.0 + lax.erf(pre * 0.7071067811865476))
    dens = jnp.exp(-0.5 * pre * pre) * 0.3989422804014327
    return (pre * cdf, cdf + pre * dens)


def rows(start, size=T):
    return pl.ds(pl.multiple_of(start * T, T), size)


def finish(made, back, sums, out, fgrad, grad1, grad2):
    out[...] = made[...]
    fgrad[...] = back[...]
    scale = 1.0 / math.sqrt(LON * T * LAT * T)
    for g, ref in enumerate((grad2, grad1)):
        for k in range(9):
            for h in range(2):
                ref[k * 16 : (k + 1) * 16, h * 128 : (h + 1) * 128] = sums[k, h, g].astype(F32) * scale


def kernel(
    field,
    w1_hbm,
    w2_hbm,
    cot,
    live_ref,
    links,
    out,
    fgrad,
    sums,
    sx,
    sd,
    sh,
    sg,
    zx,
    zd,
    zh,
    zg,
    zs,
    kz,
    fix,
    cols,
    corner,
    pre1,
    back2,
    slope,
    xt,
    dz,
    w1,
    w2,
    wt1,
    wt2,
    ext,
    send_ns,
    send_ew,
    send_dg,
    halo_ns,
    halo_ew,
    halo_dg,
    near,
    picked,
    arrived,
    gkeep,
    gsend,
    gpair,
    gsum,
    parts2,
    tiles,
    parts3,
    own,
    final,
    w_sem,
    hs_sem,
    hr_sem,
    pas_sem,
    par_sem,
    pbs_sem,
    pbr_sem,
    s1_sem,
    r1_sem,
    s2_sem,
    r2_sem,
    s3_sem,
    r3_sem,
    s4_sem,
    r4_sem,
):
    u, v = lax.axis_index("lon"), lax.axis_index("lat")
    core, x, z = u % 2, u // 4, v // 2
    y = (u // 2) % 2 * 2 + v % 2
    spot = x * 4 + y
    north, south = v == 0, v == LAT - 1
    rim_tile = north | south
    side = jnp.where(south, 1, 0)
    live = live_ref[0, 0]
    east, west = (u + 1) % LON, (u + LON - 1) % LON

    def in_plane(place):
        px, py = place // 4, place % 4
        return {"lon": px * 4 + py // 2 * 2 + core, "lat": z * 2 + py % 2}

    def quarter(d):
        return u // 4 * 4 + (u % 4 + d) % 4

    w1_copy = pltpu.make_async_copy(w1_hbm, w1, w_sem.at[0])
    w2_copy = pltpu.make_async_copy(w2_hbm, w2, w_sem.at[1])
    w1_copy.start()
    w2_copy.start()

    barrier = pltpu.get_barrier_semaphore()

    def greet(lon, lat):
        pl.semaphore_signal(barrier, inc=1, device_id={"lon": lon, "lat": lat}, device_id_type=MESH)

    greet(east, v)
    greet(west, v)

    @pl.when(v > 0)
    def _():
        for lon in (west, u, east):
            greet(lon, v - 1)

    @pl.when(v < LAT - 1)
    def _():
        for lon in (west, u, east):
            greet(lon, v + 1)

    @pl.when(rim_tile)
    def _():
        for d in range(1, 4):
            greet(quarter(d), v)
            greet((u + 4 * d) % LON, v)

    @pl.loop(1, 16)
    def _(d):
        to = in_plane((spot + d) % 16)
        greet(to["lon"], to["lat"])

    @pl.loop(1, PLANES)
    def _(d):
        greet(u, (z + d) % PLANES * 2 + v % 2)

    lane_row = lax.broadcasted_iota(jnp.int32, (T, C), 0)

    @pl.loop(0, T)
    def _(i):
        kept = jnp.full((T, C), i, jnp.int32) < live
        for k, (src, dst) in enumerate(((field, sx), (cot, sd))):
            line = jnp.where(kept, src[i].astype(F32), 0.0)
            dst[1, rows(i + 2), :] = line.astype(BF)
            for n, col in enumerate((0, 1, T - 2, T - 1)):
                cols[k, n, pl.ds(i, 1), :] = line[col : col + 1]

    keep_col = jnp.where(lane_row < live, 1.0, 0.0)
    keep_last = jnp.where(jnp.full((T, C), T - 1, jnp.int32) < live, 1.0, 0.0)
    for s in range(2):
        for k, src in enumerate((sx, sd)):
            first = 2 if s == 0 else T
            send_ns[s, 2 * k * T : (2 * k + 2) * T, :] = src[1, first * T : (first + 2) * T, :]
            for n in range(2):
                send_ew[s, (2 * k + n) * T : (2 * k + n + 1) * T, :] = cols[k, 2 * s + n].astype(BF)
        send_ns[s, 4 * T :, :] = jnp.ones((T, C), BF) if s == 0 else keep_last.astype(BF)
        send_ew[s, 4 * T :, :] = keep_col.astype(BF)
    corner[...] = jnp.zeros_like(corner)
    for s in range(2):
        for t in range(2):
            for k in range(2):
                for r in range(2):
                    for n in range(2):
                        at = 4 * k + 2 * r + n
                        line = (0 if s == 0 else T - 2) + r
                        corner[2 * s + t, at : at + 1, :] = cols[k, 2 * t + n, line : line + 1, :]
            corner[2 * s + t, 8:9, :] = jnp.ones((1, C), F32) if s == 0 else keep_last[0:1]
    send_dg[...] = corner[...].astype(BF)

    here = jnp.where(v > 0, 3, 0) + jnp.where(v < LAT - 1, 3, 0) + jnp.where(rim_tile, 6, 0)
    pl.semaphore_wait(barrier, here + 2 + 15 + 7)

    def remote(src, dst, send, recv, to):
        return pltpu.make_async_remote_copy(
            src_ref=src, dst_ref=dst, send_sem=send, recv_sem=recv, device_id=to, device_id_type=MESH
        )

    def drain(ref, sem):
        pltpu.make_async_copy(ref, ref, sem).wait()

    def edge(src, dst, n, lon, lat):
        return remote(src, dst, hs_sem.at[n], hr_sem.at[n], {"lon": lon, "lat": lat})

    @pl.when(rim_tile)
    def _():
        for d in range(1, 4):
            remote(send_ns.at[side], near.at[u % 4], pas_sem, par_sem, {"lon": quarter(d), "lat": v}).start()

    to_west = edge(send_ew.at[0], halo_ew.at[1], 0, west, v)
    to_east = edge(send_ew.at[1], halo_ew.at[0], 1, east, v)
    to_north = [
        edge(send_ns.at[0], halo_ns.at[1], 2, u, v - 1),
        edge(send_dg.at[0], halo_dg.at[3], 3, west, v - 1),
        edge(send_dg.at[1], halo_dg.at[2], 4, east, v - 1),
    ]
    to_south = [
        edge(send_ns.at[1], halo_ns.at[0], 5, u, v + 1),
        edge(send_dg.at[2], halo_dg.at[1], 6, west, v + 1),
        edge(send_dg.at[3], halo_dg.at[0], 7, east, v + 1),
    ]

    to_west.start()
    to_east.start()

    @pl.when(v > 0)
    def _():
        for copy in to_north:
            copy.start()

    @pl.when(v < LAT - 1)
    def _():
        for copy in to_south:
            copy.start()

    @pl.loop(2, 34)
    def _(e):
        at = rows(e)
        for s in (sx, sd):
            line = s[1, at, :].astype(F32)
            s[0, at, :] = jnp.where(lane_row == 0, 0.0, pltpu.roll(line, 1, 0)).astype(BF)
            s[2, at, :] = jnp.where(lane_row == T - 1, 0.0, pltpu.roll(line, T - 1, 0)).astype(BF)

    for ref in (zx, zd, zh, zg, zs, ext, kz):
        ref[...] = jnp.zeros_like(ref)
    for b in range(3):
        sh[b, 0:T, :] = jnp.zeros((T, C), BF)
        sh[b, PX - T : PX, :] = jnp.zeros((T, C), BF)
    dz[0 : 3 * T, :] = jnp.zeros((3 * T, C), BF)
    dz[35 * T : 38 * T, :] = jnp.zeros((3 * T, C), BF)
    dz[3 * T : 35 * T, :] = sd[1, 2 * T : 34 * T, :]
    tiles[:, 9] = jnp.zeros((2, 16, C // 2), BF)

    def window(s, back, first, size):
        pieces = []
        for a in range(3):
            for b in range(3):
                start = (first + (2 - a if back else a)) * T
                pieces.append(s[2 - b if back else b, start : start + size * T, :])
        return jnp.concatenate(pieces, axis=1)

    w1_copy.wait()
    pre1[2 * T : 32 * T, :] = dot(window(sx, False, 2, 30), w1[...])

    @pl.when(rim_tile)
    def _():
        drain(near.at[pl.ds(0, 3)], par_sem)
        drain(near.at[pl.ds(0, 3)], pas_sem)
        near[u % 4] = send_ns[side]
        pivot = links[side, 0]
        n = lax.broadcasted_iota(jnp.int32, (8 * T, 4 * T), 0)
        at = lax.broadcasted_iota(jnp.int32, (8 * T, 4 * T), 1) + x * (4 * T)
        to = (n // (2 * T)) * 4 + u % 4
        n = n & (2 * T - 1)
        q = n & 15
        in_east = n >= T + 16
        ring_col = jnp.where(in_east, T, -1)
        outer_col = jnp.where(in_east, T, -2) + (q & 1)
        col = jnp.where(n < T, n, jnp.where(q == 8, ring_col, outer_col))
        hit = ((pivot - to * T - col) & (LON * T - 1)) == at
        line = jnp.where(q == 8, 4, jnp.where(q < 8, q // 2, 5))
        corners = jnp.zeros((4, T, C), F32)
        for part in range(5):
            target = part if part == 4 else part ^ 1
            pick = jnp.where(hit & ((n < T) | (line == target)), 1.0, 0.0).astype(BF)
            lines = near[:, part * T : (part + 1) * T, :].reshape(4 * T, C)
            found = dot(pick, lines).reshape(4, 2 * T, C)
            picked[:, target * T : (target + 1) * T, :] = found[:, :T].astype(BF)
            corners = corners + found[:, T:]
        picked[:, MSG:, :] = corners.astype(BF)
        for d in range(1, 4):
            to = (x + d) % 4
            remote(picked.at[to], arrived.at[x], pbs_sem, pbr_sem, {"lon": (u + 4 * d) % LON, "lat": v}).start()

    w2_copy.wait()

    @pl.loop(0, 9)
    def _(tap):
        at = pl.ds(pl.multiple_of(tap * C, C), C)
        wt2[at, :] = w2[at, :].T

    back2[2 * T : 32 * T, :] = dot(window(sd, True, 2, 30), wt2[...])

    to_west.wait_recv()
    to_east.wait_recv()

    @pl.when(v > 0)
    def _():
        for copy in to_south:
            copy.wait_recv()

    @pl.when(v < LAT - 1)
    def _():
        for copy in to_north:
            copy.wait_recv()

    @pl.when(rim_tile)
    def _():
        drain(arrived.at[pl.ds(0, 3)], pbr_sem)
        drain(arrived.at[pl.ds(0, 3)], pbs_sem)
        arrived[x] = picked[x]
        total = arrived[0].astype(F32)
        for k in range(1, 4):
            total = total + arrived[k].astype(F32)
        halo_ns[side] = total[:MSG].astype(BF)
        halo_dg[2 * side] = total[MSG : MSG + 16].astype(BF)
        halo_dg[2 * side + 1] = total[MSG + 16 :].astype(BF)

    head = lax.broadcasted_iota(jnp.int32, (16, C), 0)
    for k, (s, zz) in enumerate(((sx, zx), (sd, zd))):
        for n in range(2):
            zz[n, 2 : 2 + T, :] = halo_ew[0, (2 * k + n) * T : (2 * k + n + 1) * T, :].astype(F32)
            zz[4 + n, 2 : 2 + T, :] = halo_ew[1, (2 * k + n) * T : (2 * k + n + 1) * T, :].astype(F32)
            zz[2 + n, 2 : 2 + T, :] = cols[k, 3 * n]
        for dg in range(4):
            px = halo_dg[dg].astype(F32)
            for r in range(2):
                for n in range(2):
                    e = dg // 2 * 34 + r
                    at = 4 * k + 2 * r + n
                    zz[dg % 2 * 4 + n, e : e + 1, :] = px[at : at + 1]
        for e in (0, 1, 34, 35):
            h, r = e // 34, e % 34
            line = halo_ns[h, (2 * k + r) * T : (2 * k + r + 1) * T, :].astype(F32)
            s[1, e * T : (e + 1) * T, :] = line.astype(BF)
            s[0, e * T : (e + 1) * T, :] = jnp.where(
                lane_row == 0, zz[1, e : e + 1, :], pltpu.roll(line, 1, 0)
            ).astype(BF)
            s[2, e * T : (e + 1) * T, :] = jnp.where(
                lane_row == T - 1, zz[4, e : e + 1, :], pltpu.roll(line, T - 1, 0)
            ).astype(BF)
            zz[2, e : e + 1, :] = line[0:1]
            zz[3, e : e + 1, :] = line[T - 1 : T]

    def insert(s, zz, e):
        at = pl.ds(pl.multiple_of(e * T, T), 16)
        s[0, at, :] = jnp.where(head == 0, zz[1, pl.ds(e, 1), :], s[0, at, :].astype(F32)).astype(BF)
        at = pl.ds(pl.multiple_of(e * T + 16, 16), 16)
        s[2, at, :] = jnp.where(head == 15, zz[4, pl.ds(e, 1), :], s[2, at, :].astype(F32)).astype(BF)

    for e in (2, 3, 32, 33):
        insert(sd, zd, e)

    @pl.loop(2, 34)
    def _(e):
        insert(sx, zx, e)

    for t in range(2):
        kz[t, 2 : 2 + T, :] = halo_ew[t, 4 * T :, :].astype(F32)
        kz[t, 1:2, :] = halo_dg[t].astype(F32)[8:9]
        kz[t, 34:35, :] = halo_dg[2 + t].astype(F32)[8:9]

    def transposed(s):
        @pl.loop(0, PX // 128)
        def _(k):
            at = pl.ds(pl.multiple_of(k * 128, 128), 128)
            for b in range(3):
                xt[b * C : (b + 1) * C, at] = s[b, at, :].T

    e_out, e_ring = jnp.where(south, 35, 0), jnp.where(south, 34, 1)
    e_edge, e_in = jnp.where(south, 33, 2), jnp.where(south, 32, 3)
    far = jnp.where(south, 2, 0)

    def extend(n, s, left, right, e):
        ext[n, 2 : 2 + T, :] = s[1, rows(e), :].astype(F32)
        for k, ref in enumerate(left):
            at = 2 - len(left) + k
            ext[n, at : at + 1, :] = ref[pl.ds(e, 1), :]
        for k, ref in enumerate(right):
            ext[n, 34 + k : 35 + k, :] = ref[pl.ds(e, 1), :]

    def straight(n):
        return jnp.concatenate([ext[n, 2 - b : 42 - b, :] for b in range(3)], axis=1).astype(BF)

    def turned(n):
        return jnp.concatenate([ext[n, b : b + 40, :] for b in range(3)], axis=1).astype(BF)

    def taps(w, row):
        return w[pl.ds(pl.multiple_of(row * 3 * C, 3 * C), 3 * C), :]

    def combine(up, mid, down, back):
        if back:
            up, down = down, up
        return pltpu.roll(up, 1, 0) + mid + pltpu.roll(down, mid.shape[0] - 1, 0)

    def strips(zz, w, back):
        order = (2, 1, 0) if back else (0, 1, 2)
        both = jnp.concatenate(
            [jnp.concatenate([zz[3 * t + b] for b in order], axis=1) for t in range(2)], axis=0
        ).astype(BF)
        ring = combine(*(dot(both, w[a * 3 * C : (a + 1) * 3 * C, :]) for a in range(3)), back)
        row = lax.broadcasted_iota(jnp.int32, (STRIP, C), 0)
        for t in range(2):
            b = 2 - 2 * t if back else 2 * t
            line = zz[1 + 3 * t].astype(BF)
            res = combine(*(dot(line, w[(3 * a + b) * C : (3 * a + b + 1) * C, :]) for a in range(3)), back)
            fix[t] = jnp.where((row > 2) & (row < 33), res, 0.0)
        return ring

    def with_fix(line, e):
        line = line + jnp.where(lane_row == 0, fix[0, pl.ds(e, 1), :], 0.0)
        return line + jnp.where(lane_row == T - 1, fix[1, pl.ds(e, 1), :], 0.0)

    def spread(s, zz, e, line):
        at = rows(e)
        s[1, at, :] = line.astype(BF)
        s[0, at, :] = jnp.where(lane_row == 0, zz[0, pl.ds(e, 1), :], pltpu.roll(line, 1, 0)).astype(BF)
        s[2, at, :] = jnp.where(lane_row == T - 1, zz[1, pl.ds(e, 1), :], pltpu.roll(line, T - 1, 0)).astype(BF)

    def outer(s, back):
        return jnp.concatenate([window(s, back, 0, 2), window(s, back, 32, 2)], axis=0)

    res = dot(outer(sx, False), w1[...])
    pre1[0 : 2 * T, :] = res[: 2 * T]
    pre1[32 * T : 34 * T, :] = res[2 * T :]
    ring = strips(zx, w1, False)
    for t in range(2):
        zh[t] = ring[t * STRIP : (t + 1) * STRIP]

    @pl.when(rim_tile)
    def _():
        for n, e in enumerate((e_out, e_ring, e_edge)):
            extend(n, sx, (zx.at[0], zx.at[1]), (zx.at[4], zx.at[5]), e)
        pre = dot(straight(2), taps(w1, far)) + dot(straight(1), taps(w1, 1)) + dot(straight(0), taps(w1, 2 - far))
        pre1[rows(e_ring - 1), :] = pre[1 : 1 + T]
        for t in range(2):
            at = t * (T + 1)
            zh[t, pl.ds(e_ring, 1), :] = pre[at : at + 1]

    for t in range(2):
        act, slp = gelu_parts(zh[t])
        zh[t] = act * kz[t]
        zs[t] = slp * kz[t]

    def activate(e, mask):
        act, slp = gelu_parts(with_fix(pre1[rows(e - 1), :], e))
        slope[rows(e - 1), :] = slp * mask
        spread(sh, zh, e, act * mask)

    for s in range(2):
        activate(1 + 33 * s, halo_ns[s, 4 * T :, :].astype(F32))

    @pl.loop(2, 34)
    def _(e):
        activate(e, jnp.where(jnp.full((T, C), e - 2, jnp.int32) < live, 1.0, 0.0))

    transposed(sh)

    sibling = {"lon": u + 1 - 2 * core, "lat": v}

    def pair(g, a):
        return remote(gsend.at[g, a], gpair.at[g, a], s1_sem.at[g, a], r1_sem.at[g, a], sibling)

    def scatter(g, a):
        pair(g, a).wait()
        gsum[g, a] = (gkeep[g, a] + gpair[g, a].astype(F32)).astype(BF)

        @pl.loop(1, 16)
        def _(d):
            to = (spot + d) % 16
            remote(
                gsum.at[g, a, :, pl.ds(pl.multiple_of(to * 16, 16), 16), :],
                parts2.at[g, a, spot],
                s2_sem.at[g, a],
                r2_sem.at[g, a],
                in_plane(to),
            ).start()

    def weight_grad(g):
        @pl.loop(0, 3)
        def _(a):
            res = dot(xt[...], dz[rows(2 - a, PX), :])
            lo, hi = res[:, : C // 2], res[:, C // 2 :]
            gkeep[g, a] = jnp.where(core == 0, lo, hi).reshape(3, C, C // 2)
            gsend[g, a] = jnp.where(core == 0, hi, lo).astype(BF).reshape(3, C, C // 2)
            pair(g, a).start()

            @pl.when(a > 0)
            def _():
                scatter(g, a - 1)

    weight_grad(0)

    res = dot(outer(sd, True), wt2[...])
    back2[0 : 2 * T, :] = res[: 2 * T]
    back2[32 * T : 34 * T, :] = res[2 * T :]
    ring = strips(zd, wt2, True)
    for t in range(2):
        zg[t] = ring[t * STRIP : (t + 1) * STRIP]

    @pl.when(rim_tile)
    def _():
        for n, e in enumerate((e_out, e_ring, e_edge, e_in)):
            extend(n, sd, (zd.at[0], zd.at[1]), (zd.at[4], zd.at[5]), e)
        w_far, w_mid = taps(wt2, far), taps(wt2, 1)
        ring = dot(turned(0), w_far) + dot(straight(2), w_far) + dot(turned(1), w_mid)
        rim = dot(turned(1), w_far) + dot(straight(3), w_far) + dot(straight(2), w_mid)
        for e, res in ((e_ring, ring), (e_edge, rim)):
            back2[rows(e - 1), :] = res[1 : 1 + T]
            for t in range(2):
                at = t * (T + 1)
                zg[t, pl.ds(e, 1), :] = res[at : at + 1]

    for t in range(2):
        zg[t] = zg[t] * zs[t]
    scatter(0, 2)

    @pl.loop(1, 35)
    def _(e):
        spread(sg, zg, e, with_fix(back2[rows(e - 1), :], e) * slope[rows(e - 1), :])

    dz[3 * T : 35 * T, :] = sg[1, 2 * T : 34 * T, :]
    transposed(sx)
    weight_grad(1)

    row = lax.broadcasted_iota(jnp.int32, (T * T, C), 0) // T
    pre = dot(window(sh, False, 1, T), w2[...])
    masked = sx[1, 2 * T : 34 * T, :].astype(F32)
    out[...] = (masked + jnp.where(row < live, pre, 0.0)).astype(BF).reshape(T, T, C)

    @pl.loop(0, 9)
    def _(tap):
        at = pl.ds(pl.multiple_of(tap * C, C), C)
        wt1[at, :] = w1[at, :].T

    scatter(1, 2)

    back = dot(window(sg, True, 1, T), wt1[...])
    total = cot[...].reshape(T * T, C).astype(F32) + back
    fgrad[...] = jnp.where(row < live, total, 0.0).astype(BF).reshape(T, T, C)

    @pl.when(rim_tile)
    def _():
        for n, e in ((1, e_ring), (2, e_edge), (3, e_in)):
            extend(n, sg, (zg.at[0],), (zg.at[1],), e)
        w_far, w_mid = taps(wt1, far), taps(wt1, 1)
        rim = dot(turned(1), w_far) + dot(straight(3), w_far) + dot(straight(2), w_mid)
        i = e_edge - 2
        total = cot[i].astype(F32) + rim[1 : 1 + T]
        kept = jnp.full((T, C), i, jnp.int32) < live
        fgrad[i] = jnp.where(kept, total, 0.0).astype(BF)

    for g in range(2):
        for a in range(3):
            drain(parts2.at[g, a, pl.ds(0, 15)], r2_sem.at[g, a])
            parts2[g, a, spot] = gsum[g, a, :, pl.ds(pl.multiple_of(spot * 16, 16), 16), :]
            total = parts2[g, a, 0].astype(F32)
            for k in range(1, 16):
                total = total + parts2[g, a, k].astype(F32)
            tiles[g, 3 * a : 3 * a + 3] = total.astype(BF)

    def first_tile(plane):
        return (18 * plane + 15 - spot) // 16

    @pl.loop(1, PLANES)
    def _(d):
        to = (z + d) % PLANES
        remote(
            tiles.at[:, pl.ds(first_tile(to), 2)],
            parts3.at[z],
            s3_sem,
            r3_sem,
            {"lon": u, "lat": to * 2 + v % 2},
        ).start()

    mine = first_tile(z)
    drain(parts3.at[pl.ds(0, PLANES - 1)], r3_sem)
    parts3[z] = tiles[:, pl.ds(mine, 2)]
    total = parts3[0].astype(F32)
    for k in range(1, PLANES):
        total = total + parts3[k].astype(F32)
    for slot in range(2):
        own[slot] = total[:, slot].astype(BF)

    def deliver(slot):
        group = (mine + slot) * 16 + spot
        lat, at = group // 9, group % 9
        src, dst = own.at[slot], final.at[at, core]

        def to(d):
            return remote(src, dst, s4_sem.at[slot, d], r4_sem, {"lon": (u + d) % LON, "lat": lat})

        @pl.loop(1, LON)
        def _(d):
            to(d).start()

        @pl.when(lat == v)
        def _():
            pltpu.make_async_copy(src, dst, r4_sem).start()

        @pl.when(lat != v)
        def _():
            to(0).start()

        def left():
            @pl.loop(1, LON)
            def _(d):
                to(d).wait_send()

            @pl.when(lat != v)
            def _():
                to(0).wait_send()

        return left

    has_two = first_tile(z + 1) - mine == 2
    left0 = deliver(0)

    @pl.when(has_two)
    def _():
        deliver(1)

    drain(final, r4_sem)
    sums[...] = final[...]

    left0()

    @pl.when(has_two)
    def _():
        group = (mine + 1) * 16 + spot
        lat = group // 9
        dst = final.at[group % 9, core]

        def to(d):
            return remote(own.at[1], dst, s4_sem.at[1, d], r4_sem, {"lon": (u + d) % LON, "lat": lat})

        @pl.loop(1, LON)
        def _(d):
            to(d).wait_send()

        @pl.when(lat != v)
        def _():
            to(0).wait_send()

    to_west.wait_send()
    to_east.wait_send()

    @pl.when(v > 0)
    def _():
        for copy in to_north:
            copy.wait_send()

    @pl.when(v < LAT - 1)
    def _():
        for copy in to_south:
            copy.wait_send()

    for g in range(2):
        for a in range(3):
            drain(parts2.at[g, a, pl.ds(0, 15)], s2_sem.at[g, a])
    drain(parts3.at[pl.ds(0, PLANES - 1)], s3_sem)


def local(field, first_weight, second_weight, cotangent, live_rows, polar_links):
    vmem = pl.BlockSpec(memory_space=pltpu.VMEM)
    smem = pl.BlockSpec(memory_space=pltpu.SMEM)
    anywhere = pl.BlockSpec(memory_space=pl.ANY)
    half = C // 2
    tile = jax.ShapeDtypeStruct((T, T, C), BF)
    share = jax.ShapeDtypeStruct((SHARE, C), F32)
    flat = pltpu.VMEM((3, PX, C), BF)
    columns = pltpu.VMEM((6, STRIP, C), F32)
    two = pltpu.VMEM((2, STRIP, C), F32)
    ringed = pltpu.VMEM((RING * T, C), F32)
    weights = pltpu.VMEM((9 * C, C), BF)
    message = pltpu.VMEM((2, MSG, C), BF)
    corners = pltpu.VMEM((4, 16, C), BF)
    grads = pltpu.VMEM((2, 3, 3, C, half), BF)
    dma = pltpu.SemaphoreType.DMA
    made, back, sums = pl.pallas_call(
        kernel,
        out_shape=(tile, tile, jax.ShapeDtypeStruct((9, 2, 2, 16, half), BF)),
        in_specs=[vmem, anywhere, anywhere, vmem, smem, smem],
        out_specs=(vmem, vmem, vmem),
        scratch_shapes=[
            *([flat] * 4),
            *([columns] * 2),
            *([two] * 5),
            pltpu.VMEM((2, 4, T, C), F32),
            pltpu.VMEM((4, 16, C), F32),
            *([ringed] * 3),
            pltpu.VMEM((3 * C, PX), BF),
            pltpu.VMEM((38 * T, C), BF),
            *([weights] * 4),
            pltpu.VMEM((4, 48, C), F32),
            message,
            message,
            corners,
            message,
            message,
            corners,
            pltpu.VMEM((4, MSG, C), BF),
            pltpu.VMEM((4, PICK, C), BF),
            pltpu.VMEM((4, PICK, C), BF),
            pltpu.VMEM((2, 3, 3, C, half), F32),
            grads,
            grads,
            grads,
            pltpu.VMEM((2, 3, 16, 3, 16, half), BF),
            pltpu.VMEM((2, 10, 16, half), BF),
            pltpu.VMEM((PLANES, 2, 2, 16, half), BF),
            pltpu.VMEM((2, 2, 16, half), BF),
            pltpu.VMEM((9, 2, 2, 16, half), BF),
            dma((2,)),
            dma((8,)),
            dma((8,)),
            dma,
            dma,
            dma,
            dma,
            dma((2, 3)),
            dma((2, 3)),
            dma((2, 3)),
            dma((2, 3)),
            dma,
            dma,
            dma((2, LON)),
            dma,
        ],
        compiler_params=pltpu.CompilerParams(
            collective_id=0, has_side_effects=True, vmem_limit_bytes=56 * 1024 * 1024
        ),
        cost_estimate=pl.CostEstimate(
            flops=12 * T * T * 9 * C * C, bytes_accessed=6_000_000, transcendentals=2 * T * T * C
        ),
    )(field, first_weight, second_weight, cotangent, live_rows, polar_links)
    return pl.pallas_call(
        finish,
        out_shape=(tile, tile, share, share),
        in_specs=[vmem] * 3,
        out_specs=(vmem,) * 4,
        cost_estimate=pl.CostEstimate(flops=2 * SHARE * C, bytes_accessed=3_000_000, transcendentals=0),
    )(made, back, sums)


def solution(mesh):
    in_specs = (P("lat", "lon", None), P(), P(), P("lat", "lon", None), P("lon", "lat"), P())
    out_specs = (P("lat", "lon", None), P("lat", "lon", None), P("lat", None), P("lat", None))
    return jax.shard_map(local, mesh=mesh, in_specs=in_specs, out_specs=out_specs, check_vma=False)
```

```python
import math

import jax
import jax.numpy as jnp
from jax import lax
from jax.experimental import pallas as pl
from jax.experimental.pallas import tpu as pltpu
from jax.sharding import PartitionSpec as P

MESH = pl.DeviceIdType.MESH
BF = jnp.bfloat16
F32 = jnp.float32
C = 256
T = 32
EXT = T + 4
PX = EXT * T
RING = T + 2
MSG = 5 * T
STRIP = 40
LON = 16
LAT = 16
PLANES = 8
SHARE = 3 * T // 2 * 3
PICK = MSG + T


def dot(a, b):
    return jnp.dot(a, b, preferred_element_type=F32)


def gelu_parts(pre):
    cdf = 0.5 * (1.0 + lax.erf(pre * 0.7071067811865476))
    dens = jnp.exp(-0.5 * pre * pre) * 0.3989422804014327
    return (pre * cdf, cdf + pre * dens)


def rows(start, size=T):
    return pl.ds(pl.multiple_of(start * T, T), size)


def finish(made, back, sums, out, fgrad, grad1, grad2, share1, share2, sem):
    copies = [pltpu.make_async_copy(made, out, sem.at[0]), pltpu.make_async_copy(back, fgrad, sem.at[1])]
    for copy in copies:
        copy.start()
    scale = 1.0 / math.sqrt(LON * T * LAT * T)
    for g, (ref, dst) in enumerate(((share2, grad2), (share1, grad1))):
        for k in range(9):
            for h in range(2):
                ref[k * 16 : (k + 1) * 16, h * 128 : (h + 1) * 128] = sums[k, h, g].astype(F32) * scale
        copies.append(pltpu.make_async_copy(ref, dst, sem.at[2 + g]))
        copies[-1].start()
    for copy in copies:
        copy.wait()


def kernel(
    field_hbm,
    w1_hbm,
    w2_hbm,
    cot_hbm,
    live_ref,
    links,
    out,
    fgrad,
    sums,
    sx,
    sd,
    sh,
    sg,
    zx,
    zd,
    zh,
    zg,
    zs,
    kz,
    field,
    cot,
    cols,
    corner,
    pre1,
    back2,
    slope,
    xt,
    dz,
    w1,
    w2,
    wt1,
    wt2,
    ext,
    send_ns,
    send_ew,
    send_dg,
    halo_ns,
    halo_ew,
    halo_dg,
    near,
    picked,
    arrived,
    gkeep,
    gsend,
    gpair,
    gsum,
    parts2,
    tiles,
    parts3,
    own,
    final,
    w_sem,
    hs_sem,
    hr_sem,
    pas_sem,
    par_sem,
    pbs_sem,
    pbr_sem,
    s1_sem,
    r1_sem,
    s2_sem,
    r2_sem,
    s3_sem,
    r3_sem,
    s4_sem,
    r4_sem,
):
    u, v = lax.axis_index("lon"), lax.axis_index("lat")
    core, x, z = u % 2, u // 4, v // 2
    y = (u // 2) % 2 * 2 + v % 2
    spot = x * 4 + y
    north, south = v == 0, v == LAT - 1
    rim_tile = north | south
    side = jnp.where(south, 1, 0)
    live = live_ref[0, 0]
    east, west = (u + 1) % LON, (u + LON - 1) % LON

    def in_plane(place):
        px, py = place // 4, place % 4
        return {"lon": px * 4 + py // 2 * 2 + core, "lat": z * 2 + py % 2}

    def quarter(d):
        return u // 4 * 4 + (u % 4 + d) % 4

    fetched = [
        pltpu.make_async_copy(src, dst, w_sem.at[n])
        for n, (src, dst) in enumerate(((field_hbm, field), (cot_hbm, cot), (w1_hbm, w1), (w2_hbm, w2)))
    ]
    for copy in fetched:
        copy.start()

    barrier = pltpu.get_barrier_semaphore()

    def greet(lon, lat):
        pl.semaphore_signal(barrier, inc=1, device_id={"lon": lon, "lat": lat}, device_id_type=MESH)

    greet(east, v)
    greet(west, v)

    @pl.when(v > 0)
    def _():
        for lon in (west, u, east):
            greet(lon, v - 1)

    @pl.when(v < LAT - 1)
    def _():
        for lon in (west, u, east):
            greet(lon, v + 1)

    @pl.when(rim_tile)
    def _():
        for d in range(1, 4):
            greet(quarter(d), v)
            greet((u + 4 * d) % LON, v)

    @pl.loop(1, 16)
    def _(d):
        to = in_plane((spot + d) % 16)
        greet(to["lon"], to["lat"])

    @pl.loop(1, PLANES)
    def _(d):
        greet(u, (z + d) % PLANES * 2 + v % 2)

    lane_row = lax.broadcasted_iota(jnp.int32, (T, C), 0)
    fetched[0].wait()
    fetched[1].wait()

    @pl.loop(0, T)
    def _(i):
        kept = jnp.full((T, C), i, jnp.int32) < live
        for k, (src, dst) in enumerate(((field, sx), (cot, sd))):
            line = jnp.where(kept, src[i].astype(F32), 0.0)
            dst[1, rows(i + 2), :] = line.astype(BF)
            for n, col in enumerate((0, 1, T - 2, T - 1)):
                cols[k, n, pl.ds(i, 1), :] = line[col : col + 1]

    keep_col = jnp.where(lane_row < live, 1.0, 0.0)
    keep_last = jnp.where(jnp.full((T, C), T - 1, jnp.int32) < live, 1.0, 0.0)
    for s in range(2):
        for k, src in enumerate((sx, sd)):
            first = 2 if s == 0 else T
            send_ns[s, 2 * k * T : (2 * k + 2) * T, :] = src[1, first * T : (first + 2) * T, :]
            for n in range(2):
                send_ew[s, (2 * k + n) * T : (2 * k + n + 1) * T, :] = cols[k, 2 * s + n].astype(BF)
        send_ns[s, 4 * T :, :] = jnp.ones((T, C), BF) if s == 0 else keep_last.astype(BF)
        send_ew[s, 4 * T :, :] = keep_col.astype(BF)
    corner[...] = jnp.zeros_like(corner)
    for s in range(2):
        for t in range(2):
            for k in range(2):
                for r in range(2):
                    for n in range(2):
                        at = 4 * k + 2 * r + n
                        line = (0 if s == 0 else T - 2) + r
                        corner[2 * s + t, at : at + 1, :] = cols[k, 2 * t + n, line : line + 1, :]
            corner[2 * s + t, 8:9, :] = jnp.ones((1, C), F32) if s == 0 else keep_last[0:1]
    send_dg[...] = corner[...].astype(BF)

    here = jnp.where(v > 0, 3, 0) + jnp.where(v < LAT - 1, 3, 0) + jnp.where(rim_tile, 6, 0)
    pl.semaphore_wait(barrier, here + 2 + 15 + 7)

    def remote(src, dst, send, recv, to):
        return pltpu.make_async_remote_copy(
            src_ref=src, dst_ref=dst, send_sem=send, recv_sem=recv, device_id=to, device_id_type=MESH
        )

    def drain(ref, sem):
        pltpu.make_async_copy(ref, ref, sem).wait()

    def edge(src, dst, n, lon, lat):
        return remote(src, dst, hs_sem.at[n], hr_sem.at[n], {"lon": lon, "lat": lat})

    @pl.when(rim_tile)
    def _():
        for d in range(1, 4):
            remote(send_ns.at[side], near.at[u % 4], pas_sem, par_sem, {"lon": quarter(d), "lat": v}).start()

    to_west = edge(send_ew.at[0], halo_ew.at[1], 0, west, v)
    to_east = edge(send_ew.at[1], halo_ew.at[0], 1, east, v)
    to_north = [
        edge(send_ns.at[0], halo_ns.at[1], 2, u, v - 1),
        edge(send_dg.at[0], halo_dg.at[3], 3, west, v - 1),
        edge(send_dg.at[1], halo_dg.at[2], 4, east, v - 1),
    ]
    to_south = [
        edge(send_ns.at[1], halo_ns.at[0], 5, u, v + 1),
        edge(send_dg.at[2], halo_dg.at[1], 6, west, v + 1),
        edge(send_dg.at[3], halo_dg.at[0], 7, east, v + 1),
    ]

    to_west.start()
    to_east.start()

    @pl.when(v > 0)
    def _():
        for copy in to_north:
            copy.start()

    @pl.when(v < LAT - 1)
    def _():
        for copy in to_south:
            copy.start()

    @pl.loop(2, 34)
    def _(e):
        at = rows(e)
        for s in (sx, sd):
            line = s[1, at, :].astype(F32)
            s[0, at, :] = jnp.where(lane_row == 0, 0.0, pltpu.roll(line, 1, 0)).astype(BF)
            s[2, at, :] = jnp.where(lane_row == T - 1, 0.0, pltpu.roll(line, T - 1, 0)).astype(BF)

    for ref in (zx, zd, zh, zg, zs, ext, kz):
        ref[...] = jnp.zeros_like(ref)
    for b in range(3):
        sh[b, 0:T, :] = jnp.zeros((T, C), BF)
        sh[b, PX - T : PX, :] = jnp.zeros((T, C), BF)
    dz[0 : 3 * T, :] = jnp.zeros((3 * T, C), BF)
    dz[35 * T : 38 * T, :] = jnp.zeros((3 * T, C), BF)
    dz[3 * T : 35 * T, :] = sd[1, 2 * T : 34 * T, :]
    tiles[:, 9] = jnp.zeros((2, 16, C // 2), BF)

    def window(s, back, first, size):
        pieces = []
        for a in range(3):
            for b in range(3):
                start = (first + (2 - a if back else a)) * T
                pieces.append(s[2 - b if back else b, start : start + size * T, :])
        return jnp.concatenate(pieces, axis=1)

    def spread(s, left, right, e, line):
        at = rows(e)
        s[1, at, :] = line.astype(BF)
        s[0, at, :] = jnp.where(lane_row == 0, left, pltpu.roll(line, 1, 0)).astype(BF)
        s[2, at, :] = jnp.where(lane_row == T - 1, right, pltpu.roll(line, T - 1, 0)).astype(BF)

    fetched[2].wait()
    pre1[2 * T : 32 * T, :] = dot(window(sx, False, 2, 30), w1[...])

    @pl.loop(3, 33)
    def _(e):
        act, slp = gelu_parts(pre1[rows(e - 1), :])
        mask = jnp.where(jnp.full((T, C), e - 2, jnp.int32) < live, 1.0, 0.0)
        slope[rows(e - 1), :] = slp * mask
        spread(sh, 0.0, 0.0, e, act * mask)

    fetched[3].wait()

    @pl.loop(0, 9)
    def _(tap):
        at = pl.ds(pl.multiple_of(tap * C, C), C)
        wt2[at, :] = w2[at, :].T

    @pl.when(rim_tile)
    def _():
        drain(near.at[pl.ds(0, 3)], par_sem)
        drain(near.at[pl.ds(0, 3)], pas_sem)
        near[u % 4] = send_ns[side]
        pivot = links[side, 0]
        n = lax.broadcasted_iota(jnp.int32, (8 * T, 4 * T), 0)
        at = lax.broadcasted_iota(jnp.int32, (8 * T, 4 * T), 1) + x * (4 * T)
        to = (n // (2 * T)) * 4 + u % 4
        n = n & (2 * T - 1)
        q = n & 15
        in_east = n >= T + 16
        ring_col = jnp.where(in_east, T, -1)
        outer_col = jnp.where(in_east, T, -2) + (q & 1)
        col = jnp.where(n < T, n, jnp.where(q == 8, ring_col, outer_col))
        hit = ((pivot - to * T - col) & (LON * T - 1)) == at
        line = jnp.where(q == 8, 4, jnp.where(q < 8, q // 2, 5))
        corners = jnp.zeros((4, T, C), F32)
        for part in range(5):
            target = part if part == 4 else part ^ 1
            pick = jnp.where(hit & ((n < T) | (line == target)), 1.0, 0.0).astype(BF)
            lines = near[:, part * T : (part + 1) * T, :].reshape(4 * T, C)
            found = dot(pick, lines).reshape(4, 2 * T, C)
            picked[:, target * T : (target + 1) * T, :] = found[:, :T].astype(BF)
            corners = corners + found[:, T:]
        picked[:, MSG:, :] = corners.astype(BF)
        for d in range(1, 4):
            to = (x + d) % 4
            remote(picked.at[to], arrived.at[x], pbs_sem, pbr_sem, {"lon": (u + 4 * d) % LON, "lat": v}).start()

    back2[2 * T : 32 * T, :] = dot(window(sd, True, 2, 30), wt2[...])

    @pl.loop(3, 33)
    def _(e):
        spread(sg, 0.0, 0.0, e, back2[rows(e - 1), :] * slope[rows(e - 1), :])

    @pl.loop(0, 9)
    def _(tap):
        at = pl.ds(pl.multiple_of(tap * C, C), C)
        wt1[at, :] = w1[at, :].T

    to_west.wait_recv()
    to_east.wait_recv()

    @pl.when(v > 0)
    def _():
        for copy in to_south:
            copy.wait_recv()

    @pl.when(v < LAT - 1)
    def _():
        for copy in to_north:
            copy.wait_recv()

    @pl.when(rim_tile)
    def _():
        drain(arrived.at[pl.ds(0, 3)], pbr_sem)
        drain(arrived.at[pl.ds(0, 3)], pbs_sem)
        arrived[x] = picked[x]
        total = arrived[0].astype(F32)
        for k in range(1, 4):
            total = total + arrived[k].astype(F32)
        halo_ns[side] = total[:MSG].astype(BF)
        halo_dg[2 * side] = total[MSG : MSG + 16].astype(BF)
        halo_dg[2 * side + 1] = total[MSG + 16 :].astype(BF)

    head = lax.broadcasted_iota(jnp.int32, (16, C), 0)
    for k, (s, zz) in enumerate(((sx, zx), (sd, zd))):
        for n in range(2):
            zz[n, 2 : 2 + T, :] = halo_ew[0, (2 * k + n) * T : (2 * k + n + 1) * T, :].astype(F32)
            zz[6 + n, 2 : 2 + T, :] = halo_ew[1, (2 * k + n) * T : (2 * k + n + 1) * T, :].astype(F32)
            zz[2 + n, 2 : 2 + T, :] = cols[k, n]
            zz[4 + n, 2 : 2 + T, :] = cols[k, 2 + n]
        for dg in range(4):
            px = halo_dg[dg].astype(F32)
            for r in range(2):
                for n in range(2):
                    e = dg // 2 * 34 + r
                    at = 4 * k + 2 * r + n
                    zz[dg % 2 * 6 + n, e : e + 1, :] = px[at : at + 1]
        for e in (0, 1, 34, 35):
            h, r = e // 34, e % 34
            line = halo_ns[h, (2 * k + r) * T : (2 * k + r + 1) * T, :].astype(F32)
            spread(s, zz[1, e : e + 1, :], zz[6, e : e + 1, :], e, line)
            for n, col in enumerate((0, 1, T - 2, T - 1)):
                zz[2 + n, e : e + 1, :] = line[col : col + 1]

    def insert(s, zz, e):
        at = pl.ds(pl.multiple_of(e * T, T), 16)
        s[0, at, :] = jnp.where(head == 0, zz[1, pl.ds(e, 1), :], s[0, at, :].astype(F32)).astype(BF)
        at = pl.ds(pl.multiple_of(e * T + 16, 16), 16)
        s[2, at, :] = jnp.where(head == 15, zz[6, pl.ds(e, 1), :], s[2, at, :].astype(F32)).astype(BF)

    for e in (2, 3, 32, 33):
        insert(sd, zd, e)

    @pl.loop(2, 34)
    def _(e):
        insert(sx, zx, e)

    for t in range(2):
        kz[3 * t, 2 : 2 + T, :] = halo_ew[t, 4 * T :, :].astype(F32)
        kz[3 * t, 1:2, :] = halo_dg[t].astype(F32)[8:9]
        kz[3 * t, 34:35, :] = halo_dg[2 + t].astype(F32)[8:9]
        kz[1 + t, 2 : 2 + T, :] = keep_col
    for h in range(2):
        mask = halo_ns[h, 4 * T :, :].astype(F32)
        kz[1, 1 + 33 * h : 2 + 33 * h, :] = mask[0:1]
        kz[2, 1 + 33 * h : 2 + 33 * h, :] = mask[T - 1 : T]

    def transposed(s):
        @pl.loop(0, PX // 128)
        def _(k):
            at = pl.ds(pl.multiple_of(k * 128, 128), 128)
            for b in range(3):
                xt[b * C : (b + 1) * C, at] = s[b, at, :].T

    e_out, e_ring = jnp.where(south, 35, 0), jnp.where(south, 34, 1)
    e_edge, e_in = jnp.where(south, 33, 2), jnp.where(south, 32, 3)
    far = jnp.where(south, 2, 0)

    def extend(n, s, left, right, e):
        ext[n, 2 : 2 + T, :] = s[1, rows(e), :].astype(F32)
        for k, ref in enumerate(left):
            at = 2 - len(left) + k
            ext[n, at : at + 1, :] = ref[pl.ds(e, 1), :]
        for k, ref in enumerate(right):
            ext[n, 34 + k : 35 + k, :] = ref[pl.ds(e, 1), :]

    def straight(n):
        return jnp.concatenate([ext[n, 2 - b : 42 - b, :] for b in range(3)], axis=1).astype(BF)

    def turned(n):
        return jnp.concatenate([ext[n, b : b + 40, :] for b in range(3)], axis=1).astype(BF)

    def taps(w, row):
        return w[pl.ds(pl.multiple_of(row * 3 * C, 3 * C), 3 * C), :]

    def combine(up, mid, down, back):
        if back:
            up, down = down, up
        return pltpu.roll(up, 1, 0) + mid + pltpu.roll(down, mid.shape[0] - 1, 0)

    def strips(zz, w, back, ref):
        order = (2, 1, 0) if back else (0, 1, 2)
        lines = jnp.concatenate(
            [jnp.concatenate([zz[first + b] for b in order], axis=1) for first in (0, 1, 4, 5)], axis=0
        ).astype(BF)
        res = combine(*(dot(lines, w[a * 3 * C : (a + 1) * 3 * C, :]) for a in range(3)), back)
        for t in range(4):
            ref[t] = res[t * STRIP : (t + 1) * STRIP]

    def put_columns(s, zz):
        @pl.loop(3, 33)
        def _(e):
            c = [zz[t, pl.ds(e, 1), :] for t in range(4)]
            at = pl.ds(pl.multiple_of(e * T, T), 16)
            s[1, at, :] = jnp.where(head == 0, c[1], s[1, at, :].astype(F32)).astype(BF)
            line = jnp.where(head == 1, c[1], s[0, at, :].astype(F32))
            s[0, at, :] = jnp.where(head == 0, c[0], line).astype(BF)
            at = pl.ds(pl.multiple_of(e * T + 16, 16), 16)
            s[1, at, :] = jnp.where(head == 15, c[2], s[1, at, :].astype(F32)).astype(BF)
            line = jnp.where(head == 14, c[2], s[2, at, :].astype(F32))
            s[2, at, :] = jnp.where(head == 15, c[3], line).astype(BF)

    def of_row(res, t):
        at = (0, 1, T, T + 1)[t]
        return res[at : at + 1]

    def outer(s, back):
        return jnp.concatenate([window(s, back, 0, 2), window(s, back, 32, 2)], axis=0)

    res = dot(outer(sx, False), w1[...])
    pre1[0 : 2 * T, :] = res[: 2 * T]
    pre1[32 * T : 34 * T, :] = res[2 * T :]
    strips(zx, w1, False, zh)

    @pl.when(rim_tile)
    def _():
        for n, e in enumerate((e_out, e_ring, e_edge)):
            extend(n, sx, (zx.at[0], zx.at[1]), (zx.at[6], zx.at[7]), e)
        pre = dot(straight(2), taps(w1, far)) + dot(straight(1), taps(w1, 1)) + dot(straight(0), taps(w1, 2 - far))
        pre1[rows(e_ring - 1), :] = pre[1 : 1 + T]
        for t in range(4):
            zh[t, pl.ds(e_ring, 1), :] = of_row(pre, t)

    for t in range(4):
        act, slp = gelu_parts(zh[t])
        zh[t] = act * kz[t]
        zs[t] = slp * kz[t]

    def activate(e, mask):
        act, slp = gelu_parts(pre1[rows(e - 1), :])
        slope[rows(e - 1), :] = slp * mask
        spread(sh, zh[0, e : e + 1, :], zh[3, e : e + 1, :], e, act * mask)

    activate(1, halo_ns[0, 4 * T :, :].astype(F32))
    activate(2, jnp.where(jnp.zeros((T, C), jnp.int32) < live, 1.0, 0.0))
    activate(33, keep_last)
    activate(34, halo_ns[1, 4 * T :, :].astype(F32))
    put_columns(sh, zh)
    transposed(sh)

    sibling = {"lon": u + 1 - 2 * core, "lat": v}

    def pair(g, a):
        return remote(gsend.at[g, a], gpair.at[g, a], s1_sem.at[g, a], r1_sem.at[g, a], sibling)

    def scatter(g, a):
        pair(g, a).wait()
        gsum[g, a] = (gkeep[g, a] + gpair[g, a].astype(F32)).astype(BF)

        @pl.loop(1, 16)
        def _(d):
            to = (spot + d) % 16
            remote(
                gsum.at[g, a, :, pl.ds(pl.multiple_of(to * 16, 16), 16), :],
                parts2.at[g, a, spot],
                s2_sem.at[g, a],
                r2_sem.at[g, a],
                in_plane(to),
            ).start()

    def weight_grad(g):
        @pl.loop(0, 3)
        def _(a):
            res = dot(xt[...], dz[rows(2 - a, PX), :])
            lo, hi = res[:, : C // 2], res[:, C // 2 :]
            gkeep[g, a] = jnp.where(core == 0, lo, hi).reshape(3, C, C // 2)
            gsend[g, a] = jnp.where(core == 0, hi, lo).astype(BF).reshape(3, C, C // 2)
            pair(g, a).start()

            @pl.when(a > 0)
            def _():
                scatter(g, a - 1)

    weight_grad(0)

    res = dot(outer(sd, True), wt2[...])
    back2[0 : 2 * T, :] = res[: 2 * T]
    back2[32 * T : 34 * T, :] = res[2 * T :]
    strips(zd, wt2, True, zg)

    @pl.when(rim_tile)
    def _():
        for n, e in enumerate((e_out, e_ring, e_edge, e_in)):
            extend(n, sd, (zd.at[0], zd.at[1]), (zd.at[6], zd.at[7]), e)
        w_far, w_mid = taps(wt2, far), taps(wt2, 1)
        ring = dot(turned(0), w_far) + dot(straight(2), w_far) + dot(turned(1), w_mid)
        rim = dot(turned(1), w_far) + dot(straight(3), w_far) + dot(straight(2), w_mid)
        for e, res in ((e_ring, ring), (e_edge, rim)):
            back2[rows(e - 1), :] = res[1 : 1 + T]
            for t in range(4):
                zg[t, pl.ds(e, 1), :] = of_row(res, t)

    for t in range(4):
        zg[t] = zg[t] * zs[t]
    scatter(0, 2)
    for e in (1, 2, 33, 34):
        line = back2[rows(e - 1), :] * slope[rows(e - 1), :]
        spread(sg, zg[0, e : e + 1, :], zg[3, e : e + 1, :], e, line)
    put_columns(sg, zg)
    dz[3 * T : 35 * T, :] = sg[1, 2 * T : 34 * T, :]
    transposed(sx)
    weight_grad(1)

    size = T // 2

    def forward(first):
        row = lax.broadcasted_iota(jnp.int32, (size * T, C), 0) // T + first
        pre = dot(window(sh, False, 1 + first, size), w2[...])
        masked = sx[1, (2 + first) * T : (2 + first + size) * T, :].astype(F32)
        out[first : first + size] = (masked + jnp.where(row < live, pre, 0.0)).astype(BF).reshape(size, T, C)

    forward(0)
    scatter(1, 2)
    forward(size)

    row = lax.broadcasted_iota(jnp.int32, (T * T, C), 0) // T
    back = dot(window(sg, True, 1, T), wt1[...])
    total = cot[...].reshape(T * T, C).astype(F32) + back
    fgrad[...] = jnp.where(row < live, total, 0.0).astype(BF).reshape(T, T, C)

    @pl.when(rim_tile)
    def _():
        for n, e in ((1, e_ring), (2, e_edge), (3, e_in)):
            extend(n, sg, (zg.at[0],), (zg.at[3],), e)
        w_far, w_mid = taps(wt1, far), taps(wt1, 1)
        rim = dot(turned(1), w_far) + dot(straight(3), w_far) + dot(straight(2), w_mid)
        i = e_edge - 2
        total = cot[i].astype(F32) + rim[1 : 1 + T]
        kept = jnp.full((T, C), i, jnp.int32) < live
        fgrad[i] = jnp.where(kept, total, 0.0).astype(BF)

    for g in range(2):
        for a in range(3):
            drain(parts2.at[g, a, pl.ds(0, 15)], r2_sem.at[g, a])
            parts2[g, a, spot] = gsum[g, a, :, pl.ds(pl.multiple_of(spot * 16, 16), 16), :]
            total = parts2[g, a, 0].astype(F32)
            for k in range(1, 16):
                total = total + parts2[g, a, k].astype(F32)
            tiles[g, 3 * a : 3 * a + 3] = total.astype(BF)

    def first_tile(plane):
        return (18 * plane + 15 - spot) // 16

    @pl.loop(1, PLANES)
    def _(d):
        to = (z + d) % PLANES
        remote(
            tiles.at[:, pl.ds(first_tile(to), 2)],
            parts3.at[z],
            s3_sem,
            r3_sem,
            {"lon": u, "lat": to * 2 + v % 2},
        ).start()

    mine = first_tile(z)
    drain(parts3.at[pl.ds(0, PLANES - 1)], r3_sem)
    parts3[z] = tiles[:, pl.ds(mine, 2)]
    total = parts3[0].astype(F32)
    for k in range(1, PLANES):
        total = total + parts3[k].astype(F32)
    for slot in range(2):
        own[slot] = total[:, slot].astype(BF)

    def deliver(slot):
        group = (mine + slot) * 16 + spot
        lat, at = group // 9, group % 9
        src, dst = own.at[slot], final.at[at, core]

        def to(d):
            return remote(src, dst, s4_sem.at[slot, d], r4_sem, {"lon": (u + d) % LON, "lat": lat})

        @pl.loop(1, LON)
        def _(d):
            to(d).start()

        @pl.when(lat == v)
        def _():
            pltpu.make_async_copy(src, dst, r4_sem).start()

        @pl.when(lat != v)
        def _():
            to(0).start()

        def left():
            @pl.loop(1, LON)
            def _(d):
                to(d).wait_send()

            @pl.when(lat != v)
            def _():
                to(0).wait_send()

        return left

    has_two = first_tile(z + 1) - mine == 2
    left0 = deliver(0)

    @pl.when(has_two)
    def _():
        deliver(1)

    drain(final, r4_sem)
    sums[...] = final[...]

    left0()

    @pl.when(has_two)
    def _():
        group = (mine + 1) * 16 + spot
        lat = group // 9
        dst = final.at[group % 9, core]

        def to(d):
            return remote(own.at[1], dst, s4_sem.at[1, d], r4_sem, {"lon": (u + d) % LON, "lat": lat})

        @pl.loop(1, LON)
        def _(d):
            to(d).wait_send()

        @pl.when(lat != v)
        def _():
            to(0).wait_send()

    to_west.wait_send()
    to_east.wait_send()

    @pl.when(v > 0)
    def _():
        for copy in to_north:
            copy.wait_send()

    @pl.when(v < LAT - 1)
    def _():
        for copy in to_south:
            copy.wait_send()

    for g in range(2):
        for a in range(3):
            drain(parts2.at[g, a, pl.ds(0, 15)], s2_sem.at[g, a])
    drain(parts3.at[pl.ds(0, PLANES - 1)], s3_sem)


def local(field, first_weight, second_weight, cotangent, live_rows, polar_links):
    vmem = pl.BlockSpec(memory_space=pltpu.VMEM)
    smem = pl.BlockSpec(memory_space=pltpu.SMEM)
    anywhere = pl.BlockSpec(memory_space=pl.ANY)
    half = C // 2
    tile = jax.ShapeDtypeStruct((T, T, C), BF)
    share = jax.ShapeDtypeStruct((SHARE, C), F32)
    flat = pltpu.VMEM((3, PX, C), BF)
    columns = pltpu.VMEM((8, STRIP, C), F32)
    four = pltpu.VMEM((4, STRIP, C), F32)
    ringed = pltpu.VMEM((RING * T, C), F32)
    weights = pltpu.VMEM((9 * C, C), BF)
    message = pltpu.VMEM((2, MSG, C), BF)
    corners = pltpu.VMEM((4, 16, C), BF)
    grads = pltpu.VMEM((2, 3, 3, C, half), BF)
    dma = pltpu.SemaphoreType.DMA
    made, back, sums = pl.pallas_call(
        kernel,
        out_shape=(pltpu.VMEM((T, T, C), BF), pltpu.VMEM((T, T, C), BF), pltpu.VMEM((9, 2, 2, 16, half), BF)),
        in_specs=[anywhere, anywhere, anywhere, anywhere, smem, smem],
        out_specs=(vmem, vmem, vmem),
        scratch_shapes=[
            *([flat] * 4),
            *([columns] * 2),
            *([four] * 4),
            pltpu.VMEM((T, T, C), BF),
            pltpu.VMEM((T, T, C), BF),
            pltpu.VMEM((2, 4, T, C), F32),
            pltpu.VMEM((4, 16, C), F32),
            *([ringed] * 3),
            pltpu.VMEM((3 * C, PX), BF),
            pltpu.VMEM((38 * T, C), BF),
            *([weights] * 4),
            pltpu.VMEM((4, 48, C), F32),
            message,
            message,
            corners,
            message,
            message,
            corners,
            pltpu.VMEM((4, MSG, C), BF),
            pltpu.VMEM((4, PICK, C), BF),
            pltpu.VMEM((4, PICK, C), BF),
            pltpu.VMEM((2, 3, 3, C, half), F32),
            grads,
            grads,
            grads,
            pltpu.VMEM((2, 3, 16, 3, 16, half), BF),
            pltpu.VMEM((2, 10, 16, half), BF),
            pltpu.VMEM((PLANES, 2, 2, 16, half), BF),
            pltpu.VMEM((2, 2, 16, half), BF),
            pltpu.VMEM((9, 2, 2, 16, half), BF),
            dma((4,)),
            dma((8,)),
            dma((8,)),
            dma,
            dma,
            dma,
            dma,
            dma((2, 3)),
            dma((2, 3)),
            dma((2, 3)),
            dma((2, 3)),
            dma,
            dma,
            dma((2, LON)),
            dma,
        ],
        compiler_params=pltpu.CompilerParams(
            collective_id=0, has_side_effects=True, vmem_limit_bytes=56 * 1024 * 1024
        ),
        cost_estimate=pl.CostEstimate(
            flops=12 * T * T * 9 * C * C, bytes_accessed=6_000_000, transcendentals=2 * T * T * C
        ),
    )(field, first_weight, second_weight, cotangent, live_rows, polar_links)
    return pl.pallas_call(
        finish,
        out_shape=(tile, tile, share, share),
        in_specs=[vmem] * 3,
        out_specs=(anywhere,) * 4,
        scratch_shapes=[pltpu.VMEM((SHARE, C), F32), pltpu.VMEM((SHARE, C), F32), dma((4,))],
        cost_estimate=pl.CostEstimate(flops=2 * SHARE * C, bytes_accessed=3_000_000, transcendentals=0),
    )(made, back, sums)


def solution(mesh):
    in_specs = (P("lat", "lon", None), P(), P(), P("lat", "lon", None), P("lon", "lat"), P())
    out_specs = (P("lat", "lon", None), P("lat", "lon", None), P("lat", None), P("lat", None))
    return jax.shard_map(local, mesh=mesh, in_specs=in_specs, out_specs=out_specs, check_vma=False)
```

```python
import math

import jax
import jax.numpy as jnp
from jax import lax
from jax.experimental import pallas as pl
from jax.experimental.pallas import tpu as pltpu
from jax.sharding import PartitionSpec as P

MESH = pl.DeviceIdType.MESH
BF = jnp.bfloat16
F32 = jnp.float32
C = 256
T = 32
EXT = T + 4
PX = EXT * T
RING = T + 2
MSG = 5 * T
STRIP = 40
LON = 16
LAT = 16
PLANES = 8
SHARE = 3 * T // 2 * 3
PICK = MSG + T


def dot(a, b):
    return jnp.dot(a, b, preferred_element_type=F32)


def gelu_parts(pre):
    cdf = 0.5 * (1.0 + lax.erf(pre * 0.7071067811865476))
    dens = jnp.exp(-0.5 * pre * pre) * 0.3989422804014327
    return (pre * cdf, cdf + pre * dens)


def rows(start, size=T):
    return pl.ds(pl.multiple_of(start * T, T), size)


def finish(made, back, sums, out, fgrad, grad1, grad2, share1, share2, sem):
    copies = [pltpu.make_async_copy(made, out, sem.at[0]), pltpu.make_async_copy(back, fgrad, sem.at[1])]
    for copy in copies:
        copy.start()
    scale = 1.0 / math.sqrt(LON * T * LAT * T)
    for g, (ref, dst) in enumerate(((share2, grad2), (share1, grad1))):
        for k in range(9):
            for h in range(2):
                ref[k * 16 : (k + 1) * 16, h * 128 : (h + 1) * 128] = sums[h, k, g].astype(F32) * scale
        copies.append(pltpu.make_async_copy(ref, dst, sem.at[2 + g]))
        copies[-1].start()
    for copy in copies:
        copy.wait()


def kernel(
    field_hbm,
    w1_hbm,
    w2_hbm,
    cot_hbm,
    live_ref,
    links,
    out,
    fgrad,
    sums,
    sx,
    sd,
    sh,
    sg,
    zx,
    zd,
    zh,
    zg,
    zs,
    zp,
    zq,
    kz,
    field,
    cot,
    cols,
    corner,
    pre1,
    back2,
    slope,
    xt,
    xth,
    dz,
    dzg,
    w1,
    w2,
    wt1,
    wt2,
    ext,
    send_ns,
    send_ew,
    send_dg,
    halo_ns,
    halo_ew,
    halo_dg,
    near,
    picked,
    arrived,
    gkeep,
    gsend,
    gpair,
    gsum,
    px1,
    py1,
    sx1,
    sy1,
    py2,
    px2,
    tiles,
    parts3,
    own,
    final,
    w_sem,
    hs_sem,
    hr_sem,
    pas_sem,
    par_sem,
    pbs_sem,
    pbr_sem,
    s1_sem,
    r1_sem,
    s2_sem,
    r2_sem,
    s3_sem,
    r3_sem,
    s4_sem,
    r4_sem,
    s5_sem,
    r5_sem,
):
    u, v = lax.axis_index("lon"), lax.axis_index("lat")
    core, x, z = lax.rem(u, 2), lax.div(u, 4), lax.div(v, 2)
    low = lax.rem(u, 4)
    y_lo = lax.rem(v, 2)
    y = lax.div(low, 2) * 2 + y_lo
    spot = x * 4 + y
    north, south = v == 0, v == LAT - 1
    rim_tile = north | south
    side = jnp.where(south, 1, 0)
    live = live_ref[0, 0]
    east, west = lax.rem(u + 1, LON), lax.rem(u + LON - 1, LON)

    def in_plane(place):
        px, py = lax.div(place, 4), lax.rem(place, 4)
        return {"lon": px * 4 + lax.div(py, 2) * 2 + core, "lat": z * 2 + lax.rem(py, 2)}

    def along_x(d):
        return in_plane(lax.rem(x + d, 4) * 4 + y)

    def along_y(d):
        return in_plane(x * 4 + lax.rem(y + d, 4))

    def quarter(d):
        return x * 4 + lax.rem(low + d, 4)

    fetched = [
        pltpu.make_async_copy(src, dst, w_sem.at[n])
        for n, (src, dst) in enumerate(((field_hbm, field), (cot_hbm, cot), (w1_hbm, w1), (w2_hbm, w2)))
    ]
    for copy in fetched:
        copy.start()

    barrier = pltpu.get_barrier_semaphore()

    def greet(lon, lat):
        pl.semaphore_signal(barrier, inc=1, device_id={"lon": lon, "lat": lat}, device_id_type=MESH)

    greet(east, v)
    greet(west, v)

    @pl.when(v > 0)
    def _():
        for lon in (west, u, east):
            greet(lon, v - 1)

    @pl.when(v < LAT - 1)
    def _():
        for lon in (west, u, east):
            greet(lon, v + 1)

    @pl.when(rim_tile)
    def _():
        for d in range(1, 4):
            greet(quarter(d), v)
            greet(lax.rem(u + 4 * d, LON), v)

    for d in range(1, 4):
        for to in (along_x(d), along_y(d)):
            greet(to["lon"], to["lat"])

    @pl.loop(1, PLANES)
    def _(d):
        greet(u, lax.rem(z + d, PLANES) * 2 + y_lo)

    lane_row = lax.broadcasted_iota(jnp.int32, (T, C), 0)
    fetched[0].wait()
    fetched[1].wait()

    @pl.loop(0, T)
    def _(i):
        kept = jnp.full((T, C), i, jnp.int32) < live
        for k, (src, dst) in enumerate(((field, sx), (cot, sd))):
            line = jnp.where(kept, src[i].astype(F32), 0.0)
            dst[1, rows(i + 2), :] = line.astype(BF)
            for n, col in enumerate((0, 1, T - 2, T - 1)):
                cols[k, n, pl.ds(i, 1), :] = line[col : col + 1]

    keep_col = jnp.where(lane_row < live, 1.0, 0.0)
    keep_last = jnp.where(jnp.full((T, C), T - 1, jnp.int32) < live, 1.0, 0.0)
    for s in range(2):
        for k, src in enumerate((sx, sd)):
            first = 2 if s == 0 else T
            send_ns[s, 2 * k * T : (2 * k + 2) * T, :] = src[1, first * T : (first + 2) * T, :]
            for n in range(2):
                send_ew[s, (2 * k + n) * T : (2 * k + n + 1) * T, :] = cols[k, 2 * s + n].astype(BF)
        send_ns[s, 4 * T :, :] = jnp.ones((T, C), BF) if s == 0 else keep_last.astype(BF)
        send_ew[s, 4 * T :, :] = keep_col.astype(BF)
    corner[...] = jnp.zeros_like(corner)
    for s in range(2):
        for t in range(2):
            for k in range(2):
                for r in range(2):
                    for n in range(2):
                        at = 4 * k + 2 * r + n
                        line = (0 if s == 0 else T - 2) + r
                        corner[2 * s + t, at : at + 1, :] = cols[k, 2 * t + n, line : line + 1, :]
            corner[2 * s + t, 8:9, :] = jnp.ones((1, C), F32) if s == 0 else keep_last[0:1]
    send_dg[...] = corner[...].astype(BF)

    here = jnp.where(v > 0, 3, 0) + jnp.where(v < LAT - 1, 3, 0) + jnp.where(rim_tile, 6, 0)
    pl.semaphore_wait(barrier, here + 2 + 6 + 7)

    def remote(src, dst, send, recv, to):
        return pltpu.make_async_remote_copy(
            src_ref=src, dst_ref=dst, send_sem=send, recv_sem=recv, device_id=to, device_id_type=MESH
        )

    def drain(ref, sem):
        pltpu.make_async_copy(ref, ref, sem).wait()

    def edge(src, dst, n, lon, lat):
        return remote(src, dst, hs_sem.at[n], hr_sem.at[n], {"lon": lon, "lat": lat})

    @pl.when(rim_tile)
    def _():
        for d in range(1, 4):
            remote(send_ns.at[side], near.at[low], pas_sem, par_sem, {"lon": quarter(d), "lat": v}).start()

    to_west = edge(send_ew.at[0], halo_ew.at[1], 0, west, v)
    to_east = edge(send_ew.at[1], halo_ew.at[0], 1, east, v)
    to_north = [
        edge(send_ns.at[0], halo_ns.at[1], 2, u, v - 1),
        edge(send_dg.at[0], halo_dg.at[3], 3, west, v - 1),
        edge(send_dg.at[1], halo_dg.at[2], 4, east, v - 1),
    ]
    to_south = [
        edge(send_ns.at[1], halo_ns.at[0], 5, u, v + 1),
        edge(send_dg.at[2], halo_dg.at[1], 6, west, v + 1),
        edge(send_dg.at[3], halo_dg.at[0], 7, east, v + 1),
    ]

    to_west.start()
    to_east.start()

    @pl.when(v > 0)
    def _():
        for copy in to_north:
            copy.start()

    @pl.when(v < LAT - 1)
    def _():
        for copy in to_south:
            copy.start()

    @pl.loop(2, 34)
    def _(e):
        at = rows(e)
        for s in (sx, sd):
            line = s[1, at, :].astype(F32)
            s[0, at, :] = jnp.where(lane_row == 0, 0.0, pltpu.roll(line, 1, 0)).astype(BF)
            s[2, at, :] = jnp.where(lane_row == T - 1, 0.0, pltpu.roll(line, T - 1, 0)).astype(BF)

    for ref in (zx, zd, zh, zg, zs, zp, zq, ext, kz):
        ref[...] = jnp.zeros_like(ref)
    for b in range(3):
        sh[b, 0:T, :] = jnp.zeros((T, C), BF)
        sh[b, PX - T : PX, :] = jnp.zeros((T, C), BF)
    for ref in (dz, dzg):
        ref[0 : 3 * T, :] = jnp.zeros((3 * T, C), BF)
        ref[35 * T : 38 * T, :] = jnp.zeros((3 * T, C), BF)
    dz[3 * T : 35 * T, :] = sd[1, 2 * T : 34 * T, :]
    tiles[:, 9] = jnp.zeros((2, 16, C // 2), BF)

    def window(s, back, first, size):
        pieces = []
        for a in range(3):
            for b in range(3):
                start = (first + (2 - a if back else a)) * T
                pieces.append(s[2 - b if back else b, start : start + size * T, :])
        return jnp.concatenate(pieces, axis=1)

    def spread(s, left, right, e, line):
        at = rows(e)
        s[1, at, :] = line.astype(BF)
        s[0, at, :] = jnp.where(lane_row == 0, left, pltpu.roll(line, 1, 0)).astype(BF)
        s[2, at, :] = jnp.where(lane_row == T - 1, right, pltpu.roll(line, T - 1, 0)).astype(BF)

    fetched[2].wait()
    pre1[2 * T : 32 * T, :] = dot(window(sx, False, 2, 30), w1[...])

    @pl.loop(3, 33)
    def _(e):
        act, slp = gelu_parts(pre1[rows(e - 1), :])
        mask = jnp.where(jnp.full((T, C), e - 2, jnp.int32) < live, 1.0, 0.0)
        slope[rows(e - 1), :] = slp * mask
        spread(sh, 0.0, 0.0, e, act * mask)

    fetched[3].wait()

    @pl.loop(0, 9)
    def _(tap):
        at = pl.ds(pl.multiple_of(tap * C, C), C)
        wt2[at, :] = w2[at, :].T

    back2[2 * T : 32 * T, :] = dot(window(sd, True, 2, 30), wt2[...])

    @pl.when(rim_tile)
    def _():
        drain(near.at[pl.ds(0, 3)], par_sem)
        drain(near.at[pl.ds(0, 3)], pas_sem)
        near[low] = send_ns[side]
        pivot = links[side, 0]
        n = lax.broadcasted_iota(jnp.int32, (8 * T, 4 * T), 0)
        at = lax.broadcasted_iota(jnp.int32, (8 * T, 4 * T), 1) + x * (4 * T)
        to = (n // (2 * T)) * 4 + low
        n = n & (2 * T - 1)
        q = n & 15
        in_east = n >= T + 16
        ring_col = jnp.where(in_east, T, -1)
        outer_col = jnp.where(in_east, T, -2) + (q & 1)
        col = jnp.where(n < T, n, jnp.where(q == 8, ring_col, outer_col))
        hit = ((pivot - to * T - col) & (LON * T - 1)) == at
        line = jnp.where(q == 8, 4, jnp.where(q < 8, q // 2, 5))
        corners = jnp.zeros((4, T, C), F32)
        for part in range(5):
            target = part if part == 4 else part ^ 1
            pick = jnp.where(hit & ((n < T) | (line == target)), 1.0, 0.0).astype(BF)
            lines = near[:, part * T : (part + 1) * T, :].reshape(4 * T, C)
            found = dot(pick, lines).reshape(4, 2 * T, C)
            picked[:, target * T : (target + 1) * T, :] = found[:, :T].astype(BF)
            corners = corners + found[:, T:]
        picked[:, MSG:, :] = corners.astype(BF)
        for d in range(1, 4):
            to = lax.rem(x + d, 4)
            remote(picked.at[to], arrived.at[x], pbs_sem, pbr_sem, {"lon": lax.rem(u + 4 * d, LON), "lat": v}).start()

    @pl.loop(3, 33)
    def _(e):
        spread(sg, 0.0, 0.0, e, back2[rows(e - 1), :] * slope[rows(e - 1), :])

    @pl.loop(0, 9)
    def _(tap):
        at = pl.ds(pl.multiple_of(tap * C, C), C)
        wt1[at, :] = w1[at, :].T

    to_west.wait_recv()
    to_east.wait_recv()

    @pl.when(v > 0)
    def _():
        for copy in to_south:
            copy.wait_recv()

    @pl.when(v < LAT - 1)
    def _():
        for copy in to_north:
            copy.wait_recv()

    head = lax.broadcasted_iota(jnp.int32, (16, C), 0)

    def place(h):
        for k, (s, zz) in enumerate(((sx, zx), (sd, zd))):
            for t in range(2):
                px = halo_dg[2 * h + t].astype(F32)
                for r in range(2):
                    for n in range(2):
                        at = 4 * k + 2 * r + n
                        zz[t * 6 + n, pl.ds(34 * h + r, 1), :] = px[at : at + 1]
            for r in range(2):
                e = 34 * h + r
                line = halo_ns[h, (2 * k + r) * T : (2 * k + r + 1) * T, :].astype(F32)
                spread(s, zz[1, pl.ds(e, 1), :], zz[6, pl.ds(e, 1), :], e, line)
                for n, col in enumerate((0, 1, T - 2, T - 1)):
                    zz[2 + n, pl.ds(e, 1), :] = line[col : col + 1]
        mask = halo_ns[h, 4 * T :, :].astype(F32)
        e = 33 * h + 1
        for t in range(2):
            kz[3 * t, pl.ds(e, 1), :] = halo_dg[2 * h + t].astype(F32)[8:9]
            kz[1 + t, pl.ds(e, 1), :] = mask[t * (T - 1) : t * (T - 1) + 1]

    for k, zz in enumerate((zx, zd)):
        for n in range(2):
            zz[n, 2 : 2 + T, :] = halo_ew[0, (2 * k + n) * T : (2 * k + n + 1) * T, :].astype(F32)
            zz[6 + n, 2 : 2 + T, :] = halo_ew[1, (2 * k + n) * T : (2 * k + n + 1) * T, :].astype(F32)
            zz[2 + n, 2 : 2 + T, :] = cols[k, n]
            zz[4 + n, 2 : 2 + T, :] = cols[k, 2 + n]
    for t in range(2):
        kz[3 * t, 2 : 2 + T, :] = halo_ew[t, 4 * T :, :].astype(F32)
        kz[1 + t, 2 : 2 + T, :] = keep_col
    place(0)
    place(1)

    def insert(s, zz, e):
        at = pl.ds(pl.multiple_of(e * T, T), 16)
        s[0, at, :] = jnp.where(head == 0, zz[1, pl.ds(e, 1), :], s[0, at, :].astype(F32)).astype(BF)
        at = pl.ds(pl.multiple_of(e * T + 16, 16), 16)
        s[2, at, :] = jnp.where(head == 15, zz[6, pl.ds(e, 1), :], s[2, at, :].astype(F32)).astype(BF)

    for e in (2, 3, 32, 33):
        insert(sd, zd, e)

    @pl.loop(2, 34)
    def _(e):
        insert(sx, zx, e)

    def transpose(s, ref, k):
        at = pl.ds(pl.multiple_of(k * 128, 128), 128)
        for b in range(3):
            ref[b * C : (b + 1) * C, at] = s[b, at, :].T

    def transposed(s, ref):
        @pl.loop(0, PX // 128)
        def _(k):
            transpose(s, ref, k)

    e_out, e_ring = jnp.where(south, 35, 0), jnp.where(south, 34, 1)
    e_edge, e_in = jnp.where(south, 33, 2), jnp.where(south, 32, 3)
    far = jnp.where(south, 2, 0)

    def extend(n, s, left, right, e):
        ext[n, 2 : 2 + T, :] = s[1, rows(e), :].astype(F32)
        for k, ref in enumerate(left):
            at = 2 - len(left) + k
            ext[n, at : at + 1, :] = ref[pl.ds(e, 1), :]
        for k, ref in enumerate(right):
            ext[n, 34 + k : 35 + k, :] = ref[pl.ds(e, 1), :]

    def straight(n):
        return jnp.concatenate([ext[n, 2 - b : 42 - b, :] for b in range(3)], axis=1).astype(BF)

    def turned(n):
        return jnp.concatenate([ext[n, b : b + 40, :] for b in range(3)], axis=1).astype(BF)

    def taps(w, row):
        return w[pl.ds(pl.multiple_of(row * 3 * C, 3 * C), 3 * C), :]

    def combine(up, mid, down, back):
        if back:
            up, down = down, up
        return pltpu.roll(up, 1, 0) + mid + pltpu.roll(down, mid.shape[0] - 1, 0)

    def strips(zz, w, back, ref):
        order = (2, 1, 0) if back else (0, 1, 2)
        lines = jnp.concatenate(
            [jnp.concatenate([zz[first + b] for b in order], axis=1) for first in (0, 1, 4, 5)], axis=0
        ).astype(BF)
        res = combine(*(dot(lines, w[a * 3 * C : (a + 1) * 3 * C, :]) for a in range(3)), back)
        for t in range(4):
            ref[t] = res[t * STRIP : (t + 1) * STRIP]

    def put_columns(s, zz):
        @pl.loop(3, 33)
        def _(e):
            c = [zz[t, pl.ds(e, 1), :] for t in range(4)]
            at = pl.ds(pl.multiple_of(e * T, T), 16)
            s[1, at, :] = jnp.where(head == 0, c[1], s[1, at, :].astype(F32)).astype(BF)
            line = jnp.where(head == 1, c[1], s[0, at, :].astype(F32))
            s[0, at, :] = jnp.where(head == 0, c[0], line).astype(BF)
            at = pl.ds(pl.multiple_of(e * T + 16, 16), 16)
            s[1, at, :] = jnp.where(head == 15, c[2], s[1, at, :].astype(F32)).astype(BF)
            line = jnp.where(head == 14, c[2], s[2, at, :].astype(F32))
            s[2, at, :] = jnp.where(head == 15, c[3], line).astype(BF)

    def of_row(res, t):
        at = (0, 1, T, T + 1)[t]
        return res[at : at + 1]

    def outer(s, back):
        return jnp.concatenate([window(s, back, 0, 2), window(s, back, 32, 2)], axis=0)

    res = dot(outer(sx, False), w1[...])
    pre1[0 : 2 * T, :] = res[: 2 * T]
    pre1[32 * T : 34 * T, :] = res[2 * T :]
    strips(zx, w1, False, zp)

    def activate_strips():
        for t in range(4):
            act, slp = gelu_parts(zp[t])
            zh[t] = act * kz[t]
            zs[t] = slp * kz[t]

    def activate(e, mask):
        act, slp = gelu_parts(pre1[rows(e - 1), :])
        slope[rows(e - 1), :] = slp * mask
        spread(sh, zh[0, pl.ds(e, 1), :], zh[3, pl.ds(e, 1), :], e, act * mask)

    activate_strips()
    activate(1, halo_ns[0, 4 * T :, :].astype(F32))
    activate(2, jnp.where(jnp.zeros((T, C), jnp.int32) < live, 1.0, 0.0))
    activate(33, keep_last)
    activate(34, halo_ns[1, 4 * T :, :].astype(F32))
    put_columns(sh, zh)
    transposed(sh, xth)

    res = dot(outer(sd, True), wt2[...])
    back2[0 : 2 * T, :] = res[: 2 * T]
    back2[32 * T : 34 * T, :] = res[2 * T :]
    strips(zd, wt2, True, zq)

    def scale_strips():
        for t in range(4):
            zg[t] = zq[t] * zs[t]

    def scale(e):
        line = back2[rows(e - 1), :] * slope[rows(e - 1), :]
        spread(sg, zg[0, pl.ds(e, 1), :], zg[3, pl.ds(e, 1), :], e, line)

    scale_strips()
    for e in (1, 2, 33, 34):
        scale(e)
    put_columns(sg, zg)
    dzg[3 * T : 35 * T, :] = sg[1, 2 * T : 34 * T, :]
    transposed(sx, xt)

    @pl.when(rim_tile)
    def _():
        drain(arrived.at[pl.ds(0, 3)], pbr_sem)
        drain(arrived.at[pl.ds(0, 3)], pbs_sem)
        arrived[x] = picked[x]
        total = arrived[0].astype(F32)
        for k in range(1, 4):
            total = total + arrived[k].astype(F32)
        halo_ns[side] = total[:MSG].astype(BF)
        halo_dg[2 * side] = total[MSG : MSG + 16].astype(BF)
        halo_dg[2 * side + 1] = total[MSG + 16 :].astype(BF)
        place(side)
        for n, e in enumerate((e_out, e_ring, e_edge, e_in)):
            extend(n, sx, (zx.at[0], zx.at[1]), (zx.at[6], zx.at[7]), e)
        pre = jnp.zeros((2 * STRIP, C), F32)
        for pair_of, row in (((straight(2), turned(1)), far), ((straight(1), turned(2)), 1), ((straight(0), turned(3)), 2 - far)):
            pre = pre + dot(jnp.concatenate(pair_of, axis=0), taps(w1, row))
        for k, e in enumerate((e_ring, e_edge)):
            pre1[rows(e - 1), :] = pre[k * STRIP + 1 : k * STRIP + 1 + T]
            for t in range(4):
                zp[t, pl.ds(e, 1), :] = of_row(pre[k * STRIP : (k + 1) * STRIP], t)
        activate_strips()
        activate(e_ring, halo_ns[side, 4 * T :, :].astype(F32))
        activate(e_edge, jnp.where(jnp.full((T, C), e_edge - 2, jnp.int32) < live, 1.0, 0.0))

        for n, e in enumerate((e_out, e_ring, e_edge, e_in)):
            extend(n, sd, (zd.at[0], zd.at[1]), (zd.at[6], zd.at[7]), e)
        back = dot(jnp.concatenate([turned(0), turned(1)], axis=0), taps(wt2, far))
        back = back + dot(jnp.concatenate([straight(2), straight(3)], axis=0), taps(wt2, far))
        back = back + dot(jnp.concatenate([turned(1), straight(2)], axis=0), taps(wt2, 1))
        for k, e in enumerate((e_ring, e_edge)):
            back2[rows(e - 1), :] = back[k * STRIP + 1 : k * STRIP + 1 + T]
            for t in range(4):
                zq[t, pl.ds(e, 1), :] = of_row(back[k * STRIP : (k + 1) * STRIP], t)
        scale_strips()
        scale(e_ring)
        scale(e_edge)
        dzg[rows(e_edge + 1), :] = sg[1, rows(e_edge), :]
        transpose(sx, xt, 8 * side)
        transpose(sh, xth, 8 * side)

    sibling = {"lon": u + 1 - 2 * core, "lat": v}

    def pair(g, a):
        return remote(gsend.at[g, a], gpair.at[g, a], s1_sem.at[g, a], r1_sem.at[g, a], sibling)

    def add_pair(g, a):
        pair(g, a).wait()
        total = gkeep[g, a] + gpair[g, a].astype(F32)
        gsum[g, 3 * a : 3 * a + 3] = total.astype(BF).reshape(3, 4, 4, 16, C // 2)

    def first_axis(g):
        for d in range(1, 4):
            to = lax.rem(x + d, 4)
            remote(gsum.at[g, pl.ds(0, 5), to], px1.at[g, x], s2_sem.at[g, 0], r2_sem.at[g, 0], along_x(d)).start()
            to = lax.rem(y + d, 4)
            remote(gsum.at[g, pl.ds(5, 4), :, to], py1.at[g, y], s2_sem.at[g, 1], r2_sem.at[g, 1], along_y(d)).start()

    def total_of(ref, g):
        total = ref[g, 0].astype(F32)
        for k in range(1, 4):
            total = total + ref[g, k].astype(F32)
        return total.astype(BF)

    def second_axis(g):
        drain(px1.at[g, pl.ds(0, 3)], r2_sem.at[g, 0])
        px1[g, x] = gsum[g, 0:5, x]
        sx1[g] = total_of(px1, g)
        for d in range(1, 4):
            to = lax.rem(y + d, 4)
            remote(sx1.at[g, :, to], py2.at[g, y], s2_sem.at[g, 2], r2_sem.at[g, 2], along_y(d)).start()
        drain(py1.at[g, pl.ds(0, 3)], r2_sem.at[g, 1])
        py1[g, y] = gsum[g, 5:9, :, y]
        sy1[g] = total_of(py1, g)
        for d in range(1, 4):
            to = lax.rem(x + d, 4)
            remote(sy1.at[g, :, to], px2.at[g, x], s2_sem.at[g, 3], r2_sem.at[g, 3], along_x(d)).start()

    def plane_total(g):
        drain(py2.at[g, pl.ds(0, 3)], r2_sem.at[g, 2])
        py2[g, y] = sx1[g, :, y]
        tiles[g, 0:5] = total_of(py2, g)
        drain(px2.at[g, pl.ds(0, 3)], r2_sem.at[g, 3])
        px2[g, x] = sy1[g, :, x]
        tiles[g, 5:9] = total_of(px2, g)

    def weight_grad(g, left, right, between=None):
        for a in range(3):
            res = dot(left[...], right[(2 - a) * T : (2 - a) * T + PX, :])
            lo, hi = res[:, : C // 2], res[:, C // 2 :]
            gkeep[g, a] = jnp.where(core == 0, lo, hi).reshape(3, C, C // 2)
            gsend[g, a] = jnp.where(core == 0, hi, lo).astype(BF).reshape(3, C, C // 2)
            pair(g, a).start()
            if a:
                add_pair(g, a - 1)
            elif between is not None:
                between()

    def first_done():
        add_pair(0, 2)
        first_axis(0)

    weight_grad(0, xth, dz)
    weight_grad(1, xt, dzg, first_done)

    size = T // 2

    def forward(first):
        row = lax.broadcasted_iota(jnp.int32, (size * T, C), 0) // T + first
        pre = dot(window(sh, False, 1 + first, size), w2[...])
        masked = sx[1, (2 + first) * T : (2 + first + size) * T, :].astype(F32)
        out[first : first + size] = (masked + jnp.where(row < live, pre, 0.0)).astype(BF).reshape(size, T, C)

    forward(0)
    add_pair(1, 2)
    first_axis(1)
    forward(size)
    second_axis(0)

    row = lax.broadcasted_iota(jnp.int32, (T * T, C), 0) // T
    back = dot(window(sg, True, 1, T), wt1[...])
    total = cot[...].reshape(T * T, C).astype(F32) + back
    fgrad[...] = jnp.where(row < live, total, 0.0).astype(BF).reshape(T, T, C)

    @pl.when(rim_tile)
    def _():
        for n, e in ((1, e_ring), (2, e_edge), (3, e_in)):
            extend(n, sg, (zg.at[0],), (zg.at[3],), e)
        w_far, w_mid = taps(wt1, far), taps(wt1, 1)
        rim = dot(turned(1), w_far) + dot(straight(3), w_far) + dot(straight(2), w_mid)
        i = e_edge - 2
        total = cot[i].astype(F32) + rim[1 : 1 + T]
        kept = jnp.full((T, C), i, jnp.int32) < live
        fgrad[i] = jnp.where(kept, total, 0.0).astype(BF)

    second_axis(1)
    plane_total(0)
    plane_total(1)

    def first_tile(plane):
        return lax.div(18 * plane + 15 - spot, 16)

    for d in range(1, PLANES):
        to = lax.rem(z + d, PLANES)
        remote(
            tiles.at[:, pl.ds(first_tile(to), 2)],
            parts3.at[z],
            s3_sem,
            r3_sem,
            {"lon": u, "lat": to * 2 + y_lo},
        ).start()

    mine = first_tile(z)
    drain(parts3.at[pl.ds(0, PLANES - 1)], r3_sem)
    parts3[z] = tiles[:, pl.ds(mine, 2)]
    total = parts3[0].astype(F32)
    for k in range(1, PLANES):
        total = total + parts3[k].astype(F32)
    for slot in range(2):
        own[slot] = total[:, slot].astype(BF)

    def deliver(slot):
        group = (mine + slot) * 16 + spot
        lat, at = lax.div(group, 9), lax.rem(group, 9)
        src, dst = own.at[slot], final.at[core, at]

        def to(d):
            lon = 2 * lax.rem(lax.div(u, 2) + d, 8) + core
            return remote(src, dst, s4_sem.at[2 * slot + (d == 0)], r4_sem, {"lon": lon, "lat": lat})

        for d in range(1, 8):
            to(d).start()

        @pl.when(lat == v)
        def _():
            pltpu.make_async_copy(src, dst, r4_sem).start()

        @pl.when(lat != v)
        def _():
            to(0).start()

    def delivered(slot):
        lat = lax.div((mine + slot) * 16 + spot, 9)
        drain(final.at[0, pl.ds(0, 7)], s4_sem.at[2 * slot])

        @pl.when(lat != v)
        def _():
            drain(final.at[0, 0], s4_sem.at[2 * slot + 1])

    has_two = first_tile(z + 1) - mine == 2
    deliver(0)

    @pl.when(has_two)
    def _():
        deliver(1)

    drain(final.at[core], r4_sem)
    last = remote(final.at[core], final.at[core], s5_sem, r5_sem, sibling)
    last.start()
    for h in range(2):
        @pl.when(core == h)
        def _(h=h):
            sums[h] = final[h]
    delivered(0)

    @pl.when(has_two)
    def _():
        delivered(1)

    last.wait()
    for h in range(2):
        @pl.when(core != h)
        def _(h=h):
            sums[h] = final[h]

    to_west.wait_send()
    to_east.wait_send()

    @pl.when(v > 0)
    def _():
        for copy in to_north:
            copy.wait_send()

    @pl.when(v < LAT - 1)
    def _():
        for copy in to_south:
            copy.wait_send()

    for g in range(2):
        for k, ref in enumerate((px1, py1, py2, px2)):
            drain(ref.at[g, pl.ds(0, 3)], s2_sem.at[g, k])
    drain(parts3.at[pl.ds(0, PLANES - 1)], s3_sem)


def local(field, first_weight, second_weight, cotangent, live_rows, polar_links):
    vmem = pl.BlockSpec(memory_space=pltpu.VMEM)
    smem = pl.BlockSpec(memory_space=pltpu.SMEM)
    anywhere = pl.BlockSpec(memory_space=pl.ANY)
    half = C // 2
    tile = jax.ShapeDtypeStruct((T, T, C), BF)
    share = jax.ShapeDtypeStruct((SHARE, C), F32)
    flat = pltpu.VMEM((3, PX, C), BF)
    columns = pltpu.VMEM((8, STRIP, C), F32)
    four = pltpu.VMEM((4, STRIP, C), F32)
    ringed = pltpu.VMEM((RING * T, C), F32)
    weights = pltpu.VMEM((9 * C, C), BF)
    message = pltpu.VMEM((2, MSG, C), BF)
    corners = pltpu.VMEM((4, 16, C), BF)
    grads = pltpu.VMEM((2, 3, 3, C, half), BF)
    dma = pltpu.SemaphoreType.DMA
    made, back, sums = pl.pallas_call(
        kernel,
        out_shape=(pltpu.VMEM((T, T, C), BF), pltpu.VMEM((T, T, C), BF), pltpu.VMEM((2, 9, 2, 16, half), BF)),
        in_specs=[anywhere, anywhere, anywhere, anywhere, smem, smem],
        out_specs=(vmem, vmem, vmem),
        scratch_shapes=[
            *([flat] * 4),
            *([columns] * 2),
            *([four] * 6),
            pltpu.VMEM((T, T, C), BF),
            pltpu.VMEM((T, T, C), BF),
            pltpu.VMEM((2, 4, T, C), F32),
            pltpu.VMEM((4, 16, C), F32),
            *([ringed] * 3),
            *([pltpu.VMEM((3 * C, PX), BF)] * 2),
            *([pltpu.VMEM((38 * T, C), BF)] * 2),
            *([weights] * 4),
            pltpu.VMEM((4, 48, C), F32),
            message,
            message,
            corners,
            message,
            message,
            corners,
            pltpu.VMEM((4, MSG, C), BF),
            pltpu.VMEM((4, PICK, C), BF),
            pltpu.VMEM((4, PICK, C), BF),
            pltpu.VMEM((2, 3, 3, C, half), F32),
            grads,
            grads,
            pltpu.VMEM((2, 9, 4, 4, 16, half), BF),
            pltpu.VMEM((2, 4, 5, 4, 16, half), BF),
            pltpu.VMEM((2, 4, 4, 4, 16, half), BF),
            pltpu.VMEM((2, 5, 4, 16, half), BF),
            pltpu.VMEM((2, 4, 4, 16, half), BF),
            pltpu.VMEM((2, 4, 5, 16, half), BF),
            pltpu.VMEM((2, 4, 4, 16, half), BF),
            pltpu.VMEM((2, 10, 16, half), BF),
            pltpu.VMEM((PLANES, 2, 2, 16, half), BF),
            pltpu.VMEM((2, 2, 16, half), BF),
            pltpu.VMEM((2, 9, 2, 16, half), BF),
            dma((4,)),
            dma((8,)),
            dma((8,)),
            dma,
            dma,
            dma,
            dma,
            dma((2, 3)),
            dma((2, 3)),
            dma((2, 4)),
            dma((2, 4)),
            dma,
            dma,
            dma((4,)),
            dma,
            dma,
            dma,
        ],
        compiler_params=pltpu.CompilerParams(
            collective_id=0, has_side_effects=True, vmem_limit_bytes=56 * 1024 * 1024
        ),
        cost_estimate=pl.CostEstimate(
            flops=12 * T * T * 9 * C * C, bytes_accessed=6_000_000, transcendentals=2 * T * T * C
        ),
    )(field, first_weight, second_weight, cotangent, live_rows, polar_links)
    made, back, sums = (pltpu.with_memory_space_constraint(r, pltpu.VMEM) for r in (made, back, sums))
    return pl.pallas_call(
        finish,
        out_shape=(tile, tile, share, share),
        in_specs=[vmem] * 3,
        out_specs=(anywhere,) * 4,
        scratch_shapes=[pltpu.VMEM((SHARE, C), F32), pltpu.VMEM((SHARE, C), F32), dma((4,))],
        compiler_params=pltpu.CompilerParams(vmem_limit_bytes=4 * 1024 * 1024),
        cost_estimate=pl.CostEstimate(flops=2 * SHARE * C, bytes_accessed=3_000_000, transcendentals=0),
    )(made, back, sums)


def solution(mesh):
    in_specs = (P("lat", "lon", None), P(), P(), P("lat", "lon", None), P("lon", "lat"), P())
    out_specs = (P("lat", "lon", None), P("lat", "lon", None), P("lat", None), P("lat", None))
    return jax.shard_map(local, mesh=mesh, in_specs=in_specs, out_specs=out_specs, check_vma=False)
```

```python
import math

import jax
import jax.numpy as jnp
from jax import lax
from jax.experimental import pallas as pl
from jax.experimental.pallas import tpu as pltpu
from jax.sharding import PartitionSpec as P

MESH = pl.DeviceIdType.MESH
BF = jnp.bfloat16
F32 = jnp.float32
C = 256
T = 32
EXT = T + 4
PX = EXT * T
RING = T + 2
MSG = 5 * T
STRIP = 40
LON = 16
LAT = 16
PLANES = 8
SHARE = 3 * T // 2 * 3
PICK = MSG + T


def dot(a, b):
    return jnp.dot(a, b, preferred_element_type=F32)


def gelu_parts(pre):
    cdf = 0.5 * (1.0 + lax.erf(pre * 0.7071067811865476))
    dens = jnp.exp(-0.5 * pre * pre) * 0.3989422804014327
    return (pre * cdf, cdf + pre * dens)


def rows(start, size=T):
    return pl.ds(pl.multiple_of(start * T, T), size)


def finish(made, back, sums, out, fgrad, grad1, grad2, share1, share2, sem):
    copies = [pltpu.make_async_copy(made, out, sem.at[0]), pltpu.make_async_copy(back, fgrad, sem.at[1])]
    for copy in copies:
        copy.start()
    scale = 1.0 / math.sqrt(LON * T * LAT * T)
    for g, (ref, dst) in enumerate(((share2, grad2), (share1, grad1))):
        for k in range(9):
            for h in range(2):
                ref[k * 16 : (k + 1) * 16, h * 128 : (h + 1) * 128] = sums[h, k, g].astype(F32) * scale
        copies.append(pltpu.make_async_copy(ref, dst, sem.at[2 + g]))
        copies[-1].start()
    for copy in copies:
        copy.wait()


def kernel(
    field_hbm,
    w1_hbm,
    w2_hbm,
    cot_hbm,
    live_ref,
    links,
    out,
    fgrad,
    sums,
    sx,
    sd,
    sh,
    sg,
    zx,
    zd,
    zh,
    zg,
    zs,
    zp,
    zq,
    kz,
    field,
    cot,
    cols,
    corner,
    pre1,
    back2,
    slope,
    xt,
    xth,
    dz,
    dzg,
    w1,
    w2,
    wt1,
    wt2,
    ext,
    send_ns,
    send_ew,
    send_dg,
    halo_ns,
    halo_ew,
    halo_dg,
    near,
    picked,
    arrived,
    gkeep,
    gsend,
    gpair,
    gsum,
    px1,
    py1,
    sx1,
    sy1,
    py2,
    px2,
    tiles,
    parts3,
    own,
    final,
    w_sem,
    hs_sem,
    hr_sem,
    pas_sem,
    par_sem,
    pbs_sem,
    pbr_sem,
    s1_sem,
    r1_sem,
    s2_sem,
    r2_sem,
    s3_sem,
    r3_sem,
    s4_sem,
    r4_sem,
    s5_sem,
    r5_sem,
):
    u, v = lax.axis_index("lon"), lax.axis_index("lat")
    core, x, z = lax.rem(u, 2), lax.div(u, 4), lax.div(v, 2)
    low = lax.rem(u, 4)
    y_lo = lax.rem(v, 2)
    y = lax.div(low, 2) * 2 + y_lo
    spot = x * 4 + y
    north, south = v == 0, v == LAT - 1
    rim_tile = north | south
    side = jnp.where(south, 1, 0)
    live = live_ref[0, 0]
    east, west = lax.rem(u + 1, LON), lax.rem(u + LON - 1, LON)

    def in_plane(place):
        px, py = lax.div(place, 4), lax.rem(place, 4)
        return {"lon": px * 4 + lax.div(py, 2) * 2 + core, "lat": z * 2 + lax.rem(py, 2)}

    def along_x(d):
        return in_plane(lax.rem(x + d, 4) * 4 + y)

    def along_y(d):
        return in_plane(x * 4 + lax.rem(y + d, 4))

    def quarter(d):
        return x * 4 + lax.rem(low + d, 4)

    fetched = [
        pltpu.make_async_copy(src, dst, w_sem.at[n])
        for n, (src, dst) in enumerate(((field_hbm, field), (cot_hbm, cot), (w1_hbm, w1), (w2_hbm, w2)))
    ]
    for copy in fetched:
        copy.start()

    barrier = pltpu.get_barrier_semaphore()

    def greet(lon, lat):
        pl.semaphore_signal(barrier, inc=1, device_id={"lon": lon, "lat": lat}, device_id_type=MESH)

    greet(east, v)
    greet(west, v)

    @pl.when(v > 0)
    def _():
        for lon in (west, u, east):
            greet(lon, v - 1)

    @pl.when(v < LAT - 1)
    def _():
        for lon in (west, u, east):
            greet(lon, v + 1)

    @pl.when(rim_tile)
    def _():
        for d in range(1, 4):
            greet(quarter(d), v)
            greet(lax.rem(u + 4 * d, LON), v)

    for d in range(1, 4):
        for to in (along_x(d), along_y(d)):
            greet(to["lon"], to["lat"])

    @pl.loop(1, PLANES)
    def _(d):
        greet(u, lax.rem(z + d, PLANES) * 2 + y_lo)

    lane_row = lax.broadcasted_iota(jnp.int32, (T, C), 0)
    fetched[0].wait()
    fetched[1].wait()

    @pl.loop(0, T, unroll=4)
    def _(i):
        kept = jnp.full((T, C), i, jnp.int32) < live
        for k, (src, dst) in enumerate(((field, sx), (cot, sd))):
            line = jnp.where(kept, src[i].astype(F32), 0.0)
            dst[1, rows(i + 2), :] = line.astype(BF)
            for n, col in enumerate((0, 1, T - 2, T - 1)):
                cols[k, n, pl.ds(i, 1), :] = line[col : col + 1]

    keep_col = jnp.where(lane_row < live, 1.0, 0.0)
    keep_last = jnp.where(jnp.full((T, C), T - 1, jnp.int32) < live, 1.0, 0.0)
    for s in range(2):
        for k, src in enumerate((sx, sd)):
            first = 2 if s == 0 else T
            send_ns[s, 2 * k * T : (2 * k + 2) * T, :] = src[1, first * T : (first + 2) * T, :]
            for n in range(2):
                send_ew[s, (2 * k + n) * T : (2 * k + n + 1) * T, :] = cols[k, 2 * s + n].astype(BF)
        send_ns[s, 4 * T :, :] = jnp.ones((T, C), BF) if s == 0 else keep_last.astype(BF)
        send_ew[s, 4 * T :, :] = keep_col.astype(BF)
    corner[...] = jnp.zeros_like(corner)
    for s in range(2):
        for t in range(2):
            for k in range(2):
                for r in range(2):
                    for n in range(2):
                        at = 4 * k + 2 * r + n
                        line = (0 if s == 0 else T - 2) + r
                        corner[2 * s + t, at : at + 1, :] = cols[k, 2 * t + n, line : line + 1, :]
            corner[2 * s + t, 8:9, :] = jnp.ones((1, C), F32) if s == 0 else keep_last[0:1]
    send_dg[...] = corner[...].astype(BF)

    here = jnp.where(v > 0, 3, 0) + jnp.where(v < LAT - 1, 3, 0) + jnp.where(rim_tile, 6, 0)
    pl.semaphore_wait(barrier, here + 2 + 6 + 7)

    def remote(src, dst, send, recv, to):
        return pltpu.make_async_remote_copy(
            src_ref=src, dst_ref=dst, send_sem=send, recv_sem=recv, device_id=to, device_id_type=MESH
        )

    def drain(ref, sem):
        pltpu.make_async_copy(ref, ref, sem).wait()

    def edge(src, dst, n, lon, lat):
        return remote(src, dst, hs_sem.at[n], hr_sem.at[n], {"lon": lon, "lat": lat})

    @pl.when(rim_tile)
    def _():
        for d in range(1, 4):
            remote(send_ns.at[side], near.at[low], pas_sem, par_sem, {"lon": quarter(d), "lat": v}).start()

    to_west = edge(send_ew.at[0], halo_ew.at[1], 0, west, v)
    to_east = edge(send_ew.at[1], halo_ew.at[0], 1, east, v)
    to_north = [
        edge(send_ns.at[0], halo_ns.at[1], 2, u, v - 1),
        edge(send_dg.at[0], halo_dg.at[3], 3, west, v - 1),
        edge(send_dg.at[1], halo_dg.at[2], 4, east, v - 1),
    ]
    to_south = [
        edge(send_ns.at[1], halo_ns.at[0], 5, u, v + 1),
        edge(send_dg.at[2], halo_dg.at[1], 6, west, v + 1),
        edge(send_dg.at[3], halo_dg.at[0], 7, east, v + 1),
    ]

    to_west.start()
    to_east.start()

    @pl.when(v > 0)
    def _():
        for copy in to_north:
            copy.start()

    @pl.when(v < LAT - 1)
    def _():
        for copy in to_south:
            copy.start()

    @pl.loop(2, 34, unroll=4)
    def _(e):
        at = rows(e)
        for s in (sx, sd):
            line = s[1, at, :].astype(F32)
            s[0, at, :] = jnp.where(lane_row == 0, 0.0, pltpu.roll(line, 1, 0)).astype(BF)
            s[2, at, :] = jnp.where(lane_row == T - 1, 0.0, pltpu.roll(line, T - 1, 0)).astype(BF)

    for ref in (zx, zd, zh, zg, zs, zp, zq, ext, kz):
        ref[...] = jnp.zeros_like(ref)
    for b in range(3):
        sh[b, 0:T, :] = jnp.zeros((T, C), BF)
        sh[b, PX - T : PX, :] = jnp.zeros((T, C), BF)
    for ref in (dz, dzg):
        ref[0 : 3 * T, :] = jnp.zeros((3 * T, C), BF)
        ref[35 * T : 38 * T, :] = jnp.zeros((3 * T, C), BF)
    dz[3 * T : 35 * T, :] = sd[1, 2 * T : 34 * T, :]
    tiles[:, 9] = jnp.zeros((2, 16, C // 2), BF)

    def window(s, back, first, size):
        pieces = []
        for a in range(3):
            for b in range(3):
                start = (first + (2 - a if back else a)) * T
                pieces.append(s[2 - b if back else b, start : start + size * T, :])
        return jnp.concatenate(pieces, axis=1)

    def spread(s, left, right, e, line):
        at = rows(e)
        s[1, at, :] = line.astype(BF)
        s[0, at, :] = jnp.where(lane_row == 0, left, pltpu.roll(line, 1, 0)).astype(BF)
        s[2, at, :] = jnp.where(lane_row == T - 1, right, pltpu.roll(line, T - 1, 0)).astype(BF)

    fetched[2].wait()
    fetched[3].wait()
    pre1[2 * T : 32 * T, :] = dot(window(sx, False, 2, 30), w1[...])
    for tap in range(9):
        wt2[tap * C : (tap + 1) * C, :] = w2[tap * C : (tap + 1) * C, :].T
    back2[2 * T : 32 * T, :] = dot(window(sd, True, 2, 30), wt2[...])
    for e in range(3, 33):
        act, slp = gelu_parts(pre1[rows(e - 1), :])
        mask = jnp.where(jnp.full((T, C), e - 2, jnp.int32) < live, 1.0, 0.0)
        slope[rows(e - 1), :] = slp * mask
        spread(sh, 0.0, 0.0, e, act * mask)

    @pl.when(rim_tile)
    def _():
        drain(near.at[pl.ds(0, 3)], par_sem)
        drain(near.at[pl.ds(0, 3)], pas_sem)
        near[low] = send_ns[side]
        pivot = links[side, 0]
        n = lax.broadcasted_iota(jnp.int32, (8 * T, 4 * T), 0)
        at = lax.broadcasted_iota(jnp.int32, (8 * T, 4 * T), 1) + x * (4 * T)
        to = (n // (2 * T)) * 4 + low
        n = n & (2 * T - 1)
        q = n & 15
        in_east = n >= T + 16
        ring_col = jnp.where(in_east, T, -1)
        outer_col = jnp.where(in_east, T, -2) + (q & 1)
        col = jnp.where(n < T, n, jnp.where(q == 8, ring_col, outer_col))
        hit = ((pivot - to * T - col) & (LON * T - 1)) == at
        line = jnp.where(q == 8, 4, jnp.where(q < 8, q // 2, 5))
        corners = jnp.zeros((4, T, C), F32)
        for part in range(5):
            target = part if part == 4 else part ^ 1
            pick = jnp.where(hit & ((n < T) | (line == target)), 1.0, 0.0).astype(BF)
            lines = near[:, part * T : (part + 1) * T, :].reshape(4 * T, C)
            found = dot(pick, lines).reshape(4, 2 * T, C)
            picked[:, target * T : (target + 1) * T, :] = found[:, :T].astype(BF)
            corners = corners + found[:, T:]
        picked[:, MSG:, :] = corners.astype(BF)
        for d in range(1, 4):
            to = lax.rem(x + d, 4)
            remote(picked.at[to], arrived.at[x], pbs_sem, pbr_sem, {"lon": lax.rem(u + 4 * d, LON), "lat": v}).start()

    @pl.loop(3, 33, unroll=3)
    def _(e):
        spread(sg, 0.0, 0.0, e, back2[rows(e - 1), :] * slope[rows(e - 1), :])

    to_west.wait_recv()
    to_east.wait_recv()

    @pl.when(v > 0)
    def _():
        for copy in to_south:
            copy.wait_recv()

    @pl.when(v < LAT - 1)
    def _():
        for copy in to_north:
            copy.wait_recv()

    head = lax.broadcasted_iota(jnp.int32, (16, C), 0)

    def place(h):
        for k, (s, zz) in enumerate(((sx, zx), (sd, zd))):
            for t in range(2):
                px = halo_dg[2 * h + t].astype(F32)
                for r in range(2):
                    for n in range(2):
                        at = 4 * k + 2 * r + n
                        zz[t * 6 + n, pl.ds(34 * h + r, 1), :] = px[at : at + 1]
            for r in range(2):
                e = 34 * h + r
                line = halo_ns[h, (2 * k + r) * T : (2 * k + r + 1) * T, :].astype(F32)
                spread(s, zz[1, pl.ds(e, 1), :], zz[6, pl.ds(e, 1), :], e, line)
                for n, col in enumerate((0, 1, T - 2, T - 1)):
                    zz[2 + n, pl.ds(e, 1), :] = line[col : col + 1]
        mask = halo_ns[h, 4 * T :, :].astype(F32)
        e = 33 * h + 1
        for t in range(2):
            kz[3 * t, pl.ds(e, 1), :] = halo_dg[2 * h + t].astype(F32)[8:9]
            kz[1 + t, pl.ds(e, 1), :] = mask[t * (T - 1) : t * (T - 1) + 1]

    for k, zz in enumerate((zx, zd)):
        for n in range(2):
            zz[n, 2 : 2 + T, :] = halo_ew[0, (2 * k + n) * T : (2 * k + n + 1) * T, :].astype(F32)
            zz[6 + n, 2 : 2 + T, :] = halo_ew[1, (2 * k + n) * T : (2 * k + n + 1) * T, :].astype(F32)
            zz[2 + n, 2 : 2 + T, :] = cols[k, n]
            zz[4 + n, 2 : 2 + T, :] = cols[k, 2 + n]
    for t in range(2):
        kz[3 * t, 2 : 2 + T, :] = halo_ew[t, 4 * T :, :].astype(F32)
        kz[1 + t, 2 : 2 + T, :] = keep_col
    place(0)
    place(1)

    def insert(s, zz, e):
        at = pl.ds(pl.multiple_of(e * T, T), 16)
        s[0, at, :] = jnp.where(head == 0, zz[1, pl.ds(e, 1), :], s[0, at, :].astype(F32)).astype(BF)
        at = pl.ds(pl.multiple_of(e * T + 16, 16), 16)
        s[2, at, :] = jnp.where(head == 15, zz[6, pl.ds(e, 1), :], s[2, at, :].astype(F32)).astype(BF)

    for e in (2, 3, 32, 33):
        insert(sd, zd, e)

    @pl.loop(2, 34, unroll=4)
    def _(e):
        insert(sx, zx, e)

    def transpose(s, ref, k):
        at = pl.ds(pl.multiple_of(k * 128, 128), 128)
        for b in range(3):
            ref[b * C : (b + 1) * C, at] = s[b, at, :].T

    def transposed(s, ref):
        for k in range(PX // 128):
            transpose(s, ref, k)

    e_out, e_ring = jnp.where(south, 35, 0), jnp.where(south, 34, 1)
    e_edge, e_in = jnp.where(south, 33, 2), jnp.where(south, 32, 3)
    far = jnp.where(south, 2, 0)

    def extend(n, s, left, right, e):
        ext[n, 2 : 2 + T, :] = s[1, rows(e), :].astype(F32)
        for k, ref in enumerate(left):
            at = 2 - len(left) + k
            ext[n, at : at + 1, :] = ref[pl.ds(e, 1), :]
        for k, ref in enumerate(right):
            ext[n, 34 + k : 35 + k, :] = ref[pl.ds(e, 1), :]

    def straight(n):
        return jnp.concatenate([ext[n, 2 - b : 42 - b, :] for b in range(3)], axis=1).astype(BF)

    def turned(n):
        return jnp.concatenate([ext[n, b : b + 40, :] for b in range(3)], axis=1).astype(BF)

    def taps(w, row):
        return w[pl.ds(pl.multiple_of(row * 3 * C, 3 * C), 3 * C), :]

    def combine(up, mid, down, back):
        if back:
            up, down = down, up
        return pltpu.roll(up, 1, 0) + mid + pltpu.roll(down, mid.shape[0] - 1, 0)

    def strips(zz, w, back, ref):
        order = (2, 1, 0) if back else (0, 1, 2)
        lines = jnp.concatenate(
            [jnp.concatenate([zz[first + b] for b in order], axis=1) for first in (0, 1, 4, 5)], axis=0
        ).astype(BF)
        res = combine(*(dot(lines, w[a * 3 * C : (a + 1) * 3 * C, :]) for a in range(3)), back)
        for t in range(4):
            ref[t] = res[t * STRIP : (t + 1) * STRIP]

    def put_columns(s, zz):
        @pl.loop(3, 33, unroll=3)
        def _(e):
            c = [zz[t, pl.ds(e, 1), :] for t in range(4)]
            at = pl.ds(pl.multiple_of(e * T, T), 16)
            s[1, at, :] = jnp.where(head == 0, c[1], s[1, at, :].astype(F32)).astype(BF)
            line = jnp.where(head == 1, c[1], s[0, at, :].astype(F32))
            s[0, at, :] = jnp.where(head == 0, c[0], line).astype(BF)
            at = pl.ds(pl.multiple_of(e * T + 16, 16), 16)
            s[1, at, :] = jnp.where(head == 15, c[2], s[1, at, :].astype(F32)).astype(BF)
            line = jnp.where(head == 14, c[2], s[2, at, :].astype(F32))
            s[2, at, :] = jnp.where(head == 15, c[3], line).astype(BF)

    def of_row(res, t):
        at = (0, 1, T, T + 1)[t]
        return res[at : at + 1]

    def outer(s, back):
        return jnp.concatenate([window(s, back, 0, 2), window(s, back, 32, 2)], axis=0)

    transposed(sx, xt)
    res = dot(outer(sx, False), w1[...])
    pre1[0 : 2 * T, :] = res[: 2 * T]
    pre1[32 * T : 34 * T, :] = res[2 * T :]
    strips(zx, w1, False, zp)

    def activate_strips():
        for t in range(4):
            act, slp = gelu_parts(zp[t])
            zh[t] = act * kz[t]
            zs[t] = slp * kz[t]

    def activate(e, mask):
        act, slp = gelu_parts(pre1[rows(e - 1), :])
        slope[rows(e - 1), :] = slp * mask
        spread(sh, zh[0, pl.ds(e, 1), :], zh[3, pl.ds(e, 1), :], e, act * mask)

    activate_strips()
    activate(1, halo_ns[0, 4 * T :, :].astype(F32))
    activate(2, jnp.where(jnp.zeros((T, C), jnp.int32) < live, 1.0, 0.0))
    activate(33, keep_last)
    activate(34, halo_ns[1, 4 * T :, :].astype(F32))
    put_columns(sh, zh)
    transposed(sh, xth)

    res = dot(outer(sd, True), wt2[...])
    back2[0 : 2 * T, :] = res[: 2 * T]
    back2[32 * T : 34 * T, :] = res[2 * T :]
    strips(zd, wt2, True, zq)

    def scale_strips():
        for t in range(4):
            zg[t] = zq[t] * zs[t]

    def scale(e):
        line = back2[rows(e - 1), :] * slope[rows(e - 1), :]
        spread(sg, zg[0, pl.ds(e, 1), :], zg[3, pl.ds(e, 1), :], e, line)

    scale_strips()
    for e in (1, 2, 33, 34):
        scale(e)
    put_columns(sg, zg)
    dzg[3 * T : 35 * T, :] = sg[1, 2 * T : 34 * T, :]

    @pl.when(rim_tile)
    def _():
        drain(arrived.at[pl.ds(0, 3)], pbr_sem)
        drain(arrived.at[pl.ds(0, 3)], pbs_sem)
        arrived[x] = picked[x]
        total = arrived[0].astype(F32)
        for k in range(1, 4):
            total = total + arrived[k].astype(F32)
        halo_ns[side] = total[:MSG].astype(BF)
        halo_dg[2 * side] = total[MSG : MSG + 16].astype(BF)
        halo_dg[2 * side + 1] = total[MSG + 16 :].astype(BF)
        place(side)
        for n, e in enumerate((e_out, e_ring, e_edge, e_in)):
            extend(n, sx, (zx.at[0], zx.at[1]), (zx.at[6], zx.at[7]), e)
        pre = jnp.zeros((2 * STRIP, C), F32)
        for pair_of, row in (((straight(2), turned(1)), far), ((straight(1), turned(2)), 1), ((straight(0), turned(3)), 2 - far)):
            pre = pre + dot(jnp.concatenate(pair_of, axis=0), taps(w1, row))
        for k, e in enumerate((e_ring, e_edge)):
            pre1[rows(e - 1), :] = pre[k * STRIP + 1 : k * STRIP + 1 + T]
            for t in range(4):
                zp[t, pl.ds(e, 1), :] = of_row(pre[k * STRIP : (k + 1) * STRIP], t)
        activate_strips()
        activate(e_ring, halo_ns[side, 4 * T :, :].astype(F32))
        activate(e_edge, jnp.where(jnp.full((T, C), e_edge - 2, jnp.int32) < live, 1.0, 0.0))

        for n, e in enumerate((e_out, e_ring, e_edge, e_in)):
            extend(n, sd, (zd.at[0], zd.at[1]), (zd.at[6], zd.at[7]), e)
        back = dot(jnp.concatenate([turned(0), turned(1)], axis=0), taps(wt2, far))
        back = back + dot(jnp.concatenate([straight(2), straight(3)], axis=0), taps(wt2, far))
        back = back + dot(jnp.concatenate([turned(1), straight(2)], axis=0), taps(wt2, 1))
        for k, e in enumerate((e_ring, e_edge)):
            back2[rows(e - 1), :] = back[k * STRIP + 1 : k * STRIP + 1 + T]
            for t in range(4):
                zq[t, pl.ds(e, 1), :] = of_row(back[k * STRIP : (k + 1) * STRIP], t)
        scale_strips()
        scale(e_ring)
        scale(e_edge)
        dzg[rows(e_edge + 1), :] = sg[1, rows(e_edge), :]
        transpose(sx, xt, 8 * side)
        transpose(sh, xth, 8 * side)

    sibling = {"lon": u + 1 - 2 * core, "lat": v}

    def pair(g, a):
        return remote(gsend.at[g, a], gpair.at[g, a], s1_sem.at[g, a], r1_sem.at[g, a], sibling)

    def add_pair(g, a):
        pair(g, a).wait()
        total = gkeep[g, a] + gpair[g, a].astype(F32)
        gsum[g, 3 * a : 3 * a + 3] = total.astype(BF).reshape(3, 4, 4, 16, C // 2)

    def first_axis(g):
        for d in range(1, 4):
            to = lax.rem(x + d, 4)
            remote(gsum.at[g, pl.ds(0, 5), to], px1.at[g, x], s2_sem.at[g, 0], r2_sem.at[g, 0], along_x(d)).start()
            to = lax.rem(y + d, 4)
            remote(gsum.at[g, pl.ds(5, 4), :, to], py1.at[g, y], s2_sem.at[g, 1], r2_sem.at[g, 1], along_y(d)).start()

    def total_of(ref, g):
        total = ref[g, 0].astype(F32)
        for k in range(1, 4):
            total = total + ref[g, k].astype(F32)
        return total.astype(BF)

    def second_axis(g):
        drain(px1.at[g, pl.ds(0, 3)], r2_sem.at[g, 0])
        px1[g, x] = gsum[g, 0:5, x]
        sx1[g] = total_of(px1, g)
        for d in range(1, 4):
            to = lax.rem(y + d, 4)
            remote(sx1.at[g, :, to], py2.at[g, y], s2_sem.at[g, 2], r2_sem.at[g, 2], along_y(d)).start()
        drain(py1.at[g, pl.ds(0, 3)], r2_sem.at[g, 1])
        py1[g, y] = gsum[g, 5:9, :, y]
        sy1[g] = total_of(py1, g)
        for d in range(1, 4):
            to = lax.rem(x + d, 4)
            remote(sy1.at[g, :, to], px2.at[g, x], s2_sem.at[g, 3], r2_sem.at[g, 3], along_x(d)).start()

    def plane_total(g):
        drain(py2.at[g, pl.ds(0, 3)], r2_sem.at[g, 2])
        py2[g, y] = sx1[g, :, y]
        tiles[g, 0:5] = total_of(py2, g)
        drain(px2.at[g, pl.ds(0, 3)], r2_sem.at[g, 3])
        px2[g, x] = sy1[g, :, x]
        tiles[g, 5:9] = total_of(px2, g)

    def weight_grad(g, left, right, between=None):
        for a in range(3):
            res = dot(left[...], right[(2 - a) * T : (2 - a) * T + PX, :])
            lo, hi = res[:, : C // 2], res[:, C // 2 :]
            gkeep[g, a] = jnp.where(core == 0, lo, hi).reshape(3, C, C // 2)
            gsend[g, a] = jnp.where(core == 0, hi, lo).astype(BF).reshape(3, C, C // 2)
            pair(g, a).start()
            if a:
                add_pair(g, a - 1)
            elif between is not None:
                between()

    def first_done():
        add_pair(0, 2)
        first_axis(0)

    weight_grad(0, xth, dz)
    weight_grad(1, xt, dzg, first_done)

    size = T // 2

    def forward(first):
        row = lax.broadcasted_iota(jnp.int32, (size * T, C), 0) // T + first
        pre = dot(window(sh, False, 1 + first, size), w2[...])
        masked = sx[1, (2 + first) * T : (2 + first + size) * T, :].astype(F32)
        out[first : first + size] = (masked + jnp.where(row < live, pre, 0.0)).astype(BF).reshape(size, T, C)

    for tap in range(9):
        wt1[tap * C : (tap + 1) * C, :] = w1[tap * C : (tap + 1) * C, :].T
    forward(0)
    add_pair(1, 2)
    first_axis(1)
    forward(size)
    second_axis(0)

    row = lax.broadcasted_iota(jnp.int32, (T * T, C), 0) // T
    back = dot(window(sg, True, 1, T), wt1[...])
    total = cot[...].reshape(T * T, C).astype(F32) + back
    fgrad[...] = jnp.where(row < live, total, 0.0).astype(BF).reshape(T, T, C)

    @pl.when(rim_tile)
    def _():
        for n, e in ((1, e_ring), (2, e_edge), (3, e_in)):
            extend(n, sg, (zg.at[0],), (zg.at[3],), e)
        w_far, w_mid = taps(wt1, far), taps(wt1, 1)
        rim = dot(turned(1), w_far) + dot(straight(3), w_far) + dot(straight(2), w_mid)
        i = e_edge - 2
        total = cot[i].astype(F32) + rim[1 : 1 + T]
        kept = jnp.full((T, C), i, jnp.int32) < live
        fgrad[i] = jnp.where(kept, total, 0.0).astype(BF)

    second_axis(1)
    plane_total(0)
    plane_total(1)

    def first_tile(plane):
        return lax.div(18 * plane + 15 - spot, 16)

    for d in range(1, PLANES):
        to = lax.rem(z + d, PLANES)
        remote(
            tiles.at[:, pl.ds(first_tile(to), 2)],
            parts3.at[z],
            s3_sem,
            r3_sem,
            {"lon": u, "lat": to * 2 + y_lo},
        ).start()

    mine = first_tile(z)
    drain(parts3.at[pl.ds(0, PLANES - 1)], r3_sem)
    parts3[z] = tiles[:, pl.ds(mine, 2)]
    total = parts3[0].astype(F32)
    for k in range(1, PLANES):
        total = total + parts3[k].astype(F32)
    for slot in range(2):
        own[slot] = total[:, slot].astype(BF)

    def deliver(slot):
        group = (mine + slot) * 16 + spot
        lat, at = lax.div(group, 9), lax.rem(group, 9)
        src, dst = own.at[slot], final.at[core, at]

        def to(d):
            lon = 2 * lax.rem(lax.div(u, 2) + d, 8) + core
            return remote(src, dst, s4_sem.at[2 * slot + (d == 0)], r4_sem, {"lon": lon, "lat": lat})

        for d in range(1, 8):
            to(d).start()

        @pl.when(lat == v)
        def _():
            pltpu.make_async_copy(src, dst, r4_sem).start()

        @pl.when(lat != v)
        def _():
            to(0).start()

    def delivered(slot):
        lat = lax.div((mine + slot) * 16 + spot, 9)
        drain(final.at[0, pl.ds(0, 7)], s4_sem.at[2 * slot])

        @pl.when(lat != v)
        def _():
            drain(final.at[0, 0], s4_sem.at[2 * slot + 1])

    has_two = first_tile(z + 1) - mine == 2
    deliver(0)

    @pl.when(has_two)
    def _():
        deliver(1)

    drain(final.at[core], r4_sem)
    last = remote(final.at[core], final.at[core], s5_sem, r5_sem, sibling)
    last.start()
    for h in range(2):
        @pl.when(core == h)
        def _(h=h):
            sums[h] = final[h]
    delivered(0)

    @pl.when(has_two)
    def _():
        delivered(1)

    last.wait()
    for h in range(2):
        @pl.when(core != h)
        def _(h=h):
            sums[h] = final[h]

    to_west.wait_send()
    to_east.wait_send()

    @pl.when(v > 0)
    def _():
        for copy in to_north:
            copy.wait_send()

    @pl.when(v < LAT - 1)
    def _():
        for copy in to_south:
            copy.wait_send()

    for g in range(2):
        for k, ref in enumerate((px1, py1, py2, px2)):
            drain(ref.at[g, pl.ds(0, 3)], s2_sem.at[g, k])
    drain(parts3.at[pl.ds(0, PLANES - 1)], s3_sem)


def local(field, first_weight, second_weight, cotangent, live_rows, polar_links):
    vmem = pl.BlockSpec(memory_space=pltpu.VMEM)
    smem = pl.BlockSpec(memory_space=pltpu.SMEM)
    anywhere = pl.BlockSpec(memory_space=pl.ANY)
    half = C // 2
    tile = jax.ShapeDtypeStruct((T, T, C), BF)
    share = jax.ShapeDtypeStruct((SHARE, C), F32)
    flat = pltpu.VMEM((3, PX, C), BF)
    columns = pltpu.VMEM((8, STRIP, C), F32)
    four = pltpu.VMEM((4, STRIP, C), F32)
    ringed = pltpu.VMEM((RING * T, C), F32)
    weights = pltpu.VMEM((9 * C, C), BF)
    message = pltpu.VMEM((2, MSG, C), BF)
    corners = pltpu.VMEM((4, 16, C), BF)
    grads = pltpu.VMEM((2, 3, 3, C, half), BF)
    dma = pltpu.SemaphoreType.DMA
    made, back, sums = pl.pallas_call(
        kernel,
        out_shape=(pltpu.VMEM((T, T, C), BF), pltpu.VMEM((T, T, C), BF), pltpu.VMEM((2, 9, 2, 16, half), BF)),
        in_specs=[anywhere, anywhere, anywhere, anywhere, smem, smem],
        out_specs=(vmem, vmem, vmem),
        scratch_shapes=[
            *([flat] * 4),
            *([columns] * 2),
            *([four] * 6),
            pltpu.VMEM((T, T, C), BF),
            pltpu.VMEM((T, T, C), BF),
            pltpu.VMEM((2, 4, T, C), F32),
            pltpu.VMEM((4, 16, C), F32),
            *([ringed] * 3),
            *([pltpu.VMEM((3 * C, PX), BF)] * 2),
            *([pltpu.VMEM((38 * T, C), BF)] * 2),
            *([weights] * 4),
            pltpu.VMEM((4, 48, C), F32),
            message,
            message,
            corners,
            message,
            message,
            corners,
            pltpu.VMEM((4, MSG, C), BF),
            pltpu.VMEM((4, PICK, C), BF),
            pltpu.VMEM((4, PICK, C), BF),
            pltpu.VMEM((2, 3, 3, C, half), F32),
            grads,
            grads,
            pltpu.VMEM((2, 9, 4, 4, 16, half), BF),
            pltpu.VMEM((2, 4, 5, 4, 16, half), BF),
            pltpu.VMEM((2, 4, 4, 4, 16, half), BF),
            pltpu.VMEM((2, 5, 4, 16, half), BF),
            pltpu.VMEM((2, 4, 4, 16, half), BF),
            pltpu.VMEM((2, 4, 5, 16, half), BF),
            pltpu.VMEM((2, 4, 4, 16, half), BF),
            pltpu.VMEM((2, 10, 16, half), BF),
            pltpu.VMEM((PLANES, 2, 2, 16, half), BF),
            pltpu.VMEM((2, 2, 16, half), BF),
            pltpu.VMEM((2, 9, 2, 16, half), BF),
            dma((4,)),
            dma((8,)),
            dma((8,)),
            dma,
            dma,
            dma,
            dma,
            dma((2, 3)),
            dma((2, 3)),
            dma((2, 4)),
            dma((2, 4)),
            dma,
            dma,
            dma((4,)),
            dma,
            dma,
            dma,
        ],
        compiler_params=pltpu.CompilerParams(
            collective_id=0, has_side_effects=True, vmem_limit_bytes=56 * 1024 * 1024
        ),
        cost_estimate=pl.CostEstimate(
            flops=12 * T * T * 9 * C * C, bytes_accessed=6_000_000, transcendentals=2 * T * T * C
        ),
    )(field, first_weight, second_weight, cotangent, live_rows, polar_links)
    made, back, sums = (pltpu.with_memory_space_constraint(r, pltpu.VMEM) for r in (made, back, sums))
    return pl.pallas_call(
        finish,
        out_shape=(tile, tile, share, share),
        in_specs=[vmem] * 3,
        out_specs=(anywhere,) * 4,
        scratch_shapes=[pltpu.VMEM((SHARE, C), F32), pltpu.VMEM((SHARE, C), F32), dma((4,))],
        compiler_params=pltpu.CompilerParams(vmem_limit_bytes=4 * 1024 * 1024),
        cost_estimate=pl.CostEstimate(flops=2 * SHARE * C, bytes_accessed=3_000_000, transcendentals=0),
    )(made, back, sums)


def solution(mesh):
    in_specs = (P("lat", "lon", None), P(), P(), P("lat", "lon", None), P("lon", "lat"), P())
    out_specs = (P("lat", "lon", None), P("lat", "lon", None), P("lat", None), P("lat", None))
    return jax.shard_map(local, mesh=mesh, in_specs=in_specs, out_specs=out_specs, check_vma=False)
```

```python
import math

import jax
import jax.numpy as jnp
from jax import lax
from jax.experimental import pallas as pl
from jax.experimental.pallas import tpu as pltpu
from jax.sharding import PartitionSpec as P

MESH = pl.DeviceIdType.MESH
BF = jnp.bfloat16
F32 = jnp.float32
C = 256
T = 32
EXT = T + 4
PX = EXT * T
RING = T + 2
MSG = 5 * T
STRIP = 40
LON = 16
LAT = 16
PLANES = 8
SHARE = 3 * T // 2 * 3
PICK = MSG + T


def dot(a, b):
    return jnp.dot(a, b, preferred_element_type=F32)


def gelu_parts(pre):
    cdf = 0.5 * (1.0 + lax.erf(pre * 0.7071067811865476))
    dens = jnp.exp(-0.5 * pre * pre) * 0.3989422804014327
    return (pre * cdf, cdf + pre * dens)


def rows(start, size=T):
    return pl.ds(pl.multiple_of(start * T, T), size)


def finish(made, back, sums, out, fgrad, grad1, grad2, share1, share2, sem):
    copies = [pltpu.make_async_copy(made, out, sem.at[0]), pltpu.make_async_copy(back, fgrad, sem.at[1])]
    for copy in copies:
        copy.start()
    scale = 1.0 / math.sqrt(LON * T * LAT * T)
    for g, (ref, dst) in enumerate(((share2, grad2), (share1, grad1))):
        for k in range(9):
            for h in range(2):
                ref[k * 16 : (k + 1) * 16, h * 128 : (h + 1) * 128] = sums[h, k, g].astype(F32) * scale
        copies.append(pltpu.make_async_copy(ref, dst, sem.at[2 + g]))
        copies[-1].start()
    for copy in copies:
        copy.wait()


def kernel(
    field_hbm,
    w1_hbm,
    w2_hbm,
    cot_hbm,
    live_ref,
    links,
    out,
    fgrad,
    sums,
    sx,
    sd,
    sh,
    sg,
    zx,
    zd,
    zh,
    zg,
    zs,
    zp,
    zq,
    kz,
    field,
    cot,
    cols,
    corner,
    pre1,
    back2,
    slope,
    xt,
    xth,
    dz,
    dzg,
    gm,
    w1,
    w2,
    wt1,
    wt2,
    ext,
    send_ns,
    send_ew,
    send_dg,
    halo_ns,
    halo_ew,
    halo_dg,
    near,
    picked,
    arrived,
    gkeep,
    gsend,
    gpair,
    gsum,
    px1,
    py1,
    sx1,
    sy1,
    py2,
    px2,
    tiles,
    parts3,
    own,
    final,
    w_sem,
    hs_sem,
    hr_sem,
    pas_sem,
    par_sem,
    pbs_sem,
    pbr_sem,
    s1_sem,
    r1_sem,
    s2_sem,
    r2_sem,
    s3_sem,
    r3_sem,
    s4_sem,
    r4_sem,
    s5_sem,
    r5_sem,
):
    u, v = lax.axis_index("lon"), lax.axis_index("lat")
    core, x, z = lax.rem(u, 2), lax.div(u, 4), lax.div(v, 2)
    low = lax.rem(u, 4)
    y_lo = lax.rem(v, 2)
    y = lax.div(low, 2) * 2 + y_lo
    spot = x * 4 + y
    north, south = v == 0, v == LAT - 1
    rim_tile = north | south
    side = jnp.where(south, 1, 0)
    live = live_ref[0, 0]
    east, west = lax.rem(u + 1, LON), lax.rem(u + LON - 1, LON)

    def in_plane(place):
        px, py = lax.div(place, 4), lax.rem(place, 4)
        return {"lon": px * 4 + lax.div(py, 2) * 2 + core, "lat": z * 2 + lax.rem(py, 2)}

    def along_x(d):
        return in_plane(lax.rem(x + d, 4) * 4 + y)

    def along_y(d):
        return in_plane(x * 4 + lax.rem(y + d, 4))

    def quarter(d):
        return x * 4 + lax.rem(low + d, 4)

    fetched = [
        pltpu.make_async_copy(src, dst, w_sem.at[n])
        for n, (src, dst) in enumerate(((field_hbm, field), (cot_hbm, cot), (w1_hbm, w1), (w2_hbm, w2)))
    ]
    for copy in fetched:
        copy.start()

    barrier = pltpu.get_barrier_semaphore()

    def greet(lon, lat):
        pl.semaphore_signal(barrier, inc=1, device_id={"lon": lon, "lat": lat}, device_id_type=MESH)

    greet(east, v)
    greet(west, v)

    @pl.when(v > 0)
    def _():
        for lon in (west, u, east):
            greet(lon, v - 1)

    @pl.when(v < LAT - 1)
    def _():
        for lon in (west, u, east):
            greet(lon, v + 1)

    @pl.when(rim_tile)
    def _():
        for d in range(1, 4):
            greet(quarter(d), v)
            greet(lax.rem(u + 4 * d, LON), v)

    for d in range(1, 4):
        for to in (along_x(d), along_y(d)):
            greet(to["lon"], to["lat"])

    @pl.loop(1, PLANES)
    def _(d):
        greet(u, lax.rem(z + d, PLANES) * 2 + y_lo)

    lane_row = lax.broadcasted_iota(jnp.int32, (T, C), 0)
    fetched[0].wait()
    fetched[1].wait()

    @pl.loop(0, T, unroll=4)
    def _(i):
        kept = jnp.full((T, C), i, jnp.int32) < live
        for k, (src, dst) in enumerate(((field, sx), (cot, sd))):
            line = jnp.where(kept, src[i].astype(F32), 0.0)
            dst[1, rows(i + 2), :] = line.astype(BF)
            for n, col in enumerate((0, 1, T - 2, T - 1)):
                cols[k, n, pl.ds(i, 1), :] = line[col : col + 1]

    keep_col = jnp.where(lane_row < live, 1.0, 0.0)
    keep_last = jnp.where(jnp.full((T, C), T - 1, jnp.int32) < live, 1.0, 0.0)
    for s in range(2):
        for k, src in enumerate((sx, sd)):
            first = 2 if s == 0 else T
            send_ns[s, 2 * k * T : (2 * k + 2) * T, :] = src[1, first * T : (first + 2) * T, :]
            for n in range(2):
                send_ew[s, (2 * k + n) * T : (2 * k + n + 1) * T, :] = cols[k, 2 * s + n].astype(BF)
        send_ns[s, 4 * T :, :] = jnp.ones((T, C), BF) if s == 0 else keep_last.astype(BF)
        send_ew[s, 4 * T :, :] = keep_col.astype(BF)
    corner[...] = jnp.zeros_like(corner)
    for s in range(2):
        for t in range(2):
            for k in range(2):
                for r in range(2):
                    for n in range(2):
                        at = 4 * k + 2 * r + n
                        line = (0 if s == 0 else T - 2) + r
                        corner[2 * s + t, at : at + 1, :] = cols[k, 2 * t + n, line : line + 1, :]
            corner[2 * s + t, 8:9, :] = jnp.ones((1, C), F32) if s == 0 else keep_last[0:1]
    send_dg[...] = corner[...].astype(BF)

    here = jnp.where(v > 0, 3, 0) + jnp.where(v < LAT - 1, 3, 0) + jnp.where(rim_tile, 6, 0)
    pl.semaphore_wait(barrier, here + 2 + 6 + 7)

    def remote(src, dst, send, recv, to):
        return pltpu.make_async_remote_copy(
            src_ref=src, dst_ref=dst, send_sem=send, recv_sem=recv, device_id=to, device_id_type=MESH
        )

    def drain(ref, sem):
        pltpu.make_async_copy(ref, ref, sem).wait()

    def edge(src, dst, n, lon, lat):
        return remote(src, dst, hs_sem.at[n], hr_sem.at[n], {"lon": lon, "lat": lat})

    @pl.when(rim_tile)
    def _():
        for d in range(1, 4):
            remote(send_ns.at[side], near.at[low], pas_sem, par_sem, {"lon": quarter(d), "lat": v}).start()

    to_west = edge(send_ew.at[0], halo_ew.at[1], 0, west, v)
    to_east = edge(send_ew.at[1], halo_ew.at[0], 1, east, v)
    to_north = [
        edge(send_ns.at[0], halo_ns.at[1], 2, u, v - 1),
        edge(send_dg.at[0], halo_dg.at[3], 3, west, v - 1),
        edge(send_dg.at[1], halo_dg.at[2], 4, east, v - 1),
    ]
    to_south = [
        edge(send_ns.at[1], halo_ns.at[0], 5, u, v + 1),
        edge(send_dg.at[2], halo_dg.at[1], 6, west, v + 1),
        edge(send_dg.at[3], halo_dg.at[0], 7, east, v + 1),
    ]

    to_west.start()
    to_east.start()

    @pl.when(v > 0)
    def _():
        for copy in to_north:
            copy.start()

    @pl.when(v < LAT - 1)
    def _():
        for copy in to_south:
            copy.start()

    @pl.loop(2, 34, unroll=4)
    def _(e):
        at = rows(e)
        for s in (sx, sd):
            line = s[1, at, :].astype(F32)
            s[0, at, :] = jnp.where(lane_row == 0, 0.0, pltpu.roll(line, 1, 0)).astype(BF)
            s[2, at, :] = jnp.where(lane_row == T - 1, 0.0, pltpu.roll(line, T - 1, 0)).astype(BF)

    for ref in (zx, zd, zh, zg, zs, zp, zq, ext, kz):
        ref[...] = jnp.zeros_like(ref)
    for b in range(3):
        for first, last in ((0, 3), (33, EXT)):
            sh[b, first * T : last * T, :] = jnp.zeros(((last - first) * T, C), BF)
        for first, last in ((0, 2), (34, EXT)):
            sx[b, first * T : last * T, :] = jnp.zeros(((last - first) * T, C), BF)
    for ref in (dz, dzg):
        ref[0 : 4 * T, :] = jnp.zeros((4 * T, C), BF)
        ref[34 * T : 38 * T, :] = jnp.zeros((4 * T, C), BF)

    @pl.when(rim_tile)
    def _():
        halo_ns[side] = jnp.zeros((MSG, C), BF)
        for t in range(2):
            halo_dg[2 * side + t] = jnp.zeros((16, C), BF)

    dz[3 * T : 35 * T, :] = sd[1, 2 * T : 34 * T, :]
    tiles[:, 9] = jnp.zeros((2, 16, C // 2), BF)

    def window(s, back, first, size):
        pieces = []
        for a in range(3):
            for b in range(3):
                start = (first + (2 - a if back else a)) * T
                pieces.append(s[2 - b if back else b, start : start + size * T, :])
        return jnp.concatenate(pieces, axis=1)

    def spread(s, left, right, e, line):
        at = rows(e)
        s[1, at, :] = line.astype(BF)
        s[0, at, :] = jnp.where(lane_row == 0, left, pltpu.roll(line, 1, 0)).astype(BF)
        s[2, at, :] = jnp.where(lane_row == T - 1, right, pltpu.roll(line, T - 1, 0)).astype(BF)

    def transposed(s, ref):
        for k in range(PX // 128):
            for b in range(3):
                ref[b * C : (b + 1) * C, k * 128 : (k + 1) * 128] = s[b, k * 128 : (k + 1) * 128, :].T

    inner = (lane_row > 0) & (lane_row < T - 1)

    fetched[2].wait()
    fetched[3].wait()
    pre1[2 * T : 32 * T, :] = dot(window(sx, False, 2, 30), w1[...])
    for tap in range(9):
        wt2[tap * C : (tap + 1) * C, :] = w2[tap * C : (tap + 1) * C, :].T
    transposed(sx, xt)
    back2[2 * T : 32 * T, :] = dot(window(sd, True, 2, 30), wt2[...])
    for e in range(3, 33):
        act, slp = gelu_parts(pre1[rows(e - 1), :])
        mask = jnp.where((jnp.full((T, C), e - 2, jnp.int32) < live) & inner, 1.0, 0.0)
        slope[rows(e - 1), :] = slp * mask
        spread(sh, 0.0, 0.0, e, act * mask)

    @pl.when(rim_tile)
    def _():
        drain(near.at[pl.ds(0, 3)], par_sem)
        drain(near.at[pl.ds(0, 3)], pas_sem)
        near[low] = send_ns[side]
        pivot = links[side, 0]
        n = lax.broadcasted_iota(jnp.int32, (8 * T, 4 * T), 0)
        at = lax.broadcasted_iota(jnp.int32, (8 * T, 4 * T), 1) + x * (4 * T)
        to = (n // (2 * T)) * 4 + low
        n = n & (2 * T - 1)
        q = n & 15
        in_east = n >= T + 16
        ring_col = jnp.where(in_east, T, -1)
        outer_col = jnp.where(in_east, T, -2) + (q & 1)
        col = jnp.where(n < T, n, jnp.where(q == 8, ring_col, outer_col))
        hit = ((pivot - to * T - col) & (LON * T - 1)) == at
        line = jnp.where(q == 8, 4, jnp.where(q < 8, q // 2, 5))
        corners = jnp.zeros((4, T, C), F32)
        for part in range(5):
            target = part if part == 4 else part ^ 1
            pick = jnp.where(hit & ((n < T) | (line == target)), 1.0, 0.0).astype(BF)
            lines = near[:, part * T : (part + 1) * T, :].reshape(4 * T, C)
            found = dot(pick, lines).reshape(4, 2 * T, C)
            picked[:, target * T : (target + 1) * T, :] = found[:, :T].astype(BF)
            corners = corners + found[:, T:]
        picked[:, MSG:, :] = corners.astype(BF)
        for d in range(1, 4):
            to = lax.rem(x + d, 4)
            remote(picked.at[to], arrived.at[x], pbs_sem, pbr_sem, {"lon": lax.rem(u + 4 * d, LON), "lat": v}).start()

    @pl.loop(3, 33, unroll=3)
    def _(e):
        spread(sg, 0.0, 0.0, e, back2[rows(e - 1), :] * slope[rows(e - 1), :])

    dzg[4 * T : 34 * T, :] = sg[1, 3 * T : 33 * T, :]
    transposed(sh, xth)
    for g, left, right in ((1, xt, dzg), (0, xth, dz)):
        for a in range(3):
            gm[g, a] = dot(left[...], right[(2 - a) * T : (2 - a) * T + PX, :])

    to_west.wait_recv()
    to_east.wait_recv()

    @pl.when(v > 0)
    def _():
        for copy in to_south:
            copy.wait_recv()

    @pl.when(v < LAT - 1)
    def _():
        for copy in to_north:
            copy.wait_recv()

    head = lax.broadcasted_iota(jnp.int32, (16, C), 0)

    def place(h):
        for k, (s, zz) in enumerate(((sx, zx), (sd, zd))):
            for t in range(2):
                px = halo_dg[2 * h + t].astype(F32)
                for r in range(2):
                    for n in range(2):
                        at = 4 * k + 2 * r + n
                        zz[t * 6 + n, pl.ds(34 * h + r, 1), :] = px[at : at + 1]
            for r in range(2):
                e = 34 * h + r
                line = halo_ns[h, (2 * k + r) * T : (2 * k + r + 1) * T, :].astype(F32)
                spread(s, zz[1, pl.ds(e, 1), :], zz[6, pl.ds(e, 1), :], e, line)
                for n, col in enumerate((0, 1, T - 2, T - 1)):
                    zz[2 + n, pl.ds(e, 1), :] = line[col : col + 1]
        mask = halo_ns[h, 4 * T :, :].astype(F32)
        e = 33 * h + 1
        for t in range(2):
            kz[3 * t, pl.ds(e, 1), :] = halo_dg[2 * h + t].astype(F32)[8:9]
            kz[1 + t, pl.ds(e, 1), :] = mask[t * (T - 1) : t * (T - 1) + 1]

    for k, zz in enumerate((zx, zd)):
        for n in range(2):
            zz[n, 2 : 2 + T, :] = halo_ew[0, (2 * k + n) * T : (2 * k + n + 1) * T, :].astype(F32)
            zz[6 + n, 2 : 2 + T, :] = halo_ew[1, (2 * k + n) * T : (2 * k + n + 1) * T, :].astype(F32)
            zz[2 + n, 2 : 2 + T, :] = cols[k, n]
            zz[4 + n, 2 : 2 + T, :] = cols[k, 2 + n]
    for t in range(2):
        kz[3 * t, 2 : 2 + T, :] = halo_ew[t, 4 * T :, :].astype(F32)
        kz[1 + t, 2 : 2 + T, :] = keep_col
    place(0)
    place(1)

    def insert(s, zz, e):
        at = pl.ds(pl.multiple_of(e * T, T), 16)
        s[0, at, :] = jnp.where(head == 0, zz[1, pl.ds(e, 1), :], s[0, at, :].astype(F32)).astype(BF)
        at = pl.ds(pl.multiple_of(e * T + 16, 16), 16)
        s[2, at, :] = jnp.where(head == 15, zz[6, pl.ds(e, 1), :], s[2, at, :].astype(F32)).astype(BF)

    for e in (2, 3, 32, 33):
        insert(sx, zx, e)
        insert(sd, zd, e)

    e_out, e_ring = jnp.where(south, 35, 0), jnp.where(south, 34, 1)
    e_edge, e_in = jnp.where(south, 33, 2), jnp.where(south, 32, 3)
    far = jnp.where(south, 2, 0)

    def extend(n, s, left, right, e):
        ext[n, 2 : 2 + T, :] = s[1, rows(e), :].astype(F32)
        for k, ref in enumerate(left):
            at = 2 - len(left) + k
            ext[n, at : at + 1, :] = ref[pl.ds(e, 1), :]
        for k, ref in enumerate(right):
            ext[n, 34 + k : 35 + k, :] = ref[pl.ds(e, 1), :]

    def straight(n):
        return jnp.concatenate([ext[n, 2 - b : 42 - b, :] for b in range(3)], axis=1).astype(BF)

    def turned(n):
        return jnp.concatenate([ext[n, b : b + 40, :] for b in range(3)], axis=1).astype(BF)

    def taps(w, row):
        return w[pl.ds(pl.multiple_of(row * 3 * C, 3 * C), 3 * C), :]

    def combine(up, mid, down, back):
        if back:
            up, down = down, up
        return pltpu.roll(up, 1, 0) + mid + pltpu.roll(down, mid.shape[0] - 1, 0)

    def strips(zz, w, back, ref):
        order = (2, 1, 0) if back else (0, 1, 2)
        lines = jnp.concatenate(
            [jnp.concatenate([zz[first + b] for b in order], axis=1) for first in (0, 1, 4, 5)], axis=0
        ).astype(BF)
        res = combine(*(dot(lines, w[a * 3 * C : (a + 1) * 3 * C, :]) for a in range(3)), back)
        for t in range(4):
            ref[t] = res[t * STRIP : (t + 1) * STRIP]

    def put_columns(s, zz):
        @pl.loop(3, 33, unroll=3)
        def _(e):
            c = [zz[t, pl.ds(e, 1), :] for t in range(4)]
            at = pl.ds(pl.multiple_of(e * T, T), 16)
            s[1, at, :] = jnp.where(head == 0, c[1], s[1, at, :].astype(F32)).astype(BF)
            line = jnp.where(head == 1, c[1], s[0, at, :].astype(F32))
            s[0, at, :] = jnp.where(head == 0, c[0], line).astype(BF)
            at = pl.ds(pl.multiple_of(e * T + 16, 16), 16)
            s[1, at, :] = jnp.where(head == 15, c[2], s[1, at, :].astype(F32)).astype(BF)
            line = jnp.where(head == 14, c[2], s[2, at, :].astype(F32))
            s[2, at, :] = jnp.where(head == 15, c[3], line).astype(BF)

    def of_row(res, t):
        at = (0, 1, T, T + 1)[t]
        return res[at : at + 1]

    def outer(s, back):
        return jnp.concatenate([window(s, back, 0, 2), window(s, back, 32, 2)], axis=0)

    res = dot(outer(sx, False), w1[...])
    pre1[0 : 2 * T, :] = res[: 2 * T]
    pre1[32 * T : 34 * T, :] = res[2 * T :]
    strips(zx, w1, False, zp)

    def activate_strips():
        for t in range(4):
            act, slp = gelu_parts(zp[t])
            zh[t] = act * kz[t]
            zs[t] = slp * kz[t]

    def activate(e, mask):
        act, slp = gelu_parts(pre1[rows(e - 1), :])
        slope[rows(e - 1), :] = slp * mask
        spread(sh, zh[0, pl.ds(e, 1), :], zh[3, pl.ds(e, 1), :], e, act * mask)

    activate_strips()
    activate(1, halo_ns[0, 4 * T :, :].astype(F32))
    activate(2, jnp.where(jnp.zeros((T, C), jnp.int32) < live, 1.0, 0.0))
    activate(33, keep_last)
    activate(34, halo_ns[1, 4 * T :, :].astype(F32))

    res = dot(outer(sd, True), wt2[...])
    back2[0 : 2 * T, :] = res[: 2 * T]
    back2[32 * T : 34 * T, :] = res[2 * T :]
    strips(zd, wt2, True, zq)

    def scale_strips():
        for t in range(4):
            zg[t] = zq[t] * zs[t]

    def scale(e):
        line = back2[rows(e - 1), :] * slope[rows(e - 1), :]
        spread(sg, zg[0, pl.ds(e, 1), :], zg[3, pl.ds(e, 1), :], e, line)

    scale_strips()
    for e in (1, 2, 33, 34):
        scale(e)

    @pl.when(rim_tile)
    def _():
        drain(arrived.at[pl.ds(0, 3)], pbr_sem)
        drain(arrived.at[pl.ds(0, 3)], pbs_sem)
        arrived[x] = picked[x]
        total = arrived[0].astype(F32)
        for k in range(1, 4):
            total = total + arrived[k].astype(F32)
        halo_ns[side] = total[:MSG].astype(BF)
        halo_dg[2 * side] = total[MSG : MSG + 16].astype(BF)
        halo_dg[2 * side + 1] = total[MSG + 16 :].astype(BF)
        place(side)
        for n, e in enumerate((e_out, e_ring, e_edge, e_in)):
            extend(n, sx, (zx.at[0], zx.at[1]), (zx.at[6], zx.at[7]), e)
        pre = jnp.zeros((2 * STRIP, C), F32)
        for pair_of, row in (((straight(2), turned(1)), far), ((straight(1), turned(2)), 1), ((straight(0), turned(3)), 2 - far)):
            pre = pre + dot(jnp.concatenate(pair_of, axis=0), taps(w1, row))
        for k, e in enumerate((e_ring, e_edge)):
            pre1[rows(e - 1), :] = pre[k * STRIP + 1 : k * STRIP + 1 + T]
            for t in range(4):
                zp[t, pl.ds(e, 1), :] = of_row(pre[k * STRIP : (k + 1) * STRIP], t)
        activate_strips()
        activate(e_ring, halo_ns[side, 4 * T :, :].astype(F32))
        activate(e_edge, jnp.where(jnp.full((T, C), e_edge - 2, jnp.int32) < live, 1.0, 0.0))

        for n, e in enumerate((e_out, e_ring, e_edge, e_in)):
            extend(n, sd, (zd.at[0], zd.at[1]), (zd.at[6], zd.at[7]), e)
        back = dot(jnp.concatenate([turned(0), turned(1)], axis=0), taps(wt2, far))
        back = back + dot(jnp.concatenate([straight(2), straight(3)], axis=0), taps(wt2, far))
        back = back + dot(jnp.concatenate([turned(1), straight(2)], axis=0), taps(wt2, 1))
        for k, e in enumerate((e_ring, e_edge)):
            back2[rows(e - 1), :] = back[k * STRIP + 1 : k * STRIP + 1 + T]
            for t in range(4):
                zq[t, pl.ds(e, 1), :] = of_row(back[k * STRIP : (k + 1) * STRIP], t)
        scale_strips()
        scale(e_ring)
        scale(e_edge)

    sibling = {"lon": u + 1 - 2 * core, "lat": v}

    def pair(g, a):
        return remote(gsend.at[g, a], gpair.at[g, a], s1_sem.at[g, a], r1_sem.at[g, a], sibling)

    def add_pair(g, a):
        pair(g, a).wait()
        total = gkeep[g, a] + gpair[g, a].astype(F32)
        gsum[g, 3 * a : 3 * a + 3] = total.astype(BF).reshape(3, 4, 4, 16, C // 2)

    def first_axis(g):
        for d in range(1, 4):
            to = lax.rem(x + d, 4)
            remote(gsum.at[g, pl.ds(0, 5), to], px1.at[g, x], s2_sem.at[g, 0], r2_sem.at[g, 0], along_x(d)).start()
            to = lax.rem(y + d, 4)
            remote(gsum.at[g, pl.ds(5, 4), :, to], py1.at[g, y], s2_sem.at[g, 1], r2_sem.at[g, 1], along_y(d)).start()

    def total_of(ref, g):
        total = ref[g, 0].astype(F32)
        for k in range(1, 4):
            total = total + ref[g, k].astype(F32)
        return total.astype(BF)

    def second_axis(g):
        drain(px1.at[g, pl.ds(0, 3)], r2_sem.at[g, 0])
        px1[g, x] = gsum[g, 0:5, x]
        sx1[g] = total_of(px1, g)
        for d in range(1, 4):
            to = lax.rem(y + d, 4)
            remote(sx1.at[g, :, to], py2.at[g, y], s2_sem.at[g, 2], r2_sem.at[g, 2], along_y(d)).start()
        drain(py1.at[g, pl.ds(0, 3)], r2_sem.at[g, 1])
        py1[g, y] = gsum[g, 5:9, :, y]
        sy1[g] = total_of(py1, g)
        for d in range(1, 4):
            to = lax.rem(x + d, 4)
            remote(sy1.at[g, :, to], px2.at[g, x], s2_sem.at[g, 3], r2_sem.at[g, 3], along_x(d)).start()

    def plane_total(g):
        drain(py2.at[g, pl.ds(0, 3)], r2_sem.at[g, 2])
        py2[g, y] = sx1[g, :, y]
        tiles[g, 0:5] = total_of(py2, g)
        drain(px2.at[g, pl.ds(0, 3)], r2_sem.at[g, 3])
        px2[g, x] = sy1[g, :, x]
        tiles[g, 5:9] = total_of(px2, g)

    def column(ref, t, first, mask):
        return jnp.where(mask, ref[t, first : first + T, :], 0.0).astype(BF)

    def left_side(pieces):
        return jnp.concatenate([jnp.concatenate(p, axis=0).T for p in pieces], axis=0)

    def finish_grad(g, left, rights):
        for a, right in enumerate(rights):
            res = gm[g, a] + dot(left, jnp.concatenate(right, axis=0))
            lo, hi = res[:, : C // 2], res[:, C // 2 :]
            gkeep[g, a] = jnp.where(core == 0, lo, hi).reshape(3, C, C // 2)
            gsend[g, a] = jnp.where(core == 0, hi, lo).astype(BF).reshape(3, C, C // 2)
            pair(g, a).start()

    blank = jnp.zeros((T, C), BF)
    places = ((0, 1, None, None), (1, None, None, 2), (None, None, 2, 3))
    left = left_side(
        [
            [sh[b, T : 3 * T, :], sh[b, 33 * T : 35 * T, :]]
            + [blank if t is None else column(zh, t, 2, inner) for t in places[b]]
            for b in range(3)
        ]
    )
    rights = [
        [dz[(3 - a) * T : (5 - a) * T, :], dz[(35 - a) * T : (37 - a) * T, :]]
        + [zd[2 + q, 3 - a : 35 - a, :].astype(BF) for q in range(4)]
        for a in range(3)
    ]
    finish_grad(0, left, rights)
    left = left_side(
        [
            [sx[b, T : 4 * T, :], sx[b, 32 * T : 35 * T, :]]
            + [zx[t + b, 2 : 2 + T, :].astype(BF) for t in (1, 4)]
            for b in range(3)
        ]
    )
    rights = [
        [sg[1, e * T : (e + 1) * T, :] if k == a else blank for e in (2, 33) for k in range(3)]
        + [column(zg, t, 3 - a, (lane_row >= a) & (lane_row < T - 2 + a)) for t in (1, 2)]
        for a in range(3)
    ]
    finish_grad(1, left, rights)
    for g in range(2):
        for a in range(3):
            add_pair(g, a)
        first_axis(g)

    size = T // 2

    def forward(first):
        row = lax.broadcasted_iota(jnp.int32, (size * T, C), 0) // T + first
        pre = dot(window(sh, False, 1 + first, size), w2[...])
        masked = sx[1, (2 + first) * T : (2 + first + size) * T, :].astype(F32)
        out[first : first + size] = (masked + jnp.where(row < live, pre, 0.0)).astype(BF).reshape(size, T, C)

    put_columns(sh, zh)
    for tap in range(9):
        wt1[tap * C : (tap + 1) * C, :] = w1[tap * C : (tap + 1) * C, :].T
    forward(0)
    forward(size)
    second_axis(0)
    put_columns(sg, zg)

    row = lax.broadcasted_iota(jnp.int32, (T * T, C), 0) // T
    back = dot(window(sg, True, 1, T), wt1[...])
    total = cot[...].reshape(T * T, C).astype(F32) + back
    fgrad[...] = jnp.where(row < live, total, 0.0).astype(BF).reshape(T, T, C)

    @pl.when(rim_tile)
    def _():
        for n, e in ((1, e_ring), (2, e_edge), (3, e_in)):
            extend(n, sg, (zg.at[0],), (zg.at[3],), e)
        w_far, w_mid = taps(wt1, far), taps(wt1, 1)
        rim = dot(turned(1), w_far) + dot(straight(3), w_far) + dot(straight(2), w_mid)
        i = e_edge - 2
        total = cot[i].astype(F32) + rim[1 : 1 + T]
        kept = jnp.full((T, C), i, jnp.int32) < live
        fgrad[i] = jnp.where(kept, total, 0.0).astype(BF)

    second_axis(1)
    plane_total(0)
    plane_total(1)

    def first_tile(plane):
        return lax.div(18 * plane + 15 - spot, 16)

    for d in range(1, PLANES):
        to = lax.rem(z + d, PLANES)
        remote(
            tiles.at[:, pl.ds(first_tile(to), 2)],
            parts3.at[z],
            s3_sem,
            r3_sem,
            {"lon": u, "lat": to * 2 + y_lo},
        ).start()

    mine = first_tile(z)
    drain(parts3.at[pl.ds(0, PLANES - 1)], r3_sem)
    parts3[z] = tiles[:, pl.ds(mine, 2)]
    total = parts3[0].astype(F32)
    for k in range(1, PLANES):
        total = total + parts3[k].astype(F32)
    for slot in range(2):
        own[slot] = total[:, slot].astype(BF)

    def deliver(slot):
        group = (mine + slot) * 16 + spot
        lat, at = lax.div(group, 9), lax.rem(group, 9)
        src, dst = own.at[slot], final.at[core, at]

        def to(d):
            lon = 2 * lax.rem(lax.div(u, 2) + d, 8) + core
            return remote(src, dst, s4_sem.at[2 * slot + (d == 0)], r4_sem, {"lon": lon, "lat": lat})

        for d in range(1, 8):
            to(d).start()

        @pl.when(lat == v)
        def _():
            pltpu.make_async_copy(src, dst, r4_sem).start()

        @pl.when(lat != v)
        def _():
            to(0).start()

    def delivered(slot):
        lat = lax.div((mine + slot) * 16 + spot, 9)
        drain(final.at[0, pl.ds(0, 7)], s4_sem.at[2 * slot])

        @pl.when(lat != v)
        def _():
            drain(final.at[0, 0], s4_sem.at[2 * slot + 1])

    has_two = first_tile(z + 1) - mine == 2
    deliver(0)

    @pl.when(has_two)
    def _():
        deliver(1)

    drain(final.at[core], r4_sem)
    last = remote(final.at[core], final.at[core], s5_sem, r5_sem, sibling)
    last.start()
    for h in range(2):
        @pl.when(core == h)
        def _(h=h):
            sums[h] = final[h]
    delivered(0)

    @pl.when(has_two)
    def _():
        delivered(1)

    last.wait()
    for h in range(2):
        @pl.when(core != h)
        def _(h=h):
            sums[h] = final[h]

    to_west.wait_send()
    to_east.wait_send()

    @pl.when(v > 0)
    def _():
        for copy in to_north:
            copy.wait_send()

    @pl.when(v < LAT - 1)
    def _():
        for copy in to_south:
            copy.wait_send()

    for g in range(2):
        for k, ref in enumerate((px1, py1, py2, px2)):
            drain(ref.at[g, pl.ds(0, 3)], s2_sem.at[g, k])
    drain(parts3.at[pl.ds(0, PLANES - 1)], s3_sem)


def local(field, first_weight, second_weight, cotangent, live_rows, polar_links):
    vmem = pl.BlockSpec(memory_space=pltpu.VMEM)
    smem = pl.BlockSpec(memory_space=pltpu.SMEM)
    anywhere = pl.BlockSpec(memory_space=pl.ANY)
    half = C // 2
    tile = jax.ShapeDtypeStruct((T, T, C), BF)
    share = jax.ShapeDtypeStruct((SHARE, C), F32)
    flat = pltpu.VMEM((3, PX, C), BF)
    columns = pltpu.VMEM((8, STRIP, C), F32)
    four = pltpu.VMEM((4, STRIP, C), F32)
    ringed = pltpu.VMEM((RING * T, C), F32)
    weights = pltpu.VMEM((9 * C, C), BF)
    message = pltpu.VMEM((2, MSG, C), BF)
    corners = pltpu.VMEM((4, 16, C), BF)
    grads = pltpu.VMEM((2, 3, 3, C, half), BF)
    dma = pltpu.SemaphoreType.DMA
    made, back, sums = pl.pallas_call(
        kernel,
        out_shape=(pltpu.VMEM((T, T, C), BF), pltpu.VMEM((T, T, C), BF), pltpu.VMEM((2, 9, 2, 16, half), BF)),
        in_specs=[anywhere, anywhere, anywhere, anywhere, smem, smem],
        out_specs=(vmem, vmem, vmem),
        scratch_shapes=[
            *([flat] * 4),
            *([columns] * 2),
            *([four] * 6),
            pltpu.VMEM((T, T, C), BF),
            pltpu.VMEM((T, T, C), BF),
            pltpu.VMEM((2, 4, T, C), F32),
            pltpu.VMEM((4, 16, C), F32),
            *([ringed] * 3),
            *([pltpu.VMEM((3 * C, PX), BF)] * 2),
            *([pltpu.VMEM((38 * T, C), BF)] * 2),
            pltpu.VMEM((2, 3, 3 * C, C), F32),
            *([weights] * 4),
            pltpu.VMEM((4, 48, C), F32),
            message,
            message,
            corners,
            message,
            message,
            corners,
            pltpu.VMEM((4, MSG, C), BF),
            pltpu.VMEM((4, PICK, C), BF),
            pltpu.VMEM((4, PICK, C), BF),
            pltpu.VMEM((2, 3, 3, C, half), F32),
            grads,
            grads,
            pltpu.VMEM((2, 9, 4, 4, 16, half), BF),
            pltpu.VMEM((2, 4, 5, 4, 16, half), BF),
            pltpu.VMEM((2, 4, 4, 4, 16, half), BF),
            pltpu.VMEM((2, 5, 4, 16, half), BF),
            pltpu.VMEM((2, 4, 4, 16, half), BF),
            pltpu.VMEM((2, 4, 5, 16, half), BF),
            pltpu.VMEM((2, 4, 4, 16, half), BF),
            pltpu.VMEM((2, 10, 16, half), BF),
            pltpu.VMEM((PLANES, 2, 2, 16, half), BF),
            pltpu.VMEM((2, 2, 16, half), BF),
            pltpu.VMEM((2, 9, 2, 16, half), BF),
            dma((4,)),
            dma((8,)),
            dma((8,)),
            dma,
            dma,
            dma,
            dma,
            dma((2, 3)),
            dma((2, 3)),
            dma((2, 4)),
            dma((2, 4)),
            dma,
            dma,
            dma((4,)),
            dma,
            dma,
            dma,
        ],
        compiler_params=pltpu.CompilerParams(
            collective_id=0, has_side_effects=True, vmem_limit_bytes=56 * 1024 * 1024
        ),
        cost_estimate=pl.CostEstimate(
            flops=12 * T * T * 9 * C * C, bytes_accessed=6_000_000, transcendentals=2 * T * T * C
        ),
    )(field, first_weight, second_weight, cotangent, live_rows, polar_links)
    made, back, sums = (pltpu.with_memory_space_constraint(r, pltpu.VMEM) for r in (made, back, sums))
    return pl.pallas_call(
        finish,
        out_shape=(tile, tile, share, share),
        in_specs=[vmem] * 3,
        out_specs=(anywhere,) * 4,
        scratch_shapes=[pltpu.VMEM((SHARE, C), F32), pltpu.VMEM((SHARE, C), F32), dma((4,))],
        compiler_params=pltpu.CompilerParams(vmem_limit_bytes=4 * 1024 * 1024),
        cost_estimate=pl.CostEstimate(flops=2 * SHARE * C, bytes_accessed=3_000_000, transcendentals=0),
    )(made, back, sums)


def solution(mesh):
    in_specs = (P("lat", "lon", None), P(), P(), P("lat", "lon", None), P("lon", "lat"), P())
    out_specs = (P("lat", "lon", None), P("lat", "lon", None), P("lat", None), P("lat", None))
    return jax.shard_map(local, mesh=mesh, in_specs=in_specs, out_specs=out_specs, check_vma=False)
```

```python
import math

import jax
import jax.numpy as jnp
from jax import lax
from jax.experimental import pallas as pl
from jax.experimental.pallas import tpu as pltpu
from jax.sharding import PartitionSpec as P

MESH = pl.DeviceIdType.MESH
BF = jnp.bfloat16
F32 = jnp.float32
C = 256
T = 32
EXT = T + 4
PX = EXT * T
RING = T + 2
MSG = 5 * T
STRIP = 40
LON = 16
LAT = 16
PLANES = 8
SHARE = 3 * T // 2 * 3
XT = 3
PICK = MSG + T


def dot(a, b):
    return jnp.dot(a, b, preferred_element_type=F32)


def gelu_parts(pre):
    cdf = 0.5 * (1.0 + lax.erf(pre * 0.7071067811865476))
    dens = jnp.exp(-0.5 * pre * pre) * 0.3989422804014327
    return (pre * cdf, cdf + pre * dens)


def rows(start, size=T):
    return pl.ds(pl.multiple_of(start * T, T), size)


def finish(made, back, sums, out, fgrad, grad1, grad2, share1, share2, sem):
    copies = [pltpu.make_async_copy(made, out, sem.at[0]), pltpu.make_async_copy(back, fgrad, sem.at[1])]
    for copy in copies:
        copy.start()
    scale = 1.0 / math.sqrt(LON * T * LAT * T)
    for g, (ref, dst) in enumerate(((share2, grad2), (share1, grad1))):
        for k in range(9):
            for h in range(2):
                ref[k * 16 : (k + 1) * 16, h * 128 : (h + 1) * 128] = sums[h, k, g].astype(F32) * scale
        copies.append(pltpu.make_async_copy(ref, dst, sem.at[2 + g]))
        copies[-1].start()
    for copy in copies:
        copy.wait()


def kernel(
    field_hbm,
    w1_hbm,
    w2_hbm,
    cot_hbm,
    live_ref,
    links,
    out,
    fgrad,
    sums,
    sx,
    sd,
    sh,
    sg,
    zx,
    zd,
    zh,
    zg,
    zs,
    zp,
    zq,
    kz,
    field,
    cot,
    cols,
    corner,
    pre1,
    back2,
    slope,
    xt,
    xth,
    dz,
    dzg,
    gm,
    w1,
    w2,
    wt1,
    wt2,
    ext,
    send_ns,
    send_ew,
    send_dg,
    halo_ns,
    halo_ew,
    halo_dg,
    near,
    picked,
    arrived,
    gkeep,
    gsend,
    gpair,
    gsum,
    px1,
    py1,
    sx1,
    sy1,
    py2,
    px2,
    tiles,
    parts3,
    own,
    final,
    w_sem,
    hs_sem,
    hr_sem,
    pas_sem,
    par_sem,
    pbs_sem,
    pbr_sem,
    s1_sem,
    r1_sem,
    s2_sem,
    r2_sem,
    s3_sem,
    r3_sem,
    s4_sem,
    r4_sem,
    s5_sem,
    r5_sem,
):
    u, v = lax.axis_index("lon"), lax.axis_index("lat")
    core, x, z = lax.rem(u, 2), lax.div(u, 4), lax.div(v, 2)
    low = lax.rem(u, 4)
    y_lo = lax.rem(v, 2)
    y = lax.div(low, 2) * 2 + y_lo
    spot = x * 4 + y
    north, south = v == 0, v == LAT - 1
    rim_tile = north | south
    side = jnp.where(south, 1, 0)
    live = live_ref[0, 0]
    east, west = lax.rem(u + 1, LON), lax.rem(u + LON - 1, LON)

    def in_plane(place):
        px, py = lax.div(place, 4), lax.rem(place, 4)
        return {"lon": px * 4 + lax.div(py, 2) * 2 + core, "lat": z * 2 + lax.rem(py, 2)}

    def along_x(d):
        return in_plane(lax.rem(x + d, 4) * 4 + y)

    def along_y(d):
        return in_plane(x * 4 + lax.rem(y + d, 4))

    def quarter(d):
        return x * 4 + lax.rem(low + d, 4)

    fetched = [
        pltpu.make_async_copy(src, dst, w_sem.at[n])
        for n, (src, dst) in enumerate(((field_hbm, field), (cot_hbm, cot), (w1_hbm, w1), (w2_hbm, w2)))
    ]
    for copy in fetched:
        copy.start()

    barrier = pltpu.get_barrier_semaphore()

    def greet(lon, lat):
        pl.semaphore_signal(barrier, inc=1, device_id={"lon": lon, "lat": lat}, device_id_type=MESH)

    @pl.when(rim_tile)
    def _():
        for d in range(1, 4):
            greet(quarter(d), v)
            greet(lax.rem(u + 4 * d, LON), v)

    greet(east, v)
    greet(west, v)

    @pl.when(v > 0)
    def _():
        for lon in (west, u, east):
            greet(lon, v - 1)

    @pl.when(v < LAT - 1)
    def _():
        for lon in (west, u, east):
            greet(lon, v + 1)

    for d in range(1, 4):
        for to in (along_x(d), along_y(d)):
            greet(to["lon"], to["lat"])

    @pl.loop(1, PLANES)
    def _(d):
        greet(u, lax.rem(z + d, PLANES) * 2 + y_lo)

    lane_row = lax.broadcasted_iota(jnp.int32, (T, C), 0)
    fetched[0].wait()
    fetched[1].wait()

    @pl.loop(0, T, unroll=4)
    def _(i):
        kept = jnp.full((T, C), i, jnp.int32) < live
        for k, (src, dst) in enumerate(((field, sx), (cot, sd))):
            line = jnp.where(kept, src[i].astype(F32), 0.0)
            dst[1, rows(i + 2), :] = line.astype(BF)
            for n, col in enumerate((0, 1, T - 2, T - 1)):
                cols[k, n, pl.ds(i, 1), :] = line[col : col + 1]

    keep_col = jnp.where(lane_row < live, 1.0, 0.0)
    keep_last = jnp.where(jnp.full((T, C), T - 1, jnp.int32) < live, 1.0, 0.0)
    for s in range(2):
        for k, src in enumerate((sx, sd)):
            first = 2 if s == 0 else T
            send_ns[s, 2 * k * T : (2 * k + 2) * T, :] = src[1, first * T : (first + 2) * T, :]
            for n in range(2):
                send_ew[s, (2 * k + n) * T : (2 * k + n + 1) * T, :] = cols[k, 2 * s + n].astype(BF)
        send_ns[s, 4 * T :, :] = jnp.ones((T, C), BF) if s == 0 else keep_last.astype(BF)
        send_ew[s, 4 * T :, :] = keep_col.astype(BF)
    corner[...] = jnp.zeros_like(corner)
    for s in range(2):
        for t in range(2):
            for k in range(2):
                for r in range(2):
                    for n in range(2):
                        at = 4 * k + 2 * r + n
                        line = (0 if s == 0 else T - 2) + r
                        corner[2 * s + t, at : at + 1, :] = cols[k, 2 * t + n, line : line + 1, :]
            corner[2 * s + t, 8:9, :] = jnp.ones((1, C), F32) if s == 0 else keep_last[0:1]
    send_dg[...] = corner[...].astype(BF)

    here = jnp.where(v > 0, 3, 0) + jnp.where(v < LAT - 1, 3, 0) + jnp.where(rim_tile, 6, 0)
    pl.semaphore_wait(barrier, here + 2 + 6 + 7)

    def remote(src, dst, send, recv, to):
        return pltpu.make_async_remote_copy(
            src_ref=src, dst_ref=dst, send_sem=send, recv_sem=recv, device_id=to, device_id_type=MESH
        )

    def drain(ref, sem):
        pltpu.make_async_copy(ref, ref, sem).wait()

    def edge(src, dst, n, lon, lat):
        return remote(src, dst, hs_sem.at[n], hr_sem.at[n], {"lon": lon, "lat": lat})

    @pl.when(rim_tile)
    def _():
        for d in range(1, 4):
            remote(send_ns.at[side], near.at[low], pas_sem, par_sem, {"lon": quarter(d), "lat": v}).start()

    to_west = edge(send_ew.at[0], halo_ew.at[1], 0, west, v)
    to_east = edge(send_ew.at[1], halo_ew.at[0], 1, east, v)
    to_north = [
        edge(send_ns.at[0], halo_ns.at[1], 2, u, v - 1),
        edge(send_dg.at[0], halo_dg.at[3], 3, west, v - 1),
        edge(send_dg.at[1], halo_dg.at[2], 4, east, v - 1),
    ]
    to_south = [
        edge(send_ns.at[1], halo_ns.at[0], 5, u, v + 1),
        edge(send_dg.at[2], halo_dg.at[1], 6, west, v + 1),
        edge(send_dg.at[3], halo_dg.at[0], 7, east, v + 1),
    ]

    to_west.start()
    to_east.start()

    @pl.when(v > 0)
    def _():
        for copy in to_north:
            copy.start()

    @pl.when(v < LAT - 1)
    def _():
        for copy in to_south:
            copy.start()

    @pl.loop(2, 34, unroll=4)
    def _(e):
        at = rows(e)
        for s in (sx, sd):
            line = s[1, at, :].astype(F32)
            s[0, at, :] = jnp.where(lane_row == 0, 0.0, pltpu.roll(line, 1, 0)).astype(BF)
            s[2, at, :] = jnp.where(lane_row == T - 1, 0.0, pltpu.roll(line, T - 1, 0)).astype(BF)

    for ref in (zx, zd, zh, zg, zs, zp, zq, ext, kz):
        ref[...] = jnp.zeros_like(ref)
    for b in range(3):
        for first, last in ((0, 3), (33, EXT)):
            sh[b, first * T : last * T, :] = jnp.zeros(((last - first) * T, C), BF)
        for first, last in ((0, 2), (34, EXT)):
            sx[b, first * T : last * T, :] = jnp.zeros(((last - first) * T, C), BF)
    for ref in (dz, dzg):
        ref[0 : 4 * T, :] = jnp.zeros((4 * T, C), BF)
        ref[34 * T : 38 * T, :] = jnp.zeros((4 * T, C), BF)

    @pl.when(rim_tile)
    def _():
        halo_ns[side] = jnp.zeros((MSG, C), BF)
        for t in range(2):
            halo_dg[2 * side + t] = jnp.zeros((16, C), BF)

    dz[3 * T : 35 * T, :] = sd[1, 2 * T : 34 * T, :]
    tiles[:, 9] = jnp.zeros((2, 16, C // 2), BF)

    def window(s, back, first, size):
        pieces = []
        for a in range(3):
            for b in range(3):
                start = (first + (2 - a if back else a)) * T
                pieces.append(s[2 - b if back else b, start : start + size * T, :])
        return jnp.concatenate(pieces, axis=1)

    def spread(s, left, right, e, line):
        at = rows(e)
        s[1, at, :] = line.astype(BF)
        s[0, at, :] = jnp.where(lane_row == 0, left, pltpu.roll(line, 1, 0)).astype(BF)
        s[2, at, :] = jnp.where(lane_row == T - 1, right, pltpu.roll(line, T - 1, 0)).astype(BF)

    def transposed(s, ref):
        for k in range(PX // 128):
            for b in range(3):
                ref[b * C : (b + 1) * C, k * 128 : (k + 1) * 128] = s[b, k * 128 : (k + 1) * 128, :].T

    inner = (lane_row > 0) & (lane_row < T - 1)

    fetched[2].wait()
    fetched[3].wait()
    pre1[2 * T : 32 * T, :] = dot(window(sx, False, 2, 30), w1[...])
    for tap in range(9):
        wt2[tap * C : (tap + 1) * C, :] = w2[tap * C : (tap + 1) * C, :].T
    transposed(sx, xt)
    back2[2 * T : 32 * T, :] = dot(window(sd, True, 2, 30), wt2[...])
    for e in range(3, 33):
        act, slp = gelu_parts(pre1[rows(e - 1), :])
        mask = jnp.where((jnp.full((T, C), e - 2, jnp.int32) < live) & inner, 1.0, 0.0)
        slope[rows(e - 1), :] = slp * mask
        spread(sh, 0.0, 0.0, e, act * mask)

    @pl.when(rim_tile)
    def _():
        drain(near.at[pl.ds(0, 3)], par_sem)
        drain(near.at[pl.ds(0, 3)], pas_sem)
        near[low] = send_ns[side]
        pivot = links[side, 0]
        n = lax.broadcasted_iota(jnp.int32, (8 * T, 4 * T), 0)
        at = lax.broadcasted_iota(jnp.int32, (8 * T, 4 * T), 1) + x * (4 * T)
        to = (n // (2 * T)) * 4 + low
        n = n & (2 * T - 1)
        q = n & 15
        in_east = n >= T + 16
        ring_col = jnp.where(in_east, T, -1)
        outer_col = jnp.where(in_east, T, -2) + (q & 1)
        col = jnp.where(n < T, n, jnp.where(q == 8, ring_col, outer_col))
        hit = ((pivot - to * T - col) & (LON * T - 1)) == at
        line = jnp.where(q == 8, 4, jnp.where(q < 8, q // 2, 5))
        corners = jnp.zeros((4, T, C), F32)
        for part in range(5):
            target = part if part == 4 else part ^ 1
            pick = jnp.where(hit & ((n < T) | (line == target)), 1.0, 0.0).astype(BF)
            lines = near[:, part * T : (part + 1) * T, :].reshape(4 * T, C)
            found = dot(pick, lines).reshape(4, 2 * T, C)
            picked[:, target * T : (target + 1) * T, :] = found[:, :T].astype(BF)
            corners = corners + found[:, T:]
        picked[:, MSG:, :] = corners.astype(BF)
        for d in range(1, 4):
            to = lax.rem(x + d, 4)
            remote(picked.at[to], arrived.at[x], pbs_sem, pbr_sem, {"lon": lax.rem(u + 4 * d, LON), "lat": v}).start()

    @pl.loop(3, 33, unroll=3)
    def _(e):
        spread(sg, 0.0, 0.0, e, back2[rows(e - 1), :] * slope[rows(e - 1), :])

    dzg[4 * T : 34 * T, :] = sg[1, 3 * T : 33 * T, :]
    transposed(sh, xth)
    for g, left, right in ((1, xt, dzg), (0, xth, dz)):
        for a in range(3):
            gm[g, a] = dot(left[...], right[(2 - a) * T : (2 - a) * T + PX, :])

    to_west.wait_recv()
    to_east.wait_recv()

    @pl.when(v > 0)
    def _():
        for copy in to_south:
            copy.wait_recv()

    @pl.when(v < LAT - 1)
    def _():
        for copy in to_north:
            copy.wait_recv()

    head = lax.broadcasted_iota(jnp.int32, (16, C), 0)

    def place(h):
        for k, (s, zz) in enumerate(((sx, zx), (sd, zd))):
            for t in range(2):
                px = halo_dg[2 * h + t].astype(F32)
                for r in range(2):
                    for n in range(2):
                        at = 4 * k + 2 * r + n
                        zz[t * 6 + n, pl.ds(34 * h + r, 1), :] = px[at : at + 1]
            for r in range(2):
                e = 34 * h + r
                line = halo_ns[h, (2 * k + r) * T : (2 * k + r + 1) * T, :].astype(F32)
                spread(s, zz[1, pl.ds(e, 1), :], zz[6, pl.ds(e, 1), :], e, line)
                for n, col in enumerate((0, 1, T - 2, T - 1)):
                    zz[2 + n, pl.ds(e, 1), :] = line[col : col + 1]
        mask = halo_ns[h, 4 * T :, :].astype(F32)
        e = 33 * h + 1
        for t in range(2):
            kz[3 * t, pl.ds(e, 1), :] = halo_dg[2 * h + t].astype(F32)[8:9]
            kz[1 + t, pl.ds(e, 1), :] = mask[t * (T - 1) : t * (T - 1) + 1]

    for k, zz in enumerate((zx, zd)):
        for n in range(2):
            zz[n, 2 : 2 + T, :] = halo_ew[0, (2 * k + n) * T : (2 * k + n + 1) * T, :].astype(F32)
            zz[6 + n, 2 : 2 + T, :] = halo_ew[1, (2 * k + n) * T : (2 * k + n + 1) * T, :].astype(F32)
            zz[2 + n, 2 : 2 + T, :] = cols[k, n]
            zz[4 + n, 2 : 2 + T, :] = cols[k, 2 + n]
    for t in range(2):
        kz[3 * t, 2 : 2 + T, :] = halo_ew[t, 4 * T :, :].astype(F32)
        kz[1 + t, 2 : 2 + T, :] = keep_col
    place(0)
    place(1)

    def insert(s, zz, e):
        at = pl.ds(pl.multiple_of(e * T, T), 16)
        s[0, at, :] = jnp.where(head == 0, zz[1, pl.ds(e, 1), :], s[0, at, :].astype(F32)).astype(BF)
        at = pl.ds(pl.multiple_of(e * T + 16, 16), 16)
        s[2, at, :] = jnp.where(head == 15, zz[6, pl.ds(e, 1), :], s[2, at, :].astype(F32)).astype(BF)

    for e in (2, 3, 32, 33):
        insert(sx, zx, e)
        insert(sd, zd, e)

    e_out, e_ring = jnp.where(south, 35, 0), jnp.where(south, 34, 1)
    e_edge, e_in = jnp.where(south, 33, 2), jnp.where(south, 32, 3)
    far = jnp.where(south, 2, 0)

    def extend(n, s, left, right, e):
        ext[n, 2 : 2 + T, :] = s[1, rows(e), :].astype(F32)
        for k, ref in enumerate(left):
            at = 2 - len(left) + k
            ext[n, at : at + 1, :] = ref[pl.ds(e, 1), :]
        for k, ref in enumerate(right):
            ext[n, 34 + k : 35 + k, :] = ref[pl.ds(e, 1), :]

    def straight(n):
        return jnp.concatenate([ext[n, 2 - b : 42 - b, :] for b in range(3)], axis=1).astype(BF)

    def turned(n):
        return jnp.concatenate([ext[n, b : b + 40, :] for b in range(3)], axis=1).astype(BF)

    def taps(w, row):
        return w[pl.ds(pl.multiple_of(row * 3 * C, 3 * C), 3 * C), :]

    def combine(up, mid, down, back):
        if back:
            up, down = down, up
        return pltpu.roll(up, 1, 0) + mid + pltpu.roll(down, mid.shape[0] - 1, 0)

    def strips(zz, w, back, ref):
        order = (2, 1, 0) if back else (0, 1, 2)
        lines = jnp.concatenate(
            [jnp.concatenate([zz[first + b] for b in order], axis=1) for first in (0, 1, 4, 5)], axis=0
        ).astype(BF)
        res = combine(*(dot(lines, w[a * 3 * C : (a + 1) * 3 * C, :]) for a in range(3)), back)
        for t in range(4):
            ref[t] = res[t * STRIP : (t + 1) * STRIP]

    def put_columns(s, zz):
        @pl.loop(3, 33, unroll=3)
        def _(e):
            c = [zz[t, pl.ds(e, 1), :] for t in range(4)]
            at = pl.ds(pl.multiple_of(e * T, T), 16)
            s[1, at, :] = jnp.where(head == 0, c[1], s[1, at, :].astype(F32)).astype(BF)
            line = jnp.where(head == 1, c[1], s[0, at, :].astype(F32))
            s[0, at, :] = jnp.where(head == 0, c[0], line).astype(BF)
            at = pl.ds(pl.multiple_of(e * T + 16, 16), 16)
            s[1, at, :] = jnp.where(head == 15, c[2], s[1, at, :].astype(F32)).astype(BF)
            line = jnp.where(head == 14, c[2], s[2, at, :].astype(F32))
            s[2, at, :] = jnp.where(head == 15, c[3], line).astype(BF)

    def of_row(res, t):
        at = (0, 1, T, T + 1)[t]
        return res[at : at + 1]

    def outer(s, back):
        return jnp.concatenate([window(s, back, 0, 2), window(s, back, 32, 2)], axis=0)

    res = dot(outer(sx, False), w1[...])
    pre1[0 : 2 * T, :] = res[: 2 * T]
    pre1[32 * T : 34 * T, :] = res[2 * T :]
    strips(zx, w1, False, zp)

    def activate_strips():
        for t in range(4):
            act, slp = gelu_parts(zp[t])
            zh[t] = act * kz[t]
            zs[t] = slp * kz[t]

    def activate(e, mask):
        act, slp = gelu_parts(pre1[rows(e - 1), :])
        slope[rows(e - 1), :] = slp * mask
        spread(sh, zh[0, pl.ds(e, 1), :], zh[3, pl.ds(e, 1), :], e, act * mask)

    activate_strips()
    activate(1, halo_ns[0, 4 * T :, :].astype(F32))
    activate(2, jnp.where(jnp.zeros((T, C), jnp.int32) < live, 1.0, 0.0))
    activate(33, keep_last)
    activate(34, halo_ns[1, 4 * T :, :].astype(F32))

    res = dot(outer(sd, True), wt2[...])
    back2[0 : 2 * T, :] = res[: 2 * T]
    back2[32 * T : 34 * T, :] = res[2 * T :]
    strips(zd, wt2, True, zq)

    def scale_strips():
        for t in range(4):
            zg[t] = zq[t] * zs[t]

    def scale(e):
        line = back2[rows(e - 1), :] * slope[rows(e - 1), :]
        spread(sg, zg[0, pl.ds(e, 1), :], zg[3, pl.ds(e, 1), :], e, line)

    scale_strips()
    for e in (1, 2, 33, 34):
        scale(e)

    @pl.when(rim_tile)
    def _():
        drain(arrived.at[pl.ds(0, 3)], pbr_sem)
        drain(arrived.at[pl.ds(0, 3)], pbs_sem)
        arrived[x] = picked[x]
        total = arrived[0].astype(F32)
        for k in range(1, 4):
            total = total + arrived[k].astype(F32)
        halo_ns[side] = total[:MSG].astype(BF)
        halo_dg[2 * side] = total[MSG : MSG + 16].astype(BF)
        halo_dg[2 * side + 1] = total[MSG + 16 :].astype(BF)
        place(side)
        for n, e in enumerate((e_out, e_ring, e_edge, e_in)):
            extend(n, sx, (zx.at[0], zx.at[1]), (zx.at[6], zx.at[7]), e)
        pre = jnp.zeros((2 * STRIP, C), F32)
        for pair_of, row in (((straight(2), turned(1)), far), ((straight(1), turned(2)), 1), ((straight(0), turned(3)), 2 - far)):
            pre = pre + dot(jnp.concatenate(pair_of, axis=0), taps(w1, row))
        for k, e in enumerate((e_ring, e_edge)):
            pre1[rows(e - 1), :] = pre[k * STRIP + 1 : k * STRIP + 1 + T]
            for t in range(4):
                zp[t, pl.ds(e, 1), :] = of_row(pre[k * STRIP : (k + 1) * STRIP], t)
        activate_strips()
        activate(e_ring, halo_ns[side, 4 * T :, :].astype(F32))
        activate(e_edge, jnp.where(jnp.full((T, C), e_edge - 2, jnp.int32) < live, 1.0, 0.0))

        for n, e in enumerate((e_out, e_ring, e_edge, e_in)):
            extend(n, sd, (zd.at[0], zd.at[1]), (zd.at[6], zd.at[7]), e)
        back = dot(jnp.concatenate([turned(0), turned(1)], axis=0), taps(wt2, far))
        back = back + dot(jnp.concatenate([straight(2), straight(3)], axis=0), taps(wt2, far))
        back = back + dot(jnp.concatenate([turned(1), straight(2)], axis=0), taps(wt2, 1))
        for k, e in enumerate((e_ring, e_edge)):
            back2[rows(e - 1), :] = back[k * STRIP + 1 : k * STRIP + 1 + T]
            for t in range(4):
                zq[t, pl.ds(e, 1), :] = of_row(back[k * STRIP : (k + 1) * STRIP], t)
        scale_strips()
        scale(e_ring)
        scale(e_edge)

    sibling = {"lon": u + 1 - 2 * core, "lat": v}

    def pair(g, a):
        return remote(gsend.at[g, a], gpair.at[g, a], s1_sem.at[g, a], r1_sem.at[g, a], sibling)

    def add_pair(g, a):
        pair(g, a).wait()
        total = gkeep[g, a] + gpair[g, a].astype(F32)
        gsum[g, 3 * a : 3 * a + 3] = total.astype(BF).reshape(3, 4, 4, 16, C // 2)

    def first_axis(g):
        for d in range(1, 4):
            to = lax.rem(x + d, 4)
            remote(gsum.at[g, pl.ds(0, XT), to], px1.at[g, x], s2_sem.at[g, 0], r2_sem.at[g, 0], along_x(d)).start()
            to = lax.rem(y + d, 4)
            remote(gsum.at[g, pl.ds(XT, 9 - XT), :, to], py1.at[g, y], s2_sem.at[g, 1], r2_sem.at[g, 1], along_y(d)).start()

    def total_of(ref, g):
        total = ref[g, 0].astype(F32)
        for k in range(1, 4):
            total = total + ref[g, k].astype(F32)
        return total.astype(BF)

    def second_axis(g):
        drain(px1.at[g, pl.ds(0, 3)], r2_sem.at[g, 0])
        px1[g, x] = gsum[g, 0:XT, x]
        sx1[g] = total_of(px1, g)
        for d in range(1, 4):
            to = lax.rem(y + d, 4)
            remote(sx1.at[g, :, to], py2.at[g, y], s2_sem.at[g, 2], r2_sem.at[g, 2], along_y(d)).start()
        drain(py1.at[g, pl.ds(0, 3)], r2_sem.at[g, 1])
        py1[g, y] = gsum[g, XT:9, :, y]
        sy1[g] = total_of(py1, g)
        for d in range(1, 4):
            to = lax.rem(x + d, 4)
            remote(sy1.at[g, :, to], px2.at[g, x], s2_sem.at[g, 3], r2_sem.at[g, 3], along_x(d)).start()

    def plane_total(g):
        drain(py2.at[g, pl.ds(0, 3)], r2_sem.at[g, 2])
        py2[g, y] = sx1[g, :, y]
        tiles[g, 0:XT] = total_of(py2, g)
        drain(px2.at[g, pl.ds(0, 3)], r2_sem.at[g, 3])
        px2[g, x] = sy1[g, :, x]
        tiles[g, XT:9] = total_of(px2, g)

    def column(ref, t, first, mask):
        return jnp.where(mask, ref[t, first : first + T, :], 0.0).astype(BF)

    def left_side(pieces):
        return jnp.concatenate([jnp.concatenate(p, axis=0).T for p in pieces], axis=0)

    def finish_grad(g, left, rights):
        for a, right in enumerate(rights):
            res = gm[g, a] + dot(left, jnp.concatenate(right, axis=0))
            lo, hi = res[:, : C // 2], res[:, C // 2 :]
            gkeep[g, a] = jnp.where(core == 0, lo, hi).reshape(3, C, C // 2)
            gsend[g, a] = jnp.where(core == 0, hi, lo).astype(BF).reshape(3, C, C // 2)
            pair(g, a).start()

    blank = jnp.zeros((T, C), BF)
    places = ((0, 1, None, None), (1, None, None, 2), (None, None, 2, 3))
    left = left_side(
        [
            [sh[b, T : 3 * T, :], sh[b, 33 * T : 35 * T, :]]
            + [blank if t is None else column(zh, t, 2, inner) for t in places[b]]
            for b in range(3)
        ]
    )
    rights = [
        [dz[(3 - a) * T : (5 - a) * T, :], dz[(35 - a) * T : (37 - a) * T, :]]
        + [zd[2 + q, 3 - a : 35 - a, :].astype(BF) for q in range(4)]
        for a in range(3)
    ]
    finish_grad(0, left, rights)
    left = left_side(
        [
            [sx[b, T : 4 * T, :], sx[b, 32 * T : 35 * T, :]]
            + [zx[t + b, 2 : 2 + T, :].astype(BF) for t in (1, 4)]
            for b in range(3)
        ]
    )
    rights = [
        [sg[1, e * T : (e + 1) * T, :] if k == a else blank for e in (2, 33) for k in range(3)]
        + [column(zg, t, 3 - a, (lane_row >= a) & (lane_row < T - 2 + a)) for t in (1, 2)]
        for a in range(3)
    ]
    finish_grad(1, left, rights)
    for g in range(2):
        for a in range(3):
            add_pair(g, a)
        first_axis(g)

    size = T // 2

    def forward(first):
        row = lax.broadcasted_iota(jnp.int32, (size * T, C), 0) // T + first
        pre = dot(window(sh, False, 1 + first, size), w2[...])
        masked = sx[1, (2 + first) * T : (2 + first + size) * T, :].astype(F32)
        out[first : first + size] = (masked + jnp.where(row < live, pre, 0.0)).astype(BF).reshape(size, T, C)

    put_columns(sh, zh)
    for tap in range(9):
        wt1[tap * C : (tap + 1) * C, :] = w1[tap * C : (tap + 1) * C, :].T
    forward(0)
    forward(size)
    put_columns(sg, zg)

    row = lax.broadcasted_iota(jnp.int32, (T * T, C), 0) // T
    back = dot(window(sg, True, 1, T), wt1[...])
    total = cot[...].reshape(T * T, C).astype(F32) + back
    fgrad[...] = jnp.where(row < live, total, 0.0).astype(BF).reshape(T, T, C)

    @pl.when(rim_tile)
    def _():
        for n, e in ((1, e_ring), (2, e_edge), (3, e_in)):
            extend(n, sg, (zg.at[0],), (zg.at[3],), e)
        w_far, w_mid = taps(wt1, far), taps(wt1, 1)
        rim = dot(turned(1), w_far) + dot(straight(3), w_far) + dot(straight(2), w_mid)
        i = e_edge - 2
        total = cot[i].astype(F32) + rim[1 : 1 + T]
        kept = jnp.full((T, C), i, jnp.int32) < live
        fgrad[i] = jnp.where(kept, total, 0.0).astype(BF)

    second_axis(0)
    second_axis(1)
    plane_total(0)
    plane_total(1)

    def first_tile(plane):
        return lax.div(18 * plane + 15 - spot, 16)

    for d in range(1, PLANES):
        to = lax.rem(z + d, PLANES)
        remote(
            tiles.at[:, pl.ds(first_tile(to), 2)],
            parts3.at[z],
            s3_sem,
            r3_sem,
            {"lon": u, "lat": to * 2 + y_lo},
        ).start()

    mine = first_tile(z)
    drain(parts3.at[pl.ds(0, PLANES - 1)], r3_sem)
    parts3[z] = tiles[:, pl.ds(mine, 2)]
    total = parts3[0].astype(F32)
    for k in range(1, PLANES):
        total = total + parts3[k].astype(F32)
    for slot in range(2):
        own[slot] = total[:, slot].astype(BF)

    def deliver(slot):
        group = (mine + slot) * 16 + spot
        lat, at = lax.div(group, 9), lax.rem(group, 9)
        src, dst = own.at[slot], final.at[core, at]

        def to(d):
            lon = 2 * lax.rem(lax.div(u, 2) + d, 8) + core
            return remote(src, dst, s4_sem.at[2 * slot + (d == 0)], r4_sem, {"lon": lon, "lat": lat})

        for d in range(1, 8):
            to(d).start()

        @pl.when(lat == v)
        def _():
            pltpu.make_async_copy(src, dst, r4_sem).start()

        @pl.when(lat != v)
        def _():
            to(0).start()

    def delivered(slot):
        lat = lax.div((mine + slot) * 16 + spot, 9)
        drain(final.at[0, pl.ds(0, 7)], s4_sem.at[2 * slot])

        @pl.when(lat != v)
        def _():
            drain(final.at[0, 0], s4_sem.at[2 * slot + 1])

    has_two = first_tile(z + 1) - mine == 2
    deliver(0)

    @pl.when(has_two)
    def _():
        deliver(1)

    drain(final.at[core], r4_sem)
    last = remote(final.at[core], final.at[core], s5_sem, r5_sem, sibling)
    last.start()
    for h in range(2):
        @pl.when(core == h)
        def _(h=h):
            sums[h] = final[h]
    delivered(0)

    @pl.when(has_two)
    def _():
        delivered(1)

    last.wait()
    for h in range(2):
        @pl.when(core != h)
        def _(h=h):
            sums[h] = final[h]

    to_west.wait_send()
    to_east.wait_send()

    @pl.when(v > 0)
    def _():
        for copy in to_north:
            copy.wait_send()

    @pl.when(v < LAT - 1)
    def _():
        for copy in to_south:
            copy.wait_send()

    for g in range(2):
        for k, ref in enumerate((px1, py1, py2, px2)):
            drain(ref.at[g, pl.ds(0, 3)], s2_sem.at[g, k])
    drain(parts3.at[pl.ds(0, PLANES - 1)], s3_sem)


def local(field, first_weight, second_weight, cotangent, live_rows, polar_links):
    vmem = pl.BlockSpec(memory_space=pltpu.VMEM)
    smem = pl.BlockSpec(memory_space=pltpu.SMEM)
    anywhere = pl.BlockSpec(memory_space=pl.ANY)
    half = C // 2
    tile = jax.ShapeDtypeStruct((T, T, C), BF)
    share = jax.ShapeDtypeStruct((SHARE, C), F32)
    flat = pltpu.VMEM((3, PX, C), BF)
    columns = pltpu.VMEM((8, STRIP, C), F32)
    four = pltpu.VMEM((4, STRIP, C), F32)
    ringed = pltpu.VMEM((RING * T, C), F32)
    weights = pltpu.VMEM((9 * C, C), BF)
    message = pltpu.VMEM((2, MSG, C), BF)
    corners = pltpu.VMEM((4, 16, C), BF)
    grads = pltpu.VMEM((2, 3, 3, C, half), BF)
    dma = pltpu.SemaphoreType.DMA
    made, back, sums = pl.pallas_call(
        kernel,
        out_shape=(pltpu.VMEM((T, T, C), BF), pltpu.VMEM((T, T, C), BF), pltpu.VMEM((2, 9, 2, 16, half), BF)),
        in_specs=[anywhere, anywhere, anywhere, anywhere, smem, smem],
        out_specs=(vmem, vmem, vmem),
        scratch_shapes=[
            *([flat] * 4),
            *([columns] * 2),
            *([four] * 6),
            pltpu.VMEM((T, T, C), BF),
            pltpu.VMEM((T, T, C), BF),
            pltpu.VMEM((2, 4, T, C), F32),
            pltpu.VMEM((4, 16, C), F32),
            *([ringed] * 3),
            *([pltpu.VMEM((3 * C, PX), BF)] * 2),
            *([pltpu.VMEM((38 * T, C), BF)] * 2),
            pltpu.VMEM((2, 3, 3 * C, C), F32),
            *([weights] * 4),
            pltpu.VMEM((4, 48, C), F32),
            message,
            message,
            corners,
            message,
            message,
            corners,
            pltpu.VMEM((4, MSG, C), BF),
            pltpu.VMEM((4, PICK, C), BF),
            pltpu.VMEM((4, PICK, C), BF),
            pltpu.VMEM((2, 3, 3, C, half), F32),
            grads,
            grads,
            pltpu.VMEM((2, 9, 4, 4, 16, half), BF),
            pltpu.VMEM((2, 4, XT, 4, 16, half), BF),
            pltpu.VMEM((2, 4, 9 - XT, 4, 16, half), BF),
            pltpu.VMEM((2, XT, 4, 16, half), BF),
            pltpu.VMEM((2, 9 - XT, 4, 16, half), BF),
            pltpu.VMEM((2, 4, XT, 16, half), BF),
            pltpu.VMEM((2, 4, 9 - XT, 16, half), BF),
            pltpu.VMEM((2, 10, 16, half), BF),
            pltpu.VMEM((PLANES, 2, 2, 16, half), BF),
            pltpu.VMEM((2, 2, 16, half), BF),
            pltpu.VMEM((2, 9, 2, 16, half), BF),
            dma((4,)),
            dma((8,)),
            dma((8,)),
            dma,
            dma,
            dma,
            dma,
            dma((2, 3)),
            dma((2, 3)),
            dma((2, 4)),
            dma((2, 4)),
            dma,
            dma,
            dma((4,)),
            dma,
            dma,
            dma,
        ],
        compiler_params=pltpu.CompilerParams(
            collective_id=0, has_side_effects=True, vmem_limit_bytes=56 * 1024 * 1024
        ),
        cost_estimate=pl.CostEstimate(
            flops=12 * T * T * 9 * C * C, bytes_accessed=6_000_000, transcendentals=2 * T * T * C
        ),
    )(field, first_weight, second_weight, cotangent, live_rows, polar_links)
    made, back, sums = (pltpu.with_memory_space_constraint(r, pltpu.VMEM) for r in (made, back, sums))
    return pl.pallas_call(
        finish,
        out_shape=(tile, tile, share, share),
        in_specs=[vmem] * 3,
        out_specs=(anywhere,) * 4,
        scratch_shapes=[pltpu.VMEM((SHARE, C), F32), pltpu.VMEM((SHARE, C), F32), dma((4,))],
        compiler_params=pltpu.CompilerParams(vmem_limit_bytes=4 * 1024 * 1024),
        cost_estimate=pl.CostEstimate(flops=2 * SHARE * C, bytes_accessed=3_000_000, transcendentals=0),
    )(made, back, sums)


def solution(mesh):
    in_specs = (P("lat", "lon", None), P(), P(), P("lat", "lon", None), P("lon", "lat"), P())
    out_specs = (P("lat", "lon", None), P("lat", "lon", None), P("lat", None), P("lat", None))
    return jax.shard_map(local, mesh=mesh, in_specs=in_specs, out_specs=out_specs, check_vma=False)
```

```python
import math

import jax
import jax.numpy as jnp
from jax import lax
from jax.experimental import pallas as pl
from jax.experimental.pallas import tpu as pltpu
from jax.sharding import PartitionSpec as P

MESH = pl.DeviceIdType.MESH
BF = jnp.bfloat16
F32 = jnp.float32
C = 256
T = 32
EXT = T + 4
PX = EXT * T
RING = T + 2
MSG = 5 * T
STRIP = 40
LON = 16
LAT = 16
PLANES = 8
SHARE = 3 * T // 2 * 3
XT = (5, 4)
NEAR = 4 * T + 16
PICK = 5 * T


def dot(a, b):
    return jnp.dot(a, b, preferred_element_type=F32)


def gelu_parts(pre):
    cdf = 0.5 * (1.0 + lax.erf(pre * 0.7071067811865476))
    dens = jnp.exp(-0.5 * pre * pre) * 0.3989422804014327
    return (pre * cdf, cdf + pre * dens)


def rows(start, size=T):
    return pl.ds(pl.multiple_of(start * T, T), size)


def finish(made, back, sums, out, fgrad, grad1, grad2, share1, share2, sem):
    copies = [pltpu.make_async_copy(made, out, sem.at[0]), pltpu.make_async_copy(back, fgrad, sem.at[1])]
    for copy in copies:
        copy.start()
    scale = 1.0 / math.sqrt(LON * T * LAT * T)
    for g, (ref, dst) in enumerate(((share2, grad2), (share1, grad1))):
        for k in range(9):
            for h in range(2):
                ref[k * 16 : (k + 1) * 16, h * 128 : (h + 1) * 128] = sums[h, k, g].astype(F32) * scale
        copies.append(pltpu.make_async_copy(ref, dst, sem.at[2 + g]))
        copies[-1].start()
    for copy in copies:
        copy.wait()


def kernel(
    field_hbm,
    w1_hbm,
    w2_hbm,
    cot_hbm,
    live_ref,
    links,
    out,
    fgrad,
    sums,
    sx,
    sd,
    sh,
    sg,
    zx,
    zd,
    zh,
    zg,
    zs,
    zp,
    zq,
    kz,
    field,
    cot,
    cols,
    corner,
    pre1,
    back2,
    slope,
    xt,
    xth,
    dz,
    dzg,
    gm,
    w1,
    w2,
    wt1,
    wt2,
    ext,
    send_ns,
    send_ew,
    send_dg,
    halo_ns,
    halo_ew,
    halo_dg,
    near,
    picked,
    arrived,
    gkeep,
    gsend,
    gpair,
    gsum,
    px1,
    py1,
    sx1,
    sy1,
    py2,
    px2,
    tiles,
    parts3,
    own,
    final,
    w_sem,
    hs_sem,
    hr_sem,
    pas_sem,
    par_sem,
    pbs_sem,
    pbr_sem,
    s1_sem,
    r1_sem,
    s2_sem,
    r2_sem,
    s3_sem,
    r3_sem,
    s4_sem,
    r4_sem,
    s5_sem,
    r5_sem,
):
    u, v = lax.axis_index("lon"), lax.axis_index("lat")
    core, x, z = lax.rem(u, 2), lax.div(u, 4), lax.div(v, 2)
    low = lax.rem(u, 4)
    y_lo = lax.rem(v, 2)
    y = lax.div(low, 2) * 2 + y_lo
    spot = x * 4 + y
    north, south = v == 0, v == LAT - 1
    rim_tile = north | south
    side = jnp.where(south, 1, 0)
    live = live_ref[0, 0]
    east, west = lax.rem(u + 1, LON), lax.rem(u + LON - 1, LON)

    def in_plane(place):
        px, py = lax.div(place, 4), lax.rem(place, 4)
        return {"lon": px * 4 + lax.div(py, 2) * 2 + core, "lat": z * 2 + lax.rem(py, 2)}

    def along_x(d):
        return in_plane(lax.rem(x + d, 4) * 4 + y)

    def along_y(d):
        return in_plane(x * 4 + lax.rem(y + d, 4))

    def quarter(d):
        return x * 4 + lax.rem(low + d, 4)

    fetched = [
        pltpu.make_async_copy(src, dst, w_sem.at[n])
        for n, (src, dst) in enumerate(((field_hbm, field), (cot_hbm, cot), (w1_hbm, w1), (w2_hbm, w2)))
    ]
    for copy in fetched:
        copy.start()

    barrier = pltpu.get_barrier_semaphore()

    def greet(lon, lat):
        pl.semaphore_signal(barrier, inc=1, device_id={"lon": lon, "lat": lat}, device_id_type=MESH)

    @pl.when(rim_tile)
    def _():
        for d in range(1, 4):
            greet(quarter(d), v)
            greet(lax.rem(u + 4 * d, LON), v)

    greet(east, v)
    greet(west, v)

    @pl.when(v > 0)
    def _():
        for lon in (west, u, east):
            greet(lon, v - 1)

    @pl.when(v < LAT - 1)
    def _():
        for lon in (west, u, east):
            greet(lon, v + 1)

    for d in range(1, 4):
        for to in (along_x(d), along_y(d)):
            greet(to["lon"], to["lat"])

    @pl.loop(1, PLANES)
    def _(d):
        greet(u, lax.rem(z + d, PLANES) * 2 + y_lo)

    lane_row = lax.broadcasted_iota(jnp.int32, (T, C), 0)
    fetched[0].wait()
    fetched[1].wait()

    @pl.loop(0, T, unroll=4)
    def _(i):
        kept = jnp.full((T, C), i, jnp.int32) < live
        for k, (src, dst) in enumerate(((field, sx), (cot, sd))):
            line = jnp.where(kept, src[i].astype(F32), 0.0)
            dst[1, rows(i + 2), :] = line.astype(BF)
            for n, col in enumerate((0, 1, T - 2, T - 1)):
                cols[k, n, pl.ds(i, 1), :] = line[col : col + 1]

    keep_col = jnp.where(lane_row < live, 1.0, 0.0)
    keep_last = jnp.where(jnp.full((T, C), T - 1, jnp.int32) < live, 1.0, 0.0)
    for s in range(2):
        for k, src in enumerate((sx, sd)):
            first = 2 if s == 0 else T
            send_ns[s, 2 * k * T : (2 * k + 2) * T, :] = src[1, first * T : (first + 2) * T, :]
            for n in range(2):
                send_ew[s, (2 * k + n) * T : (2 * k + n + 1) * T, :] = cols[k, 2 * s + n].astype(BF)
        send_ns[s, 4 * T :, :] = jnp.ones((T, C), BF) if s == 0 else keep_last.astype(BF)
        send_ew[s, 4 * T :, :] = keep_col.astype(BF)
    corner[...] = jnp.zeros_like(corner)
    for s in range(2):
        for t in range(2):
            for k in range(2):
                for r in range(2):
                    for n in range(2):
                        at = 4 * k + 2 * r + n
                        line = (0 if s == 0 else T - 2) + r
                        corner[2 * s + t, at : at + 1, :] = cols[k, 2 * t + n, line : line + 1, :]
            corner[2 * s + t, 8:9, :] = jnp.ones((1, C), F32) if s == 0 else keep_last[0:1]
    send_dg[...] = corner[...].astype(BF)

    here = jnp.where(v > 0, 3, 0) + jnp.where(v < LAT - 1, 3, 0) + jnp.where(rim_tile, 6, 0)
    pl.semaphore_wait(barrier, here + 2 + 6 + 7)

    def remote(src, dst, send, recv, to):
        return pltpu.make_async_remote_copy(
            src_ref=src, dst_ref=dst, send_sem=send, recv_sem=recv, device_id=to, device_id_type=MESH
        )

    def drain(ref, sem):
        pltpu.make_async_copy(ref, ref, sem).wait()

    def edge(src, dst, n, lon, lat):
        return remote(src, dst, hs_sem.at[n], hr_sem.at[n], {"lon": lon, "lat": lat})

    @pl.when(rim_tile)
    def _():
        for d in range(1, 4):
            remote(send_ns.at[side, pl.ds(0, NEAR)], near.at[low], pas_sem, par_sem, {"lon": quarter(d), "lat": v}).start()

    to_west = edge(send_ew.at[0], halo_ew.at[1], 0, west, v)
    to_east = edge(send_ew.at[1], halo_ew.at[0], 1, east, v)
    to_north = [
        edge(send_ns.at[0], halo_ns.at[1], 2, u, v - 1),
        edge(send_dg.at[0], halo_dg.at[3], 3, west, v - 1),
        edge(send_dg.at[1], halo_dg.at[2], 4, east, v - 1),
    ]
    to_south = [
        edge(send_ns.at[1], halo_ns.at[0], 5, u, v + 1),
        edge(send_dg.at[2], halo_dg.at[1], 6, west, v + 1),
        edge(send_dg.at[3], halo_dg.at[0], 7, east, v + 1),
    ]

    to_west.start()
    to_east.start()

    @pl.when(v > 0)
    def _():
        for copy in to_north:
            copy.start()

    @pl.when(v < LAT - 1)
    def _():
        for copy in to_south:
            copy.start()

    @pl.loop(2, 34, unroll=4)
    def _(e):
        at = rows(e)
        for s in (sx, sd):
            line = s[1, at, :].astype(F32)
            s[0, at, :] = jnp.where(lane_row == 0, 0.0, pltpu.roll(line, 1, 0)).astype(BF)
            s[2, at, :] = jnp.where(lane_row == T - 1, 0.0, pltpu.roll(line, T - 1, 0)).astype(BF)

    for ref in (zx, zd, zh, zg, zs, zp, zq, ext, kz):
        ref[...] = jnp.zeros_like(ref)
    for b in range(3):
        for first, last in ((0, 3), (33, EXT)):
            sh[b, first * T : last * T, :] = jnp.zeros(((last - first) * T, C), BF)
        for first, last in ((0, 2), (34, EXT)):
            sx[b, first * T : last * T, :] = jnp.zeros(((last - first) * T, C), BF)
    for ref in (dz, dzg):
        ref[0 : 4 * T, :] = jnp.zeros((4 * T, C), BF)
        ref[34 * T : 38 * T, :] = jnp.zeros((4 * T, C), BF)

    @pl.when(rim_tile)
    def _():
        halo_ns[side] = jnp.zeros((MSG, C), BF)
        for t in range(2):
            halo_dg[2 * side + t] = jnp.zeros((16, C), BF)

    dz[3 * T : 35 * T, :] = sd[1, 2 * T : 34 * T, :]
    tiles[:, 9] = jnp.zeros((2, 16, C // 2), BF)

    def window(s, back, first, size):
        pieces = []
        for a in range(3):
            for b in range(3):
                start = (first + (2 - a if back else a)) * T
                pieces.append(s[2 - b if back else b, start : start + size * T, :])
        return jnp.concatenate(pieces, axis=1)

    def spread(s, left, right, e, line):
        at = rows(e)
        s[1, at, :] = line.astype(BF)
        s[0, at, :] = jnp.where(lane_row == 0, left, pltpu.roll(line, 1, 0)).astype(BF)
        s[2, at, :] = jnp.where(lane_row == T - 1, right, pltpu.roll(line, T - 1, 0)).astype(BF)

    def transposed(s, ref):
        for k in range(PX // 128):
            for b in range(3):
                ref[b * C : (b + 1) * C, k * 128 : (k + 1) * 128] = s[b, k * 128 : (k + 1) * 128, :].T

    inner = (lane_row > 0) & (lane_row < T - 1)

    fetched[2].wait()
    fetched[3].wait()
    pre1[2 * T : 32 * T, :] = dot(window(sx, False, 2, 30), w1[...])
    for tap in range(9):
        wt2[tap * C : (tap + 1) * C, :] = w2[tap * C : (tap + 1) * C, :].T
    transposed(sx, xt)
    back2[2 * T : 32 * T, :] = dot(window(sd, True, 2, 30), wt2[...])
    for e in range(3, 33):
        act, slp = gelu_parts(pre1[rows(e - 1), :])
        mask = jnp.where((jnp.full((T, C), e - 2, jnp.int32) < live) & inner, 1.0, 0.0)
        slope[rows(e - 1), :] = slp * mask
        spread(sh, 0.0, 0.0, e, act * mask)

    @pl.when(rim_tile)
    def _():
        drain(near.at[pl.ds(0, 3)], par_sem)
        drain(near.at[pl.ds(0, 3)], pas_sem)
        near[low] = send_ns[side, 0:NEAR, :]
        pivot = links[side, 0]
        n = lax.broadcasted_iota(jnp.int32, (8 * T, 4 * T), 0)
        at = lax.broadcasted_iota(jnp.int32, (8 * T, 4 * T), 1) + x * (4 * T)
        to = (n // (2 * T)) * 4 + low
        n = n & (2 * T - 1)
        q = n & 15
        in_east = n >= T + 16
        outer_col = jnp.where(in_east, T, -2) + (q & 1)
        col = jnp.where(n < T, n, outer_col)
        hit = ((pivot - to * T - col) & (LON * T - 1)) == at
        line = jnp.where(q < 8, q // 2, 5)
        corners = jnp.zeros((4, T, C), F32)
        for part in range(4):
            target = part ^ 1
            pick = jnp.where(hit & ((n < T) | (line == target)), 1.0, 0.0).astype(BF)
            lines = near[:, part * T : (part + 1) * T, :].reshape(4 * T, C)
            found = dot(pick, lines).reshape(4, 2 * T, C)
            picked[:, target * T : (target + 1) * T, :] = found[:, :T].astype(BF)
            corners = corners + found[:, T:]
        lane = lax.broadcasted_iota(jnp.int32, (T, C), 1)
        lane_col = jnp.where(lane == T + 1, -1, lane)
        for k in range(4):
            tile = ((pivot - (4 * k + low) * T - lane_col) & (LON * T - 1)) // T
            flags = jnp.zeros((T, C), F32)
            for t in range(4):
                flags = flags + jnp.where(tile == 4 * x + t, near[t, 4 * T : 4 * T + 1, :].astype(F32), 0.0)
            picked[k, 4 * T :, :] = jnp.where(lane_row == 9, flags, corners[k]).astype(BF)
        for d in range(1, 4):
            to = lax.rem(x + d, 4)
            remote(picked.at[to], arrived.at[x], pbs_sem, pbr_sem, {"lon": lax.rem(u + 4 * d, LON), "lat": v}).start()

    @pl.loop(3, 33, unroll=3)
    def _(e):
        spread(sg, 0.0, 0.0, e, back2[rows(e - 1), :] * slope[rows(e - 1), :])

    dzg[4 * T : 34 * T, :] = sg[1, 3 * T : 33 * T, :]
    transposed(sh, xth)
    for g, left, right in ((1, xt, dzg), (0, xth, dz)):
        for a in range(3):
            gm[g, a] = dot(left[...], right[(2 - a) * T : (2 - a) * T + PX, :])

    to_west.wait_recv()
    to_east.wait_recv()

    @pl.when(v > 0)
    def _():
        for copy in to_south:
            copy.wait_recv()

    @pl.when(v < LAT - 1)
    def _():
        for copy in to_north:
            copy.wait_recv()

    head = lax.broadcasted_iota(jnp.int32, (16, C), 0)

    def place(h):
        for k, (s, zz) in enumerate(((sx, zx), (sd, zd))):
            for t in range(2):
                px = halo_dg[2 * h + t].astype(F32)
                for r in range(2):
                    for n in range(2):
                        at = 4 * k + 2 * r + n
                        zz[t * 6 + n, pl.ds(34 * h + r, 1), :] = px[at : at + 1]
            for r in range(2):
                e = 34 * h + r
                line = halo_ns[h, (2 * k + r) * T : (2 * k + r + 1) * T, :].astype(F32)
                spread(s, zz[1, pl.ds(e, 1), :], zz[6, pl.ds(e, 1), :], e, line)
                for n, col in enumerate((0, 1, T - 2, T - 1)):
                    zz[2 + n, pl.ds(e, 1), :] = line[col : col + 1]
        mask = halo_ns[h, 4 * T :, :].astype(F32)
        e = 33 * h + 1
        for t in range(2):
            kz[3 * t, pl.ds(e, 1), :] = halo_dg[2 * h + t].astype(F32)[8:9]
            kz[1 + t, pl.ds(e, 1), :] = mask[t * (T - 1) : t * (T - 1) + 1]

    for k, zz in enumerate((zx, zd)):
        for n in range(2):
            zz[n, 2 : 2 + T, :] = halo_ew[0, (2 * k + n) * T : (2 * k + n + 1) * T, :].astype(F32)
            zz[6 + n, 2 : 2 + T, :] = halo_ew[1, (2 * k + n) * T : (2 * k + n + 1) * T, :].astype(F32)
            zz[2 + n, 2 : 2 + T, :] = cols[k, n]
            zz[4 + n, 2 : 2 + T, :] = cols[k, 2 + n]
    for t in range(2):
        kz[3 * t, 2 : 2 + T, :] = halo_ew[t, 4 * T :, :].astype(F32)
        kz[1 + t, 2 : 2 + T, :] = keep_col
    place(0)
    place(1)

    def insert(s, zz, e):
        at = pl.ds(pl.multiple_of(e * T, T), 16)
        s[0, at, :] = jnp.where(head == 0, zz[1, pl.ds(e, 1), :], s[0, at, :].astype(F32)).astype(BF)
        at = pl.ds(pl.multiple_of(e * T + 16, 16), 16)
        s[2, at, :] = jnp.where(head == 15, zz[6, pl.ds(e, 1), :], s[2, at, :].astype(F32)).astype(BF)

    for e in (2, 3, 32, 33):
        insert(sx, zx, e)
        insert(sd, zd, e)

    e_out, e_ring = jnp.where(south, 35, 0), jnp.where(south, 34, 1)
    e_edge, e_in = jnp.where(south, 33, 2), jnp.where(south, 32, 3)
    far = jnp.where(south, 2, 0)

    def extend(n, s, left, right, e):
        ext[n, 2 : 2 + T, :] = s[1, rows(e), :].astype(F32)
        for k, ref in enumerate(left):
            at = 2 - len(left) + k
            ext[n, at : at + 1, :] = ref[pl.ds(e, 1), :]
        for k, ref in enumerate(right):
            ext[n, 34 + k : 35 + k, :] = ref[pl.ds(e, 1), :]

    def straight(n):
        return jnp.concatenate([ext[n, 2 - b : 42 - b, :] for b in range(3)], axis=1).astype(BF)

    def turned(n):
        return jnp.concatenate([ext[n, b : b + 40, :] for b in range(3)], axis=1).astype(BF)

    def taps(w, row):
        return w[pl.ds(pl.multiple_of(row * 3 * C, 3 * C), 3 * C), :]

    def combine(up, mid, down, back):
        if back:
            up, down = down, up
        return pltpu.roll(up, 1, 0) + mid + pltpu.roll(down, mid.shape[0] - 1, 0)

    def strips(zz, w, back, ref):
        order = (2, 1, 0) if back else (0, 1, 2)
        lines = jnp.concatenate(
            [jnp.concatenate([zz[first + b] for b in order], axis=1) for first in (0, 1, 4, 5)], axis=0
        ).astype(BF)
        res = combine(*(dot(lines, w[a * 3 * C : (a + 1) * 3 * C, :]) for a in range(3)), back)
        for t in range(4):
            ref[t] = res[t * STRIP : (t + 1) * STRIP]

    def put_columns(s, zz):
        @pl.loop(3, 33, unroll=3)
        def _(e):
            c = [zz[t, pl.ds(e, 1), :] for t in range(4)]
            at = pl.ds(pl.multiple_of(e * T, T), 16)
            s[1, at, :] = jnp.where(head == 0, c[1], s[1, at, :].astype(F32)).astype(BF)
            line = jnp.where(head == 1, c[1], s[0, at, :].astype(F32))
            s[0, at, :] = jnp.where(head == 0, c[0], line).astype(BF)
            at = pl.ds(pl.multiple_of(e * T + 16, 16), 16)
            s[1, at, :] = jnp.where(head == 15, c[2], s[1, at, :].astype(F32)).astype(BF)
            line = jnp.where(head == 14, c[2], s[2, at, :].astype(F32))
            s[2, at, :] = jnp.where(head == 15, c[3], line).astype(BF)

    def of_row(res, t):
        at = (0, 1, T, T + 1)[t]
        return res[at : at + 1]

    def outer(s, back):
        return jnp.concatenate([window(s, back, 0, 2), window(s, back, 32, 2)], axis=0)

    res = dot(outer(sx, False), w1[...])
    pre1[0 : 2 * T, :] = res[: 2 * T]
    pre1[32 * T : 34 * T, :] = res[2 * T :]
    strips(zx, w1, False, zp)

    def activate_strips():
        for t in range(4):
            act, slp = gelu_parts(zp[t])
            zh[t] = act * kz[t]
            zs[t] = slp * kz[t]

    def activate(e, mask):
        act, slp = gelu_parts(pre1[rows(e - 1), :])
        slope[rows(e - 1), :] = slp * mask
        spread(sh, zh[0, pl.ds(e, 1), :], zh[3, pl.ds(e, 1), :], e, act * mask)

    activate_strips()
    activate(1, halo_ns[0, 4 * T :, :].astype(F32))
    activate(2, jnp.where(jnp.zeros((T, C), jnp.int32) < live, 1.0, 0.0))
    activate(33, keep_last)
    activate(34, halo_ns[1, 4 * T :, :].astype(F32))

    res = dot(outer(sd, True), wt2[...])
    back2[0 : 2 * T, :] = res[: 2 * T]
    back2[32 * T : 34 * T, :] = res[2 * T :]
    strips(zd, wt2, True, zq)

    def scale_strips():
        for t in range(4):
            zg[t] = zq[t] * zs[t]

    def scale(e):
        line = back2[rows(e - 1), :] * slope[rows(e - 1), :]
        spread(sg, zg[0, pl.ds(e, 1), :], zg[3, pl.ds(e, 1), :], e, line)

    scale_strips()
    for e in (1, 2, 33, 34):
        scale(e)

    @pl.when(rim_tile)
    def _():
        drain(arrived.at[pl.ds(0, 3)], pbr_sem)
        drain(arrived.at[pl.ds(0, 3)], pbs_sem)
        arrived[x] = picked[x]
        total = arrived[0].astype(F32)
        for k in range(1, 4):
            total = total + arrived[k].astype(F32)
        lane = lax.broadcasted_iota(jnp.int32, (T, C), 1)
        flags = jnp.broadcast_to(total[4 * T + 9 : 4 * T + 10], (T, C))

        def flag(hit):
            return jnp.broadcast_to(jnp.sum(jnp.where(hit, flags, 0.0), axis=1, keepdims=True), (T, C))

        halo_ns[side, 0 : 4 * T, :] = total[: 4 * T].astype(BF)
        halo_ns[side, 4 * T :, :] = flag(lane == lane_row).astype(BF)
        ends = jnp.where(lane_row < 16, flag(lane == T + 1), flag(lane == T))
        ends = jnp.where((lane_row & 15) == 8, ends, total[4 * T :]).astype(BF)
        halo_dg[2 * side] = ends[:16]
        halo_dg[2 * side + 1] = ends[16:]
        place(side)
        for n, e in enumerate((e_out, e_ring, e_edge, e_in)):
            extend(n, sx, (zx.at[0], zx.at[1]), (zx.at[6], zx.at[7]), e)
        pre = jnp.zeros((2 * STRIP, C), F32)
        for pair_of, row in (((straight(2), turned(1)), far), ((straight(1), turned(2)), 1), ((straight(0), turned(3)), 2 - far)):
            pre = pre + dot(jnp.concatenate(pair_of, axis=0), taps(w1, row))
        for k, e in enumerate((e_ring, e_edge)):
            pre1[rows(e - 1), :] = pre[k * STRIP + 1 : k * STRIP + 1 + T]
            for t in range(4):
                zp[t, pl.ds(e, 1), :] = of_row(pre[k * STRIP : (k + 1) * STRIP], t)
        activate_strips()
        activate(e_ring, halo_ns[side, 4 * T :, :].astype(F32))
        activate(e_edge, jnp.where(jnp.full((T, C), e_edge - 2, jnp.int32) < live, 1.0, 0.0))

        for n, e in enumerate((e_out, e_ring, e_edge, e_in)):
            extend(n, sd, (zd.at[0], zd.at[1]), (zd.at[6], zd.at[7]), e)
        back = dot(jnp.concatenate([turned(0), turned(1)], axis=0), taps(wt2, far))
        back = back + dot(jnp.concatenate([straight(2), straight(3)], axis=0), taps(wt2, far))
        back = back + dot(jnp.concatenate([turned(1), straight(2)], axis=0), taps(wt2, 1))
        for k, e in enumerate((e_ring, e_edge)):
            back2[rows(e - 1), :] = back[k * STRIP + 1 : k * STRIP + 1 + T]
            for t in range(4):
                zq[t, pl.ds(e, 1), :] = of_row(back[k * STRIP : (k + 1) * STRIP], t)
        scale_strips()
        scale(e_ring)
        scale(e_edge)

    sibling = {"lon": u + 1 - 2 * core, "lat": v}

    def pair(g, a):
        return remote(gsend.at[g, a], gpair.at[g, a], s1_sem.at[g, a], r1_sem.at[g, a], sibling)

    def add_pair(g, a):
        pair(g, a).wait()
        total = gkeep[g, a] + gpair[g, a].astype(F32)
        gsum[g, 3 * a : 3 * a + 3] = total.astype(BF).reshape(3, 4, 4, 16, C // 2)

    def first_axis(g):
        n, m = XT[g], 9 - XT[g]
        for d in range(1, 4):
            to = lax.rem(x + d, 4)
            dst = px1.at[g, x, pl.ds(0, n)]
            remote(gsum.at[g, pl.ds(0, n), to], dst, s2_sem.at[g, 0], r2_sem.at[g, 0], along_x(d)).start()
            to = lax.rem(y + d, 4)
            dst = py1.at[g, y, pl.ds(0, m)]
            remote(gsum.at[g, pl.ds(n, m), :, to], dst, s2_sem.at[g, 1], r2_sem.at[g, 1], along_y(d)).start()

    def total_of(ref, g, n):
        total = ref[g, 0, 0:n].astype(F32)
        for k in range(1, 4):
            total = total + ref[g, k, 0:n].astype(F32)
        return total.astype(BF)

    def three(ref, g, n):
        return ref.at[g, pl.ds(0, 3), pl.ds(0, n)]

    def second_axis(g):
        n, m = XT[g], 9 - XT[g]
        drain(three(px1, g, n), r2_sem.at[g, 0])
        px1[g, x, 0:n] = gsum[g, 0:n, x]
        sx1[g, 0:n] = total_of(px1, g, n)
        for d in range(1, 4):
            to = lax.rem(y + d, 4)
            dst = py2.at[g, y, pl.ds(0, n)]
            remote(sx1.at[g, pl.ds(0, n), to], dst, s2_sem.at[g, 2], r2_sem.at[g, 2], along_y(d)).start()
        drain(three(py1, g, m), r2_sem.at[g, 1])
        py1[g, y, 0:m] = gsum[g, n:9, :, y]
        sy1[g, 0:m] = total_of(py1, g, m)
        for d in range(1, 4):
            to = lax.rem(x + d, 4)
            dst = px2.at[g, x, pl.ds(0, m)]
            remote(sy1.at[g, pl.ds(0, m), to], dst, s2_sem.at[g, 3], r2_sem.at[g, 3], along_x(d)).start()

    def plane_total(g):
        n, m = XT[g], 9 - XT[g]
        drain(three(py2, g, n), r2_sem.at[g, 2])
        py2[g, y, 0:n] = sx1[g, 0:n, y]
        tiles[g, 0:n] = total_of(py2, g, n)
        drain(three(px2, g, m), r2_sem.at[g, 3])
        px2[g, x, 0:m] = sy1[g, 0:m, x]
        tiles[g, n:9] = total_of(px2, g, m)

    def column(ref, t, first, mask):
        return jnp.where(mask, ref[t, first : first + T, :], 0.0).astype(BF)

    def left_side(pieces):
        return jnp.concatenate([jnp.concatenate(p, axis=0).T for p in pieces], axis=0)

    def finish_grad(g, left, rights):
        for a, right in enumerate(rights):
            res = gm[g, a] + dot(left, jnp.concatenate(right, axis=0))
            lo, hi = res[:, : C // 2], res[:, C // 2 :]
            gkeep[g, a] = jnp.where(core == 0, lo, hi).reshape(3, C, C // 2)
            gsend[g, a] = jnp.where(core == 0, hi, lo).astype(BF).reshape(3, C, C // 2)
            pair(g, a).start()

    blank = jnp.zeros((T, C), BF)
    places = ((0, 1, None, None), (1, None, None, 2), (None, None, 2, 3))
    left = left_side(
        [
            [sh[b, T : 3 * T, :], sh[b, 33 * T : 35 * T, :]]
            + [blank if t is None else column(zh, t, 2, inner) for t in places[b]]
            for b in range(3)
        ]
    )
    rights = [
        [dz[(3 - a) * T : (5 - a) * T, :], dz[(35 - a) * T : (37 - a) * T, :]]
        + [zd[2 + q, 3 - a : 35 - a, :].astype(BF) for q in range(4)]
        for a in range(3)
    ]
    finish_grad(0, left, rights)
    left = left_side(
        [
            [sx[b, T : 4 * T, :], sx[b, 32 * T : 35 * T, :]]
            + [zx[t + b, 2 : 2 + T, :].astype(BF) for t in (1, 4)]
            for b in range(3)
        ]
    )
    rights = [
        [sg[1, e * T : (e + 1) * T, :] if k == a else blank for e in (2, 33) for k in range(3)]
        + [column(zg, t, 3 - a, (lane_row >= a) & (lane_row < T - 2 + a)) for t in (1, 2)]
        for a in range(3)
    ]
    finish_grad(1, left, rights)
    for g in range(2):
        for a in range(3):
            add_pair(g, a)
        first_axis(g)

    size = T // 2

    def forward(first):
        row = lax.broadcasted_iota(jnp.int32, (size * T, C), 0) // T + first
        pre = dot(window(sh, False, 1 + first, size), w2[...])
        masked = sx[1, (2 + first) * T : (2 + first + size) * T, :].astype(F32)
        out[first : first + size] = (masked + jnp.where(row < live, pre, 0.0)).astype(BF).reshape(size, T, C)

    put_columns(sh, zh)
    for tap in range(9):
        wt1[tap * C : (tap + 1) * C, :] = w1[tap * C : (tap + 1) * C, :].T
    forward(0)
    forward(size)
    second_axis(0)
    put_columns(sg, zg)

    row = lax.broadcasted_iota(jnp.int32, (T * T, C), 0) // T
    back = dot(window(sg, True, 1, T), wt1[...])
    total = cot[...].reshape(T * T, C).astype(F32) + back
    fgrad[...] = jnp.where(row < live, total, 0.0).astype(BF).reshape(T, T, C)

    @pl.when(rim_tile)
    def _():
        for n, e in ((1, e_ring), (2, e_edge), (3, e_in)):
            extend(n, sg, (zg.at[0],), (zg.at[3],), e)
        w_far, w_mid = taps(wt1, far), taps(wt1, 1)
        rim = dot(turned(1), w_far) + dot(straight(3), w_far) + dot(straight(2), w_mid)
        i = e_edge - 2
        total = cot[i].astype(F32) + rim[1 : 1 + T]
        kept = jnp.full((T, C), i, jnp.int32) < live
        fgrad[i] = jnp.where(kept, total, 0.0).astype(BF)

    second_axis(1)
    plane_total(0)
    plane_total(1)

    def first_tile(plane):
        return lax.div(18 * plane + 15 - spot, 16)

    for d in range(1, PLANES):
        to = lax.rem(z + d, PLANES)
        remote(
            tiles.at[:, pl.ds(first_tile(to), 2)],
            parts3.at[z],
            s3_sem,
            r3_sem,
            {"lon": u, "lat": to * 2 + y_lo},
        ).start()

    mine = first_tile(z)
    drain(parts3.at[pl.ds(0, PLANES - 1)], r3_sem)
    parts3[z] = tiles[:, pl.ds(mine, 2)]
    total = parts3[0].astype(F32)
    for k in range(1, PLANES):
        total = total + parts3[k].astype(F32)
    for slot in range(2):
        own[slot] = total[:, slot].astype(BF)

    def deliver(slot):
        group = (mine + slot) * 16 + spot
        lat, at = lax.div(group, 9), lax.rem(group, 9)
        src, dst = own.at[slot], final.at[core, at]

        def to(d):
            lon = 2 * lax.rem(lax.div(u, 2) + d, 8) + core
            return remote(src, dst, s4_sem.at[2 * slot + (d == 0)], r4_sem, {"lon": lon, "lat": lat})

        for d in range(1, 8):
            to(d).start()

        @pl.when(lat == v)
        def _():
            pltpu.make_async_copy(src, dst, r4_sem).start()

        @pl.when(lat != v)
        def _():
            to(0).start()

    def delivered(slot):
        lat = lax.div((mine + slot) * 16 + spot, 9)
        drain(final.at[0, pl.ds(0, 7)], s4_sem.at[2 * slot])

        @pl.when(lat != v)
        def _():
            drain(final.at[0, 0], s4_sem.at[2 * slot + 1])

    has_two = first_tile(z + 1) - mine == 2
    deliver(0)

    @pl.when(has_two)
    def _():
        deliver(1)

    drain(final.at[core], r4_sem)
    last = remote(final.at[core], final.at[core], s5_sem, r5_sem, sibling)
    last.start()
    for h in range(2):
        @pl.when(core == h)
        def _(h=h):
            sums[h] = final[h]
    delivered(0)

    @pl.when(has_two)
    def _():
        delivered(1)

    last.wait()
    for h in range(2):
        @pl.when(core != h)
        def _(h=h):
            sums[h] = final[h]

    to_west.wait_send()
    to_east.wait_send()

    @pl.when(v > 0)
    def _():
        for copy in to_north:
            copy.wait_send()

    @pl.when(v < LAT - 1)
    def _():
        for copy in to_south:
            copy.wait_send()

    for g in range(2):
        n, m = XT[g], 9 - XT[g]
        for k, (ref, size) in enumerate(((px1, n), (py1, m), (py2, n), (px2, m))):
            drain(three(ref, g, size), s2_sem.at[g, k])
    drain(parts3.at[pl.ds(0, PLANES - 1)], s3_sem)


def local(field, first_weight, second_weight, cotangent, live_rows, polar_links):
    vmem = pl.BlockSpec(memory_space=pltpu.VMEM)
    smem = pl.BlockSpec(memory_space=pltpu.SMEM)
    anywhere = pl.BlockSpec(memory_space=pl.ANY)
    half = C // 2
    tile = jax.ShapeDtypeStruct((T, T, C), BF)
    share = jax.ShapeDtypeStruct((SHARE, C), F32)
    flat = pltpu.VMEM((3, PX, C), BF)
    columns = pltpu.VMEM((8, STRIP, C), F32)
    four = pltpu.VMEM((4, STRIP, C), F32)
    ringed = pltpu.VMEM((RING * T, C), F32)
    weights = pltpu.VMEM((9 * C, C), BF)
    message = pltpu.VMEM((2, MSG, C), BF)
    corners = pltpu.VMEM((4, 16, C), BF)
    grads = pltpu.VMEM((2, 3, 3, C, half), BF)
    dma = pltpu.SemaphoreType.DMA
    made, back, sums = pl.pallas_call(
        kernel,
        out_shape=(pltpu.VMEM((T, T, C), BF), pltpu.VMEM((T, T, C), BF), pltpu.VMEM((2, 9, 2, 16, half), BF)),
        in_specs=[anywhere, anywhere, anywhere, anywhere, smem, smem],
        out_specs=(vmem, vmem, vmem),
        scratch_shapes=[
            *([flat] * 4),
            *([columns] * 2),
            *([four] * 6),
            pltpu.VMEM((T, T, C), BF),
            pltpu.VMEM((T, T, C), BF),
            pltpu.VMEM((2, 4, T, C), F32),
            pltpu.VMEM((4, 16, C), F32),
            *([ringed] * 3),
            *([pltpu.VMEM((3 * C, PX), BF)] * 2),
            *([pltpu.VMEM((38 * T, C), BF)] * 2),
            pltpu.VMEM((2, 3, 3 * C, C), F32),
            *([weights] * 4),
            pltpu.VMEM((4, 48, C), F32),
            message,
            message,
            corners,
            message,
            message,
            corners,
            pltpu.VMEM((4, NEAR, C), BF),
            pltpu.VMEM((4, PICK, C), BF),
            pltpu.VMEM((4, PICK, C), BF),
            pltpu.VMEM((2, 3, 3, C, half), F32),
            grads,
            grads,
            pltpu.VMEM((2, 9, 4, 4, 16, half), BF),
            *([pltpu.VMEM((2, 4, 5, 4, 16, half), BF)] * 2),
            *([pltpu.VMEM((2, 5, 4, 16, half), BF)] * 2),
            *([pltpu.VMEM((2, 4, 5, 16, half), BF)] * 2),
            pltpu.VMEM((2, 10, 16, half), BF),
            pltpu.VMEM((PLANES, 2, 2, 16, half), BF),
            pltpu.VMEM((2, 2, 16, half), BF),
            pltpu.VMEM((2, 9, 2, 16, half), BF),
            dma((4,)),
            dma((8,)),
            dma((8,)),
            dma,
            dma,
            dma,
            dma,
            dma((2, 3)),
            dma((2, 3)),
            dma((2, 4)),
            dma((2, 4)),
            dma,
            dma,
            dma((4,)),
            dma,
            dma,
            dma,
        ],
        compiler_params=pltpu.CompilerParams(
            collective_id=0, has_side_effects=True, vmem_limit_bytes=56 * 1024 * 1024
        ),
        cost_estimate=pl.CostEstimate(
            flops=12 * T * T * 9 * C * C, bytes_accessed=6_000_000, transcendentals=2 * T * T * C
        ),
    )(field, first_weight, second_weight, cotangent, live_rows, polar_links)
    made, back, sums = (pltpu.with_memory_space_constraint(r, pltpu.VMEM) for r in (made, back, sums))
    return pl.pallas_call(
        finish,
        out_shape=(tile, tile, share, share),
        in_specs=[vmem] * 3,
        out_specs=(anywhere,) * 4,
        scratch_shapes=[pltpu.VMEM((SHARE, C), F32), pltpu.VMEM((SHARE, C), F32), dma((4,))],
        compiler_params=pltpu.CompilerParams(vmem_limit_bytes=4 * 1024 * 1024),
        cost_estimate=pl.CostEstimate(flops=2 * SHARE * C, bytes_accessed=3_000_000, transcendentals=0),
    )(made, back, sums)


def solution(mesh):
    in_specs = (P("lat", "lon", None), P(), P(), P("lat", "lon", None), P("lon", "lat"), P())
    out_specs = (P("lat", "lon", None), P("lat", "lon", None), P("lat", None), P("lat", None))
    return jax.shard_map(local, mesh=mesh, in_specs=in_specs, out_specs=out_specs, check_vma=False)
```

```python
import math

import jax
import jax.numpy as jnp
from jax import lax
from jax.experimental import pallas as pl
from jax.experimental.pallas import tpu as pltpu
from jax.sharding import PartitionSpec as P

MESH = pl.DeviceIdType.MESH
BF = jnp.bfloat16
F32 = jnp.float32
C = 256
T = 32
EXT = T + 4
PX = EXT * T
RING = T + 2
MSG = 5 * T
STRIP = 40
LON = 16
LAT = 16
PLANES = 8
SHARE = 3 * T // 2 * 3
XT = (5, 4)
NEAR = 4 * T + 16
PICK = 5 * T


def dot(a, b):
    return jnp.dot(a, b, preferred_element_type=F32)


def gelu_parts(pre):
    cdf = 0.5 * (1.0 + lax.erf(pre * 0.7071067811865476))
    dens = jnp.exp(-0.5 * pre * pre) * 0.3989422804014327
    return (pre * cdf, cdf + pre * dens)


def rows(start, size=T):
    return pl.ds(pl.multiple_of(start * T, T), size)


def finish(made, back, sums, out, fgrad, grad1, grad2, share1, share2, sem):
    copies = [pltpu.make_async_copy(made, out, sem.at[0]), pltpu.make_async_copy(back, fgrad, sem.at[1])]
    for copy in copies:
        copy.start()
    scale = 1.0 / math.sqrt(LON * T * LAT * T)
    for g, (ref, dst) in enumerate(((share2, grad2), (share1, grad1))):
        for k in range(9):
            for h in range(2):
                ref[k * 16 : (k + 1) * 16, h * 128 : (h + 1) * 128] = sums[h, k, g].astype(F32) * scale
        copies.append(pltpu.make_async_copy(ref, dst, sem.at[2 + g]))
        copies[-1].start()
    for copy in copies:
        copy.wait()


def kernel(
    field_hbm,
    w1_hbm,
    w2_hbm,
    cot_hbm,
    live_ref,
    links,
    out,
    fgrad,
    sums,
    sx,
    sd,
    sh,
    sg,
    zx,
    zd,
    zh,
    zg,
    zs,
    zp,
    zq,
    kz,
    field,
    cot,
    cols,
    corner,
    pre1,
    back2,
    slope,
    xt,
    xth,
    dz,
    dzg,
    gm,
    w1,
    w2,
    wt1,
    wt2,
    ext,
    send_ns,
    send_ew,
    send_dg,
    halo_ns,
    halo_ew,
    halo_dg,
    near,
    picked,
    arrived,
    gkeep,
    gsend,
    gpair,
    gsum,
    px1,
    py1,
    sx1,
    sy1,
    py2,
    px2,
    tiles,
    parts3,
    own,
    final,
    w_sem,
    hs_sem,
    hr_sem,
    pas_sem,
    par_sem,
    pbs_sem,
    pbr_sem,
    s1_sem,
    r1_sem,
    s2_sem,
    r2_sem,
    s3_sem,
    r3_sem,
    s4_sem,
    r4_sem,
    s5_sem,
    r5_sem,
):
    u, v = lax.axis_index("lon"), lax.axis_index("lat")
    core, x, z = lax.rem(u, 2), lax.div(u, 4), lax.div(v, 2)
    low = lax.rem(u, 4)
    y_lo = lax.rem(v, 2)
    y = lax.div(low, 2) * 2 + y_lo
    spot = x * 4 + y
    north, south = v == 0, v == LAT - 1
    rim_tile = north | south
    side = jnp.where(south, 1, 0)
    live = live_ref[0, 0]
    east, west = lax.rem(u + 1, LON), lax.rem(u + LON - 1, LON)

    def in_plane(place):
        px, py = lax.div(place, 4), lax.rem(place, 4)
        return {"lon": px * 4 + lax.div(py, 2) * 2 + core, "lat": z * 2 + lax.rem(py, 2)}

    def along_x(d):
        return in_plane(lax.rem(x + d, 4) * 4 + y)

    def along_y(d):
        return in_plane(x * 4 + lax.rem(y + d, 4))

    def quarter(d):
        return x * 4 + lax.rem(low + d, 4)

    fetched = [
        pltpu.make_async_copy(src, dst, w_sem.at[n])
        for n, (src, dst) in enumerate(((field_hbm, field), (cot_hbm, cot), (w1_hbm, w1), (w2_hbm, w2)))
    ]
    for copy in fetched:
        copy.start()

    barrier = pltpu.get_barrier_semaphore()

    def greet(lon, lat):
        pl.semaphore_signal(barrier, inc=1, device_id={"lon": lon, "lat": lat}, device_id_type=MESH)

    @pl.when(rim_tile)
    def _():
        for d in range(1, 4):
            greet(quarter(d), v)
            greet(lax.rem(u + 4 * d, LON), v)

    greet(east, v)
    greet(west, v)

    @pl.when(v > 0)
    def _():
        for lon in (west, u, east):
            greet(lon, v - 1)

    @pl.when(v < LAT - 1)
    def _():
        for lon in (west, u, east):
            greet(lon, v + 1)

    for d in range(1, 4):
        for to in (along_x(d), along_y(d)):
            greet(to["lon"], to["lat"])

    @pl.loop(1, PLANES)
    def _(d):
        greet(u, lax.rem(z + d, PLANES) * 2 + y_lo)

    lane_row = lax.broadcasted_iota(jnp.int32, (T, C), 0)
    fetched[0].wait()
    fetched[1].wait()

    @pl.loop(0, T, unroll=4)
    def _(i):
        kept = jnp.full((T, C), i, jnp.int32) < live
        for k, (src, dst) in enumerate(((field, sx), (cot, sd))):
            line = jnp.where(kept, src[i].astype(F32), 0.0)
            dst[1, rows(i + 2), :] = line.astype(BF)
            for n, col in enumerate((0, 1, T - 2, T - 1)):
                cols[k, n, pl.ds(i, 1), :] = line[col : col + 1]

    keep_col = jnp.where(lane_row < live, 1.0, 0.0)
    keep_last = jnp.where(jnp.full((T, C), T - 1, jnp.int32) < live, 1.0, 0.0)
    for s in range(2):
        for k, src in enumerate((sx, sd)):
            first = 2 if s == 0 else T
            send_ns[s, 2 * k * T : (2 * k + 2) * T, :] = src[1, first * T : (first + 2) * T, :]
            for n in range(2):
                send_ew[s, (2 * k + n) * T : (2 * k + n + 1) * T, :] = cols[k, 2 * s + n].astype(BF)
        send_ns[s, 4 * T :, :] = jnp.ones((T, C), BF) if s == 0 else keep_last.astype(BF)
        send_ew[s, 4 * T :, :] = keep_col.astype(BF)
    corner[...] = jnp.zeros_like(corner)
    for s in range(2):
        for t in range(2):
            for k in range(2):
                for r in range(2):
                    for n in range(2):
                        at = 4 * k + 2 * r + n
                        line = (0 if s == 0 else T - 2) + r
                        corner[2 * s + t, at : at + 1, :] = cols[k, 2 * t + n, line : line + 1, :]
            corner[2 * s + t, 8:9, :] = jnp.ones((1, C), F32) if s == 0 else keep_last[0:1]
    send_dg[...] = corner[...].astype(BF)

    here = jnp.where(v > 0, 3, 0) + jnp.where(v < LAT - 1, 3, 0) + jnp.where(rim_tile, 6, 0)
    pl.semaphore_wait(barrier, here + 2 + 6 + 7)

    def remote(src, dst, send, recv, to):
        return pltpu.make_async_remote_copy(
            src_ref=src, dst_ref=dst, send_sem=send, recv_sem=recv, device_id=to, device_id_type=MESH
        )

    def drain(ref, sem):
        pltpu.make_async_copy(ref, ref, sem).wait()

    def edge(src, dst, n, lon, lat):
        return remote(src, dst, hs_sem.at[n], hr_sem.at[n], {"lon": lon, "lat": lat})

    @pl.when(rim_tile)
    def _():
        for d in range(1, 4):
            remote(send_ns.at[side, pl.ds(0, NEAR)], near.at[low], pas_sem, par_sem, {"lon": quarter(d), "lat": v}).start()

    to_west = edge(send_ew.at[0], halo_ew.at[1], 0, west, v)
    to_east = edge(send_ew.at[1], halo_ew.at[0], 1, east, v)
    to_north = [
        edge(send_ns.at[0], halo_ns.at[1], 2, u, v - 1),
        edge(send_dg.at[0], halo_dg.at[3], 3, west, v - 1),
        edge(send_dg.at[1], halo_dg.at[2], 4, east, v - 1),
    ]
    to_south = [
        edge(send_ns.at[1], halo_ns.at[0], 5, u, v + 1),
        edge(send_dg.at[2], halo_dg.at[1], 6, west, v + 1),
        edge(send_dg.at[3], halo_dg.at[0], 7, east, v + 1),
    ]

    to_west.start()
    to_east.start()

    @pl.when(v > 0)
    def _():
        for copy in to_north:
            copy.start()

    @pl.when(v < LAT - 1)
    def _():
        for copy in to_south:
            copy.start()

    @pl.loop(2, 34, unroll=4)
    def _(e):
        at = rows(e)
        for s in (sx, sd):
            line = s[1, at, :].astype(F32)
            s[0, at, :] = jnp.where(lane_row == 0, 0.0, pltpu.roll(line, 1, 0)).astype(BF)
            s[2, at, :] = jnp.where(lane_row == T - 1, 0.0, pltpu.roll(line, T - 1, 0)).astype(BF)

    for ref in (zx, zd, zh, zg, zs, zp, zq, ext, kz):
        ref[...] = jnp.zeros_like(ref)
    for b in range(3):
        for first, last in ((0, 3), (33, EXT)):
            sh[b, first * T : last * T, :] = jnp.zeros(((last - first) * T, C), BF)
        for first, last in ((0, 2), (34, EXT)):
            sx[b, first * T : last * T, :] = jnp.zeros(((last - first) * T, C), BF)
    for ref in (dz, dzg):
        ref[0 : 4 * T, :] = jnp.zeros((4 * T, C), BF)
        ref[34 * T : 38 * T, :] = jnp.zeros((4 * T, C), BF)

    @pl.when(rim_tile)
    def _():
        halo_ns[side] = jnp.zeros((MSG, C), BF)
        for t in range(2):
            halo_dg[2 * side + t] = jnp.zeros((16, C), BF)

    dz[3 * T : 35 * T, :] = sd[1, 2 * T : 34 * T, :]
    tiles[:, 9] = jnp.zeros((2, 16, C // 2), BF)

    def window(s, back, first, size):
        pieces = []
        for a in range(3):
            for b in range(3):
                start = (first + (2 - a if back else a)) * T
                pieces.append(s[2 - b if back else b, start : start + size * T, :])
        return jnp.concatenate(pieces, axis=1)

    def spread(s, left, right, e, line):
        at = rows(e)
        s[1, at, :] = line.astype(BF)
        s[0, at, :] = jnp.where(lane_row == 0, left, pltpu.roll(line, 1, 0)).astype(BF)
        s[2, at, :] = jnp.where(lane_row == T - 1, right, pltpu.roll(line, T - 1, 0)).astype(BF)

    def transposed(s, ref):
        for k in range(PX // 128):
            for b in range(3):
                ref[b * C : (b + 1) * C, k * 128 : (k + 1) * 128] = s[b, k * 128 : (k + 1) * 128, :].T

    inner = (lane_row > 0) & (lane_row < T - 1)

    fetched[2].wait()
    fetched[3].wait()
    pre1[2 * T : 32 * T, :] = dot(window(sx, False, 2, 30), w1[...])
    for tap in range(9):
        wt2[tap * C : (tap + 1) * C, :] = w2[tap * C : (tap + 1) * C, :].T
    transposed(sx, xt)
    back2[2 * T : 32 * T, :] = dot(window(sd, True, 2, 30), wt2[...])
    for e in range(3, 33):
        act, slp = gelu_parts(pre1[rows(e - 1), :])
        mask = jnp.where((jnp.full((T, C), e - 2, jnp.int32) < live) & inner, 1.0, 0.0)
        slope[rows(e - 1), :] = slp * mask
        spread(sh, 0.0, 0.0, e, act * mask)

    @pl.when(rim_tile)
    def _():
        drain(near.at[pl.ds(0, 3)], par_sem)
        near[low] = send_ns[side, 0:NEAR, :]
        pivot = links[side, 0]
        n = lax.broadcasted_iota(jnp.int32, (8 * T, 4 * T), 0)
        at = lax.broadcasted_iota(jnp.int32, (8 * T, 4 * T), 1) + x * (4 * T)
        to = (n // (2 * T)) * 4 + low
        n = n & (2 * T - 1)
        q = n & 15
        in_east = n >= T + 16
        outer_col = jnp.where(in_east, T, -2) + (q & 1)
        col = jnp.where(n < T, n, outer_col)
        hit = ((pivot - to * T - col) & (LON * T - 1)) == at
        line = jnp.where(q < 8, q // 2, 5)
        corners = jnp.zeros((4, T, C), F32)
        for part in range(4):
            target = part ^ 1
            pick = jnp.where(hit & ((n < T) | (line == target)), 1.0, 0.0).astype(BF)
            lines = near[:, part * T : (part + 1) * T, :].reshape(4 * T, C)
            found = dot(pick, lines).reshape(4, 2 * T, C)
            picked[:, target * T : (target + 1) * T, :] = found[:, :T].astype(BF)
            corners = corners + found[:, T:]
        lane = lax.broadcasted_iota(jnp.int32, (T, C), 1)
        lane_col = jnp.where(lane == T + 1, -1, lane)
        for k in range(4):
            tile = ((pivot - (4 * k + low) * T - lane_col) & (LON * T - 1)) // T
            flags = jnp.zeros((T, C), F32)
            for t in range(4):
                flags = flags + jnp.where(tile == 4 * x + t, near[t, 4 * T : 4 * T + 16, :].astype(F32)[0:1], 0.0)
            picked[k, 4 * T :, :] = jnp.where(lane_row == 9, flags, corners[k]).astype(BF)
        for d in range(1, 4):
            to = lax.rem(x + d, 4)
            remote(picked.at[to], arrived.at[x], pbs_sem, pbr_sem, {"lon": lax.rem(u + 4 * d, LON), "lat": v}).start()

    @pl.loop(3, 33, unroll=3)
    def _(e):
        spread(sg, 0.0, 0.0, e, back2[rows(e - 1), :] * slope[rows(e - 1), :])

    dzg[4 * T : 34 * T, :] = sg[1, 3 * T : 33 * T, :]
    transposed(sh, xth)
    for g, left, right in ((1, xt, dzg), (0, xth, dz)):
        for a in range(3):
            gm[g, a] = dot(left[...], right[(2 - a) * T : (2 - a) * T + PX, :])

    to_west.wait_recv()
    to_east.wait_recv()

    @pl.when(v > 0)
    def _():
        for copy in to_south:
            copy.wait_recv()

    @pl.when(v < LAT - 1)
    def _():
        for copy in to_north:
            copy.wait_recv()

    head = lax.broadcasted_iota(jnp.int32, (16, C), 0)

    def place(h):
        for k, (s, zz) in enumerate(((sx, zx), (sd, zd))):
            for t in range(2):
                px = halo_dg[2 * h + t].astype(F32)
                for r in range(2):
                    for n in range(2):
                        at = 4 * k + 2 * r + n
                        zz[t * 6 + n, pl.ds(34 * h + r, 1), :] = px[at : at + 1]
            for r in range(2):
                e = 34 * h + r
                line = halo_ns[h, (2 * k + r) * T : (2 * k + r + 1) * T, :].astype(F32)
                spread(s, zz[1, pl.ds(e, 1), :], zz[6, pl.ds(e, 1), :], e, line)
                for n, col in enumerate((0, 1, T - 2, T - 1)):
                    zz[2 + n, pl.ds(e, 1), :] = line[col : col + 1]
        mask = halo_ns[h, 4 * T :, :].astype(F32)
        e = 33 * h + 1
        for t in range(2):
            kz[3 * t, pl.ds(e, 1), :] = halo_dg[2 * h + t].astype(F32)[8:9]
            kz[1 + t, pl.ds(e, 1), :] = mask[t * (T - 1) : t * (T - 1) + 1]

    for k, zz in enumerate((zx, zd)):
        for n in range(2):
            zz[n, 2 : 2 + T, :] = halo_ew[0, (2 * k + n) * T : (2 * k + n + 1) * T, :].astype(F32)
            zz[6 + n, 2 : 2 + T, :] = halo_ew[1, (2 * k + n) * T : (2 * k + n + 1) * T, :].astype(F32)
            zz[2 + n, 2 : 2 + T, :] = cols[k, n]
            zz[4 + n, 2 : 2 + T, :] = cols[k, 2 + n]
    for t in range(2):
        kz[3 * t, 2 : 2 + T, :] = halo_ew[t, 4 * T :, :].astype(F32)
        kz[1 + t, 2 : 2 + T, :] = keep_col
    place(0)
    place(1)

    def insert(s, zz, e):
        at = pl.ds(pl.multiple_of(e * T, T), 16)
        s[0, at, :] = jnp.where(head == 0, zz[1, pl.ds(e, 1), :], s[0, at, :].astype(F32)).astype(BF)
        at = pl.ds(pl.multiple_of(e * T + 16, 16), 16)
        s[2, at, :] = jnp.where(head == 15, zz[6, pl.ds(e, 1), :], s[2, at, :].astype(F32)).astype(BF)

    for e in (2, 3, 32, 33):
        insert(sx, zx, e)
        insert(sd, zd, e)

    e_out, e_ring = jnp.where(south, 35, 0), jnp.where(south, 34, 1)
    e_edge, e_in = jnp.where(south, 33, 2), jnp.where(south, 32, 3)
    far = jnp.where(south, 2, 0)

    def extend(n, s, left, right, e):
        ext[n, 2 : 2 + T, :] = s[1, rows(e), :].astype(F32)
        for k, ref in enumerate(left):
            at = 2 - len(left) + k
            ext[n, at : at + 1, :] = ref[pl.ds(e, 1), :]
        for k, ref in enumerate(right):
            ext[n, 34 + k : 35 + k, :] = ref[pl.ds(e, 1), :]

    def straight(n):
        return jnp.concatenate([ext[n, 2 - b : 42 - b, :] for b in range(3)], axis=1).astype(BF)

    def turned(n):
        return jnp.concatenate([ext[n, b : b + 40, :] for b in range(3)], axis=1).astype(BF)

    def taps(w, row):
        return w[pl.ds(pl.multiple_of(row * 3 * C, 3 * C), 3 * C), :]

    def combine(up, mid, down, back):
        if back:
            up, down = down, up
        return pltpu.roll(up, 1, 0) + mid + pltpu.roll(down, mid.shape[0] - 1, 0)

    def strips(zz, w, back, ref):
        order = (2, 1, 0) if back else (0, 1, 2)
        lines = jnp.concatenate(
            [jnp.concatenate([zz[first + b] for b in order], axis=1) for first in (0, 1, 4, 5)], axis=0
        ).astype(BF)
        res = combine(*(dot(lines, w[a * 3 * C : (a + 1) * 3 * C, :]) for a in range(3)), back)
        for t in range(4):
            ref[t] = res[t * STRIP : (t + 1) * STRIP]

    def put_columns(s, zz):
        @pl.loop(3, 33, unroll=3)
        def _(e):
            c = [zz[t, pl.ds(e, 1), :] for t in range(4)]
            at = pl.ds(pl.multiple_of(e * T, T), 16)
            s[1, at, :] = jnp.where(head == 0, c[1], s[1, at, :].astype(F32)).astype(BF)
            line = jnp.where(head == 1, c[1], s[0, at, :].astype(F32))
            s[0, at, :] = jnp.where(head == 0, c[0], line).astype(BF)
            at = pl.ds(pl.multiple_of(e * T + 16, 16), 16)
            s[1, at, :] = jnp.where(head == 15, c[2], s[1, at, :].astype(F32)).astype(BF)
            line = jnp.where(head == 14, c[2], s[2, at, :].astype(F32))
            s[2, at, :] = jnp.where(head == 15, c[3], line).astype(BF)

    def of_row(res, t):
        at = (0, 1, T, T + 1)[t]
        return res[at : at + 1]

    def outer(s, back):
        return jnp.concatenate([window(s, back, 0, 2), window(s, back, 32, 2)], axis=0)

    res = dot(outer(sx, False), w1[...])
    pre1[0 : 2 * T, :] = res[: 2 * T]
    pre1[32 * T : 34 * T, :] = res[2 * T :]
    strips(zx, w1, False, zp)

    def activate_strips():
        for t in range(4):
            act, slp = gelu_parts(zp[t])
            zh[t] = act * kz[t]
            zs[t] = slp * kz[t]

    def activate(e, mask):
        act, slp = gelu_parts(pre1[rows(e - 1), :])
        slope[rows(e - 1), :] = slp * mask
        spread(sh, zh[0, pl.ds(e, 1), :], zh[3, pl.ds(e, 1), :], e, act * mask)

    activate_strips()
    activate(1, halo_ns[0, 4 * T :, :].astype(F32))
    activate(2, jnp.where(jnp.zeros((T, C), jnp.int32) < live, 1.0, 0.0))
    activate(33, keep_last)
    activate(34, halo_ns[1, 4 * T :, :].astype(F32))

    res = dot(outer(sd, True), wt2[...])
    back2[0 : 2 * T, :] = res[: 2 * T]
    back2[32 * T : 34 * T, :] = res[2 * T :]
    strips(zd, wt2, True, zq)

    def scale_strips():
        for t in range(4):
            zg[t] = zq[t] * zs[t]

    def scale(e):
        line = back2[rows(e - 1), :] * slope[rows(e - 1), :]
        spread(sg, zg[0, pl.ds(e, 1), :], zg[3, pl.ds(e, 1), :], e, line)

    scale_strips()
    for e in (1, 2, 33, 34):
        scale(e)

    @pl.when(rim_tile)
    def _():
        drain(arrived.at[pl.ds(0, 3)], pbr_sem)
        arrived[x] = picked[x]
        total = arrived[0].astype(F32)
        for k in range(1, 4):
            total = total + arrived[k].astype(F32)
        lane = lax.broadcasted_iota(jnp.int32, (T, C), 1)
        flags = jnp.broadcast_to(total[4 * T + 9 : 4 * T + 10], (T, C))

        def flag(hit):
            return jnp.broadcast_to(jnp.sum(jnp.where(hit, flags, 0.0), axis=1, keepdims=True), (T, C))

        halo_ns[side, 0 : 4 * T, :] = total[: 4 * T].astype(BF)
        halo_ns[side, 4 * T :, :] = flag(lane == lane_row).astype(BF)
        ends = jnp.where(lane_row < 16, flag(lane == T + 1), flag(lane == T))
        ends = jnp.where((lane_row & 15) == 8, ends, total[4 * T :]).astype(BF)
        halo_dg[2 * side] = ends[:16]
        halo_dg[2 * side + 1] = ends[16:]
        place(side)
        for n, e in enumerate((e_out, e_ring, e_edge, e_in)):
            extend(n, sx, (zx.at[0], zx.at[1]), (zx.at[6], zx.at[7]), e)
        pre = jnp.zeros((2 * STRIP, C), F32)
        for pair_of, row in (((straight(2), turned(1)), far), ((straight(1), turned(2)), 1), ((straight(0), turned(3)), 2 - far)):
            pre = pre + dot(jnp.concatenate(pair_of, axis=0), taps(w1, row))
        for k, e in enumerate((e_ring, e_edge)):
            pre1[rows(e - 1), :] = pre[k * STRIP + 1 : k * STRIP + 1 + T]
            for t in range(4):
                zp[t, pl.ds(e, 1), :] = of_row(pre[k * STRIP : (k + 1) * STRIP], t)
        activate_strips()
        activate(e_ring, halo_ns[side, 4 * T :, :].astype(F32))
        activate(e_edge, jnp.where(jnp.full((T, C), e_edge - 2, jnp.int32) < live, 1.0, 0.0))

        for n, e in enumerate((e_out, e_ring, e_edge, e_in)):
            extend(n, sd, (zd.at[0], zd.at[1]), (zd.at[6], zd.at[7]), e)
        back = dot(jnp.concatenate([turned(0), turned(1)], axis=0), taps(wt2, far))
        back = back + dot(jnp.concatenate([straight(2), straight(3)], axis=0), taps(wt2, far))
        back = back + dot(jnp.concatenate([turned(1), straight(2)], axis=0), taps(wt2, 1))
        for k, e in enumerate((e_ring, e_edge)):
            back2[rows(e - 1), :] = back[k * STRIP + 1 : k * STRIP + 1 + T]
            for t in range(4):
                zq[t, pl.ds(e, 1), :] = of_row(back[k * STRIP : (k + 1) * STRIP], t)
        scale_strips()
        scale(e_ring)
        scale(e_edge)

    sibling = {"lon": u + 1 - 2 * core, "lat": v}

    def pair(g, a):
        return remote(gsend.at[g, a], gpair.at[g, a], s1_sem.at[g, a], r1_sem.at[g, a], sibling)

    def add_pair(g, a):
        pair(g, a).wait()
        total = gkeep[g, a] + gpair[g, a].astype(F32)
        gsum[g, 3 * a : 3 * a + 3] = total.astype(BF).reshape(3, 4, 4, 16, C // 2)

    def first_axis(g):
        n, m = XT[g], 9 - XT[g]
        for d in range(1, 4):
            to = lax.rem(x + d, 4)
            dst = px1.at[g, x, pl.ds(0, n)]
            remote(gsum.at[g, pl.ds(0, n), to], dst, s2_sem.at[g, 0], r2_sem.at[g, 0], along_x(d)).start()
            to = lax.rem(y + d, 4)
            dst = py1.at[g, y, pl.ds(0, m)]
            remote(gsum.at[g, pl.ds(n, m), :, to], dst, s2_sem.at[g, 1], r2_sem.at[g, 1], along_y(d)).start()

    def total_of(ref, g, n):
        total = ref[g, 0, 0:n].astype(F32)
        for k in range(1, 4):
            total = total + ref[g, k, 0:n].astype(F32)
        return total.astype(BF)

    def three(ref, g, n):
        return ref.at[g, pl.ds(0, 3), pl.ds(0, n)]

    def second_axis(g):
        n, m = XT[g], 9 - XT[g]
        drain(three(px1, g, n), r2_sem.at[g, 0])
        px1[g, x, 0:n] = gsum[g, 0:n, x]
        sx1[g, 0:n] = total_of(px1, g, n)
        for d in range(1, 4):
            to = lax.rem(y + d, 4)
            dst = py2.at[g, y, pl.ds(0, n)]
            remote(sx1.at[g, pl.ds(0, n), to], dst, s2_sem.at[g, 2], r2_sem.at[g, 2], along_y(d)).start()
        drain(three(py1, g, m), r2_sem.at[g, 1])
        py1[g, y, 0:m] = gsum[g, n:9, :, y]
        sy1[g, 0:m] = total_of(py1, g, m)
        for d in range(1, 4):
            to = lax.rem(x + d, 4)
            dst = px2.at[g, x, pl.ds(0, m)]
            remote(sy1.at[g, pl.ds(0, m), to], dst, s2_sem.at[g, 3], r2_sem.at[g, 3], along_x(d)).start()

    def plane_total(g):
        n, m = XT[g], 9 - XT[g]
        drain(three(py2, g, n), r2_sem.at[g, 2])
        py2[g, y, 0:n] = sx1[g, 0:n, y]
        tiles[g, 0:n] = total_of(py2, g, n)
        drain(three(px2, g, m), r2_sem.at[g, 3])
        px2[g, x, 0:m] = sy1[g, 0:m, x]
        tiles[g, n:9] = total_of(px2, g, m)

    def column(ref, t, first, mask):
        return jnp.where(mask, ref[t, first : first + T, :], 0.0).astype(BF)

    def left_side(pieces):
        return jnp.concatenate([jnp.concatenate(p, axis=0).T for p in pieces], axis=0)

    def finish_grad(g, left, rights):
        for a, right in enumerate(rights):
            res = gm[g, a] + dot(left, jnp.concatenate(right, axis=0))
            lo, hi = res[:, : C // 2], res[:, C // 2 :]
            gkeep[g, a] = jnp.where(core == 0, lo, hi).reshape(3, C, C // 2)
            gsend[g, a] = jnp.where(core == 0, hi, lo).astype(BF).reshape(3, C, C // 2)
            pair(g, a).start()

    blank = jnp.zeros((T, C), BF)
    places = ((0, 1, None, None), (1, None, None, 2), (None, None, 2, 3))
    left = left_side(
        [
            [sh[b, T : 3 * T, :], sh[b, 33 * T : 35 * T, :]]
            + [blank if t is None else column(zh, t, 2, inner) for t in places[b]]
            for b in range(3)
        ]
    )
    rights = [
        [dz[(3 - a) * T : (5 - a) * T, :], dz[(35 - a) * T : (37 - a) * T, :]]
        + [zd[2 + q, 3 - a : 35 - a, :].astype(BF) for q in range(4)]
        for a in range(3)
    ]
    finish_grad(0, left, rights)
    left = left_side(
        [
            [sx[b, T : 4 * T, :], sx[b, 32 * T : 35 * T, :]]
            + [zx[t + b, 2 : 2 + T, :].astype(BF) for t in (1, 4)]
            for b in range(3)
        ]
    )
    rights = [
        [sg[1, e * T : (e + 1) * T, :] if k == a else blank for e in (2, 33) for k in range(3)]
        + [column(zg, t, 3 - a, (lane_row >= a) & (lane_row < T - 2 + a)) for t in (1, 2)]
        for a in range(3)
    ]
    finish_grad(1, left, rights)
    for g in range(2):
        for a in range(3):
            add_pair(g, a)
        first_axis(g)

    size = T // 2

    def forward(first):
        row = lax.broadcasted_iota(jnp.int32, (size * T, C), 0) // T + first
        pre = dot(window(sh, False, 1 + first, size), w2[...])
        masked = sx[1, (2 + first) * T : (2 + first + size) * T, :].astype(F32)
        out[first : first + size] = (masked + jnp.where(row < live, pre, 0.0)).astype(BF).reshape(size, T, C)

    put_columns(sh, zh)
    for tap in range(9):
        wt1[tap * C : (tap + 1) * C, :] = w1[tap * C : (tap + 1) * C, :].T
    forward(0)
    forward(size)
    second_axis(0)
    put_columns(sg, zg)

    row = lax.broadcasted_iota(jnp.int32, (T * T, C), 0) // T
    back = dot(window(sg, True, 1, T), wt1[...])
    total = cot[...].reshape(T * T, C).astype(F32) + back
    fgrad[...] = jnp.where(row < live, total, 0.0).astype(BF).reshape(T, T, C)

    @pl.when(rim_tile)
    def _():
        for n, e in ((1, e_ring), (2, e_edge), (3, e_in)):
            extend(n, sg, (zg.at[0],), (zg.at[3],), e)
        w_far, w_mid = taps(wt1, far), taps(wt1, 1)
        rim = dot(turned(1), w_far) + dot(straight(3), w_far) + dot(straight(2), w_mid)
        i = e_edge - 2
        total = cot[i].astype(F32) + rim[1 : 1 + T]
        kept = jnp.full((T, C), i, jnp.int32) < live
        fgrad[i] = jnp.where(kept, total, 0.0).astype(BF)

    second_axis(1)
    plane_total(0)
    plane_total(1)

    def first_tile(plane):
        return lax.div(18 * plane + 15 - spot, 16)

    for d in range(1, PLANES):
        to = lax.rem(z + d, PLANES)
        remote(
            tiles.at[:, pl.ds(first_tile(to), 2)],
            parts3.at[z],
            s3_sem,
            r3_sem,
            {"lon": u, "lat": to * 2 + y_lo},
        ).start()

    mine = first_tile(z)
    drain(parts3.at[pl.ds(0, PLANES - 1)], r3_sem)
    parts3[z] = tiles[:, pl.ds(mine, 2)]
    total = parts3[0].astype(F32)
    for k in range(1, PLANES):
        total = total + parts3[k].astype(F32)
    for slot in range(2):
        own[slot] = total[:, slot].astype(BF)

    def deliver(slot):
        group = (mine + slot) * 16 + spot
        lat, at = lax.div(group, 9), lax.rem(group, 9)
        src, dst = own.at[slot], final.at[core, at]

        def to(d):
            lon = 2 * lax.rem(lax.div(u, 2) + d, 8) + core
            return remote(src, dst, s4_sem.at[2 * slot + (d == 0)], r4_sem, {"lon": lon, "lat": lat})

        for d in range(1, 8):
            to(d).start()

        @pl.when(lat == v)
        def _():
            pltpu.make_async_copy(src, dst, r4_sem).start()

        @pl.when(lat != v)
        def _():
            to(0).start()

    def delivered(slot):
        lat = lax.div((mine + slot) * 16 + spot, 9)
        drain(final.at[0, pl.ds(0, 7)], s4_sem.at[2 * slot])

        @pl.when(lat != v)
        def _():
            drain(final.at[0, 0], s4_sem.at[2 * slot + 1])

    has_two = first_tile(z + 1) - mine == 2
    deliver(0)

    @pl.when(has_two)
    def _():
        deliver(1)

    drain(final.at[core], r4_sem)
    last = remote(final.at[core], final.at[core], s5_sem, r5_sem, sibling)
    last.start()
    for h in range(2):
        @pl.when(core == h)
        def _(h=h):
            sums[h] = final[h]
    delivered(0)

    @pl.when(has_two)
    def _():
        delivered(1)

    last.wait()
    for h in range(2):
        @pl.when(core != h)
        def _(h=h):
            sums[h] = final[h]

    @pl.when(rim_tile)
    def _():
        drain(near.at[pl.ds(0, 3)], pas_sem)
        drain(arrived.at[pl.ds(0, 3)], pbs_sem)

    to_west.wait_send()
    to_east.wait_send()

    @pl.when(v > 0)
    def _():
        for copy in to_north:
            copy.wait_send()

    @pl.when(v < LAT - 1)
    def _():
        for copy in to_south:
            copy.wait_send()

    for g in range(2):
        n, m = XT[g], 9 - XT[g]
        for k, (ref, size) in enumerate(((px1, n), (py1, m), (py2, n), (px2, m))):
            drain(three(ref, g, size), s2_sem.at[g, k])
    drain(parts3.at[pl.ds(0, PLANES - 1)], s3_sem)


def local(field, first_weight, second_weight, cotangent, live_rows, polar_links):
    vmem = pl.BlockSpec(memory_space=pltpu.VMEM)
    smem = pl.BlockSpec(memory_space=pltpu.SMEM)
    anywhere = pl.BlockSpec(memory_space=pl.ANY)
    half = C // 2
    tile = jax.ShapeDtypeStruct((T, T, C), BF)
    share = jax.ShapeDtypeStruct((SHARE, C), F32)
    flat = pltpu.VMEM((3, PX, C), BF)
    columns = pltpu.VMEM((8, STRIP, C), F32)
    four = pltpu.VMEM((4, STRIP, C), F32)
    ringed = pltpu.VMEM((RING * T, C), F32)
    weights = pltpu.VMEM((9 * C, C), BF)
    message = pltpu.VMEM((2, MSG, C), BF)
    corners = pltpu.VMEM((4, 16, C), BF)
    grads = pltpu.VMEM((2, 3, 3, C, half), BF)
    dma = pltpu.SemaphoreType.DMA
    made, back, sums = pl.pallas_call(
        kernel,
        out_shape=(pltpu.VMEM((T, T, C), BF), pltpu.VMEM((T, T, C), BF), pltpu.VMEM((2, 9, 2, 16, half), BF)),
        in_specs=[anywhere, anywhere, anywhere, anywhere, smem, smem],
        out_specs=(vmem, vmem, vmem),
        scratch_shapes=[
            *([flat] * 4),
            *([columns] * 2),
            *([four] * 6),
            pltpu.VMEM((T, T, C), BF),
            pltpu.VMEM((T, T, C), BF),
            pltpu.VMEM((2, 4, T, C), F32),
            pltpu.VMEM((4, 16, C), F32),
            *([ringed] * 3),
            *([pltpu.VMEM((3 * C, PX), BF)] * 2),
            *([pltpu.VMEM((38 * T, C), BF)] * 2),
            pltpu.VMEM((2, 3, 3 * C, C), F32),
            *([weights] * 4),
            pltpu.VMEM((4, 48, C), F32),
            message,
            message,
            corners,
            message,
            message,
            corners,
            pltpu.VMEM((4, NEAR, C), BF),
            pltpu.VMEM((4, PICK, C), BF),
            pltpu.VMEM((4, PICK, C), BF),
            pltpu.VMEM((2, 3, 3, C, half), F32),
            grads,
            grads,
            pltpu.VMEM((2, 9, 4, 4, 16, half), BF),
            *([pltpu.VMEM((2, 4, 5, 4, 16, half), BF)] * 2),
            *([pltpu.VMEM((2, 5, 4, 16, half), BF)] * 2),
            *([pltpu.VMEM((2, 4, 5, 16, half), BF)] * 2),
            pltpu.VMEM((2, 10, 16, half), BF),
            pltpu.VMEM((PLANES, 2, 2, 16, half), BF),
            pltpu.VMEM((2, 2, 16, half), BF),
            pltpu.VMEM((2, 9, 2, 16, half), BF),
            dma((4,)),
            dma((8,)),
            dma((8,)),
            dma,
            dma,
            dma,
            dma,
            dma((2, 3)),
            dma((2, 3)),
            dma((2, 4)),
            dma((2, 4)),
            dma,
            dma,
            dma((4,)),
            dma,
            dma,
            dma,
        ],
        compiler_params=pltpu.CompilerParams(
            collective_id=0, has_side_effects=True, vmem_limit_bytes=56 * 1024 * 1024
        ),
        cost_estimate=pl.CostEstimate(
            flops=12 * T * T * 9 * C * C, bytes_accessed=6_000_000, transcendentals=2 * T * T * C
        ),
    )(field, first_weight, second_weight, cotangent, live_rows, polar_links)
    made, back, sums = (pltpu.with_memory_space_constraint(r, pltpu.VMEM) for r in (made, back, sums))
    return pl.pallas_call(
        finish,
        out_shape=(tile, tile, share, share),
        in_specs=[vmem] * 3,
        out_specs=(anywhere,) * 4,
        scratch_shapes=[pltpu.VMEM((SHARE, C), F32), pltpu.VMEM((SHARE, C), F32), dma((4,))],
        compiler_params=pltpu.CompilerParams(vmem_limit_bytes=4 * 1024 * 1024),
        cost_estimate=pl.CostEstimate(flops=2 * SHARE * C, bytes_accessed=3_000_000, transcendentals=0),
    )(made, back, sums)


def solution(mesh):
    in_specs = (P("lat", "lon", None), P(), P(), P("lat", "lon", None), P("lon", "lat"), P())
    out_specs = (P("lat", "lon", None), P("lat", "lon", None), P("lat", None), P("lat", None))
    return jax.shard_map(local, mesh=mesh, in_specs=in_specs, out_specs=out_specs, check_vma=False)
```
